32 devices in a mesh: dp: 4 (over z), expert: 8 (over y, x, core).
Axes of the slice: x: 2, y: 2, z: 4, core: 2. Of those that a mesh axis runs over, the one named last changes fastest.
Arguments:
- tokens: bfloat16 [32768, 768], P(('dp', 'expert')), may hold values from -6 to 6
- segments: int32 [32, 1024], P(('dp', 'expert')), may hold values from 0 to 7, never falling along the last dimension, each value on 1 to 512 neighbouring positions
- routes: int32 [32768, 1], P(('dp', 'expert')), may hold values from 0 to 7; in each aligned block of 1024 rows (0 to 1023, 1024 to 2047, ...) at most 256 rows name the same one
- cotangent: bfloat16 [32768, 768], P(('dp', 'expert')), may hold values from -6 to 6
- w_qkv: bfloat16 [768, 2304], replicated, may hold values from -0.21875 to 0.21875
- w_attn_out: bfloat16 [768, 768], replicated, may hold values from -1.25 to 1.25
- gain_attn: float32 [768], replicated, may hold values from 0.5 to 1.5
- gain_ffn: float32 [768], replicated, may hold values from 0.5 to 1.5
- w_router: bfloat16 [768, 16], replicated, may hold values from -0.21875 to 0.21875
- embed: float32 [8, 16], replicated, may hold values from -5 to 5
- w_in: bfloat16 [8, 768, 3072], P('expert'), may hold values from -0.21875 to 0.21875
- w_out: bfloat16 [8, 3072, 768], P('expert'), may hold values from -0.875 to 0.875
Outputs:
- out_tokens: bfloat16 [32768, 768], P(('dp', 'expert'))
- grad_tokens: float32 [32768, 768], P(('dp', 'expert'))
- grad_w_qkv: float32 [768, 2304], replicated
- grad_w_attn_out: float32 [768, 768], replicated
- grad_gain_attn: float32 [768], replicated
- grad_gain_ffn: float32 [768], replicated
- grad_w_router: float32 [768, 16], replicated
- grad_embed: float32 [8, 16], replicated
- grad_w_in: float32 [8, 768, 3072], P('expert', None, 'dp')
- grad_w_out: float32 [8, 3072, 768], P('expert', 'dp')
The draws below stay inside these ranges and needn't reach their ends.
Inputs may be any that keep to these rules, and one draw needn't show every extreme that they name: `routes`: among the 1024 rows of one device no expert is named more than 256 times, and in every draw some device names some expert exactly 256 times. `segments`: segment numbers never fall along a sequence; a segment has at most half of 1024 tokens, and one has exactly that many.
All inputs are finite; a program needn't handle non-finite values.
Results may differ from the reference program's by a relative error of at most 0.013.
The reference program's roundings to bfloat16 on the way count: a program that leaves them out, or rounds other values in their place, can miss the bound.
Values may be sent and summed in bfloat16 or wider, within the bound.
No kernel may reach another device: no remote copies, remote signals or barrier semaphores. Data moves between devices by JAX's collectives and lax.ppermute only.
A program may use at most 384 MiB of HBM per device.

```python
import math
import jax
import jax.numpy as jnp
import numpy as np
from jax import lax

D = 768
HEADS = 12
HEAD = 64
FF = 3072
RDIM = 16
SEQ_LEN = 1024
EXPERTS = 8
TOK_DEV = 1024
SEQS = 32
TOKENS = 32768
CAP = 256
DEVICES = 32


def block_scale(rng, dims, cuts, low, high):
    gain, own = 1.0, jax.random.fold_in(rng, 6)
    for dim, blocks in cuts:
        steps = jnp.exp(jax.random.uniform(jax.random.fold_in(own, dim), (blocks,), jnp.float32, low / len(cuts), high / len(cuts)))
        gain = gain * jnp.repeat(steps, dims[dim] // blocks).reshape([-1 if axis == dim else 1 for axis in range(len(dims))])
    return gain


def length_profile(number_of, total, most, skew):
    portions = [(1 << 20) // math.isqrt(rank ** skew) + 1 for rank in range(2, number_of + 1)]
    surplus, counts = total - most - (number_of - 1), [1] * (number_of - 1)
    while surplus > 0:
        movable = [i for i in range(number_of - 1) if counts[i] < most]
        whole, budget = sum([portions[i] for i in movable]), surplus
        for i in movable:
            extra = min(most - counts[i], max(1, budget * portions[i] // whole), surplus)
            counts[i] = counts[i] + extra
            surplus = surplus - extra
    return np.array([most] + counts)


def uneven(rng, count, total, most, skew):
    if count == 2:
        one = jax.random.randint(rng, (), max(1, total - most), min(most, total - 1) + 1)
        return jnp.stack([one, total - one])
    lengths = jnp.asarray(length_profile(count, total, most, skew), jnp.int32)
    couples = (count - 1) // 2
    giver, receiver = lengths[1:1 + 2 * couples:2], lengths[2:2 + 2 * couples:2]
    room = jnp.minimum(giver - 1, most - receiver)
    moved = jax.random.randint(jax.random.fold_in(rng, 1), (couples,), 0, 1 << 20) % (room + 1)
    lengths = lengths.at[1:1 + 2 * couples:2].set(giver - moved).at[2:2 + 2 * couples:2].set(receiver + moved)
    return lengths[jax.random.permutation(jax.random.fold_in(rng, 2), count)]


def routed_block(rng, own, number, rows, count, top, reach, skew):
    order = jax.random.permutation(rng, count)
    crowded, common = load_shares(count, rows * top, reach, skew, True), load_shares(count, rows * top, reach, skew, False)
    places = jnp.arange(count)

    def named(lengths, rotation):
        used = int((lengths > 0).sum())
        fixed = max(1, used // 4)
        passed = fixed + (places - fixed + rotation * (used - fixed)) % max(1, count - fixed)
        return jnp.zeros((count,), jnp.int32).at[order[jnp.where(places < fixed, places, passed)]].set(jnp.asarray(lengths, jnp.int32))

    lengths = jnp.where(number % 4 == 0, named(crowded, number // 4), named(common, number - number // 4 - 1))
    mixed = jax.random.permutation(jax.random.fold_in(own, 3), count)
    giver, sink = mixed[0:count // 2 * 2:2], mixed[1:count // 2 * 2:2]
    margin = jnp.minimum(lengths[giver] - 1, reach - lengths[sink]) // 2
    margin = jnp.where((giver == order[0]) | (sink == order[0]) | (lengths[sink] == 0), 0, jnp.maximum(margin, 0))
    passed = jax.random.randint(jax.random.fold_in(own, 4), (count // 2,), 0, 1 << 20) % (margin + 1)
    lengths = lengths.at[giver].add(-passed).at[sink].add(passed)
    members = jnp.searchsorted(jnp.cumsum(lengths), jnp.arange(rows * top), side="right").astype(jnp.int32)
    listing = members.reshape(top, rows).T
    listing = listing[jax.random.permutation(jax.random.fold_in(own, 1), rows)]
    rotation = jax.random.randint(jax.random.fold_in(own, 2), (rows, 1), 0, top)
    return jnp.take_along_axis(listing, (jnp.arange(top)[None, :] + rotation) % top, axis=1)


def load_shares(amount, total, reach, lean, full):
    portions = [(1 << 20) // math.isqrt(standing ** lean) + 1 for standing in range(1, amount + 1)]
    largest = reach if full else min(reach, max(-(-total // amount), total * portions[0] // sum(portions)))
    least = 1 if total - largest >= amount - 1 else 0
    counts, spare = [largest] + [least] * (amount - 1), total - largest - least * (amount - 1)
    while spare > 0:
        candidates = [i for i in range(1, amount) if counts[i] < largest] or [i for i in range(1, amount) if counts[i] < reach]
        mass, left = sum([portions[i] for i in candidates]), spare
        for i in candidates:
            addition = min(reach - counts[i], max(1, left * portions[i] // mass), spare)
            counts[i] = counts[i] + addition
            spare = spare - addition
    return np.array(counts)


def centred(key, dims, width, bound, pieces=(), kind=jnp.bfloat16):
    level = block_scale(key, dims, pieces, -0.22, 0.18) if pieces else 1.0
    values = jax.random.normal(key, dims, jnp.float32) * width * level
    return jnp.minimum(jnp.maximum(values, -bound), bound).astype(kind)


def setup_inputs(seed: int = 0) -> dict:
    arg_keys = jax.random.split(jax.random.key(seed), 13)
    tokens = centred(arg_keys[0], (TOKENS, D), 1.0, 6.0, ((0, 32),))
    segments = jax.vmap(lambda own: jnp.searchsorted(jnp.cumsum(uneven(own, max(SEQ_LEN // 128, 4), SEQ_LEN, SEQ_LEN // 2, 2)), jnp.arange(SEQ_LEN), side="right"))(jax.random.split(arg_keys[1], SEQS)).reshape((SEQS, SEQ_LEN)).astype(jnp.int32)
    routes_keys = jax.random.split(jax.random.fold_in(arg_keys[2], 1), TOKENS // TOK_DEV)
    routes_turns = jax.random.permutation(jax.random.fold_in(arg_keys[2], 3), TOKENS // TOK_DEV)
    routes = jax.vmap(lambda own, number: routed_block(jax.random.fold_in(arg_keys[2], 2), own, number, TOK_DEV, EXPERTS, 1, CAP, 2))(routes_keys, routes_turns).reshape((TOKENS, 1))
    cotangent = centred(arg_keys[3], (TOKENS, D), 1.0, 6.0, ((0, 32),))
    w_qkv = centred(arg_keys[4], (D, 3 * D), D ** -0.5, 0.21875)
    w_attn_out = centred(arg_keys[5], (D, D), (D // 32) ** -0.5, 1.25)
    gain_attn = jnp.clip(1.0 + 0.1 * jax.random.normal(arg_keys[6], (D,), jnp.float32), 0.5, 1.5)
    gain_ffn = jnp.clip(1.0 + 0.1 * jax.random.normal(arg_keys[7], (D,), jnp.float32), 0.5, 1.5)
    w_router = centred(arg_keys[8], (D, RDIM), D ** -0.5, 0.21875)
    embed = centred(arg_keys[9], (EXPERTS, RDIM), 1.0, 5.0, (), jnp.float32)
    w_in = centred(arg_keys[10], (EXPERTS, D, FF), D ** -0.5, 0.21875, ((0, 8),))
    w_out = centred(arg_keys[11], (EXPERTS, FF, D), (max(FF // (EXPERTS * EXPERTS), 1)) ** -0.5, 0.875, ((0, 8),))
    return {"tokens": tokens, "segments": segments, "routes": routes, "cotangent": cotangent, "w_qkv": w_qkv, "w_attn_out": w_attn_out, "gain_attn": gain_attn, "gain_ffn": gain_ffn, "w_router": w_router, "embed": embed, "w_in": w_in, "w_out": w_out}


ROUTER_WARMTH = 0.3
NORM_FLOOR = 12.0
EPSILON = 1e-05
MASK_VALUE = -1e+30
TOP_PRECISION = lax.Precision.HIGHEST

@jax.custom_vjp
def low(v):
    return lax.optimization_barrier(v.astype(jnp.bfloat16)).astype(jnp.float32)

@jax.custom_vjp
def low_back(v):
    return v

def low_keep(v):
    return (low(v), None)

def low_pass(kept, grad):
    return (grad,)

def back_keep(v):
    return (v, None)

def back_low(kept, grad):
    return (low(grad),)
low.defvjp(low_keep, low_pass)
low_back.defvjp(back_keep, back_low)

def rms_scale(values, gain_vec):
    return values * lax.rsqrt(lax.optimization_barrier(jnp.mean(values * values, axis=-1, keepdims=True)) + EPSILON) * gain_vec

def attend_sequence(seq_rows, seq_marks, w_qkv, w_attn_out, gain_attn):
    length = seq_rows.shape[0]
    normed = low(rms_scale(seq_rows, gain_attn))
    router_projected = low(low_back(jnp.dot(normed, w_qkv, precision=TOP_PRECISION)))
    router_projected = router_projected.reshape(length, 3, HEADS, HEAD)
    queries = router_projected[:, 0]
    keys_all = router_projected[:, 1]
    values_all = router_projected[:, 2]
    cosine_scores = low_back(jnp.einsum('qhd,khd->hqk', queries, keys_all, precision=TOP_PRECISION) * HEAD ** (-0.5))
    places = jnp.arange(length)
    allowed = (places[:, None] >= places[None, :]) & (seq_marks[:, None] == seq_marks[None, :])
    cosine_scores = jnp.where(allowed[None], cosine_scores, MASK_VALUE)
    weights = jax.nn.softmax(cosine_scores, axis=-1)
    mixed_heads = jnp.einsum('hqk,khd->qhd', low(weights), values_all, precision=TOP_PRECISION)
    mixed_heads = low(low_back(mixed_heads.reshape(length, HEADS * HEAD)))
    branch = low_back(jnp.dot(mixed_heads, w_attn_out, precision=TOP_PRECISION))
    return seq_rows + branch

def gate_values(ffn_in, w_router, embed, routes):
    router_projected = jnp.dot(ffn_in, w_router, precision=TOP_PRECISION)
    router_projected = router_projected * lax.rsqrt(jnp.maximum(lax.optimization_barrier(jnp.sum(router_projected * router_projected, axis=-1, keepdims=True)), NORM_FLOOR))
    expert_centroids = embed * lax.rsqrt(jnp.maximum(lax.optimization_barrier(jnp.sum(embed * embed, axis=-1, keepdims=True)), NORM_FLOOR))
    router_logits = jnp.dot(router_projected, expert_centroids.T, precision=TOP_PRECISION) / ROUTER_WARMTH
    chances = jax.nn.softmax(router_logits, axis=-1)
    picked = routes == jnp.arange(embed.shape[0], dtype=jnp.int32)[None, :]
    return lax.optimization_barrier(jnp.sum(jnp.where(picked, chances, 0.0), axis=-1, keepdims=True))

def expert_block(expert_in, w_in_one, w_out_one):
    hidden = low_back(jnp.dot(expert_in, w_in_one, precision=TOP_PRECISION))
    activated = low(jax.nn.gelu(hidden, approximate=False))
    return low(low_back(jnp.dot(activated, w_out_one, precision=TOP_PRECISION)))

def slot_places(routes):
    chosen = routes[:, 0].reshape(DEVICES, TOK_DEV)
    onehot = (chosen[:, :, None] == jnp.arange(EXPERTS, dtype=jnp.int32)[None, None, :]).astype(jnp.int32)
    slot_rank = lax.optimization_barrier(jnp.sum((jnp.cumsum(onehot, axis=1) - 1) * onehot, axis=-1))
    owner = jnp.arange(DEVICES, dtype=jnp.int32)[:, None]
    return (chosen * (DEVICES * CAP) + owner * CAP + slot_rank).reshape(-1).astype(jnp.int32)

def reference(tokens, segments, routes, cotangent, w_qkv, w_attn_out, gain_attn, gain_ffn, w_router, embed, w_in, w_out):
    slot_index = slot_places(routes)

    def forward(input_batch, qkv_weight, attn_weight, gain_one, gain_two, router_weight, expert_centroids, first_weight, second_weight):
        attend = jax.checkpoint(lambda packed: attend_sequence(packed[0], packed[1], qkv_weight, attn_weight, gain_one))
        residual = lax.map(attend, (input_batch.reshape(SEQS, SEQ_LEN, D), segments)).reshape(TOKENS, D)
        ffn_in = low(rms_scale(residual, gain_two))
        gate_value = gate_values(ffn_in, router_weight, expert_centroids, routes)
        expert_in = low_back(ffn_in)
        buffer = jnp.zeros((EXPERTS * DEVICES * CAP, D), expert_in.dtype).at[slot_index].set(expert_in)
        run_one = jax.checkpoint(lambda packed: expert_block(packed[0], packed[1], packed[2]))
        returned = lax.map(run_one, (buffer.reshape(EXPERTS, DEVICES * CAP, D), first_weight, second_weight))
        expert_out = returned.reshape(EXPERTS * DEVICES * CAP, D)[slot_index]
        return residual + gate_value * expert_out
    result, pull = jax.vjp(forward, tokens.astype(jnp.float32), w_qkv.astype(jnp.float32), w_attn_out.astype(jnp.float32), gain_attn.astype(jnp.float32), gain_ffn.astype(jnp.float32), w_router.astype(jnp.float32), embed.astype(jnp.float32), w_in.astype(jnp.float32), w_out.astype(jnp.float32))
    grads = pull(cotangent.astype(jnp.float32))
    return (result.astype(jnp.bfloat16), grads[0], grads[1], grads[2], grads[3], grads[4], grads[5], grads[6], grads[7], grads[8])
```

```python
import functools

import jax
import jax.numpy as jnp
from jax import lax
from jax.experimental import pallas as pl
from jax.experimental.pallas import tpu as pltpu
from jax.sharding import PartitionSpec as P

HEADS = 12
HEAD = 64
PAIRS = HEADS // 2
PAIR = 2 * HEAD
QB = 256
LANES = 128
ROUTER_WARMTH = 0.3
NORM_FLOOR = 12.0
EPSILON = 1e-05
MASK_VALUE = -1e30
F32 = jnp.float32
BF16 = jnp.bfloat16
I32 = jnp.int32
NN = (((1,), (0,)), ((), ()))
NT = (((1,), (1,)), ((), ()))
TN = (((0,), (0,)), ((), ()))
HIGHEST = lax.Precision.HIGHEST
MIB = 1 << 20


def mm(a, b, dims=NN, precision=None):
    return lax.dot_general(a, b, dims, precision=precision, preferred_element_type=F32)


def params(mib):
    return pltpu.CompilerParams(vmem_limit_bytes=mib * MIB)


def cost(flops, nbytes):
    return pl.CostEstimate(flops=int(flops), bytes_accessed=int(nbytes), transcendentals=0)


def whole(shape):
    return pl.BlockSpec(
        shape, lambda *_: (0,) * len(shape), pipeline_mode=pl.Buffered(buffer_count=1)
    )


def smem():
    return pl.BlockSpec(memory_space=pltpu.SMEM)


def ones_where(mask):
    return jnp.where(mask, 1.0, 0.0).astype(BF16)


def dispatch(me, key_row, rows, out_refs):
    cap = out_refs[0].shape[0]
    slot = lax.broadcasted_iota(I32, (cap, key_row.shape[1]), 0)
    for d, ref in enumerate(out_refs):
        target = slot + (me ^ d) * cap
        ref[...] = mm(ones_where(key_row == target), rows).astype(BF16)


def place_kernel(me_ref, rr_ref, rc_ref, cot_ref, keyr_ref, keyc_ref, *out_refs):
    toks = cot_ref.shape[0]
    peers = len(out_refs)
    cap = out_refs[0].shape[0]
    rr, rc = rr_ref[...], rc_ref[...]
    before = ones_where(
        lax.broadcasted_iota(I32, (toks, toks), 0) <= lax.broadcasted_iota(I32, (toks, toks), 1)
    )
    hot_row = jnp.where(lax.broadcasted_iota(I32, (peers, toks), 0) == rr, 1.0, 0.0)
    upto = mm(hot_row.astype(BF16), before)
    rank = jnp.sum(hot_row * upto, axis=0, keepdims=True) - 1.0
    key_row = rr * cap + rank.astype(I32)
    keyr_ref[...] = key_row
    after = ones_where(
        lax.broadcasted_iota(I32, (toks, toks), 0) >= lax.broadcasted_iota(I32, (toks, toks), 1)
    )
    hot_col = jnp.where(lax.broadcasted_iota(I32, (toks, LANES), 1) == rc, 1.0, 0.0)
    upto_col = mm(after, hot_col.astype(BF16))
    rank_col = jnp.sum(hot_col * upto_col, axis=1, keepdims=True) - 1.0
    keyc_ref[...] = rc * cap + rank_col.astype(I32)
    dispatch(me_ref[0], key_row, cot_ref[...], out_refs)


def place(me, routes, cot, peers, cap):
    toks, width = cot.shape
    block = jax.ShapeDtypeStruct((cap, width), BF16)
    return pl.pallas_call(
        place_kernel,
        out_shape=[
            jax.ShapeDtypeStruct((1, toks), I32),
            jax.ShapeDtypeStruct((toks, 1), I32),
        ]
        + [block] * peers,
        in_specs=[smem()] + [pl.BlockSpec(memory_space=pltpu.VMEM)] * 3,
        compiler_params=params(40),
        cost_estimate=cost(2 * peers * cap * toks * width, 3 * toks * width * 2),
        name="place",
    )(me, routes.reshape(1, toks), routes, cot)


def band(i):
    return max(0, i - 2) * QB, (i + 1) * QB


def fill_bias(bias_ref, segr, segc, count):
    for i in range(count):
        low, high = band(i)
        keys = lax.broadcasted_iota(I32, (high - low, QB), 0) + low
        queries = lax.broadcasted_iota(I32, (high - low, QB), 1) + i * QB
        same = segc[low:high] == segr[:, i * QB : (i + 1) * QB]
        bias_ref[i, : high - low, :] = jnp.where((keys <= queries) & same, 0.0, MASK_VALUE)


def head_mask(values, h):
    lane = lax.broadcasted_iota(I32, values.shape, 1)
    return jnp.where((lane >= h * HEAD) & (lane < (h + 1) * HEAD), values, jnp.zeros_like(values))


def attend_kernel(
    peers,
    me_ref,
    tok_ref,
    segr_ref,
    segc_ref,
    keyr_ref,
    wq_ref,
    wk_ref,
    wv_ref,
    wo_ref,
    ga_ref,
    gf_ref,
    q_ref,
    k_ref,
    v_ref,
    lse_ref,
    mixt_ref,
    attn_ref,
    res_ref,
    *rest,
):
    out_refs, (bias_ref, mix_ref) = rest[:peers], rest[peers:]
    p = pl.program_id(0)
    toks, width = tok_ref.shape
    count = toks // QB

    @pl.when(p == 0)
    def _():
        fill_bias(bias_ref, segr_ref[...], segc_ref[...], count)
        x = tok_ref[...].astype(F32)
        inv = lax.rsqrt(jnp.mean(x * x, axis=1, keepdims=True) + EPSILON)
        attn_ref[...] = (x * inv * ga_ref[...]).astype(BF16)

    attn_in = attn_ref[...]
    q_ref[...] = mm(attn_in, wq_ref[...]).astype(BF16)
    k_ref[...] = mm(attn_in, wk_ref[...]).astype(BF16)
    v = mm(attn_in, wv_ref[...])
    v_ref[...] = v.astype(BF16)
    vt = v.T.astype(BF16)
    for i in range(count):
        low, high = band(i)
        cols = slice(i * QB, (i + 1) * QB)
        q = q_ref[cols, :] * HEAD**-0.5
        keys = k_ref[low:high, :]
        parts = []
        for h in range(2):
            s = mm(keys, head_mask(q, h), NT) + bias_ref[i, : high - low, :]
            top = jnp.max(s, axis=0, keepdims=True)
            w = jnp.exp(s - top)
            total = jnp.sum(w, axis=0, keepdims=True)
            lse_ref[0, h : h + 1, cols] = top + jnp.log(total)
            chances = (w * (1.0 / total)).astype(BF16)
            parts.append(mm(vt[h * HEAD : (h + 1) * HEAD, low:high], chances))
        mixt_ref[:, cols] = jnp.concatenate(parts, axis=0).astype(BF16)
    mix_ref[pl.ds(pl.multiple_of(p * PAIR, PAIR), PAIR), :] = mixt_ref[...]

    @pl.when(p == pl.num_programs(0) - 1)
    def _():
        res = tok_ref[...].astype(F32) + mm(mix_ref[...], wo_ref[...], TN)
        res_ref[...] = res
        inv = lax.rsqrt(jnp.mean(res * res, axis=1, keepdims=True) + EPSILON)
        ffn_in = (res * inv * gf_ref[...]).astype(BF16)
        dispatch(me_ref[0], keyr_ref[...], ffn_in, out_refs)


def attend(me, tokens, segr, segc, keyr, w_qkv, w_o, ga, gf, peers, cap):
    toks, width = tokens.shape
    pair_cols = pl.BlockSpec((toks, PAIR), lambda p: (0, p))
    heads = jax.ShapeDtypeStruct((toks, width), BF16)
    block = jax.ShapeDtypeStruct((cap, width), BF16)
    weights = [
        pl.BlockSpec((width, PAIR), lambda p, part=part: (0, part * PAIRS + p)) for part in range(3)
    ]
    return pl.pallas_call(
        functools.partial(attend_kernel, peers),
        grid=(PAIRS,),
        in_specs=[
            smem(),
            whole((toks, width)),
            whole((1, toks)),
            whole((toks, 1)),
            whole((1, toks)),
            *weights,
            whole((width, width)),
            whole((1, width)),
            whole((1, width)),
        ],
        out_specs=[
            pair_cols,
            pair_cols,
            pair_cols,
            pl.BlockSpec((1, 2, toks), lambda p: (p, 0, 0)),
            pl.BlockSpec((PAIR, toks), lambda p: (p, 0)),
            whole((toks, width)),
            whole((toks, width)),
        ]
        + [whole((cap, width))] * peers,
        out_shape=[
            heads,
            heads,
            heads,
            jax.ShapeDtypeStruct((PAIRS, 2, toks), F32),
            jax.ShapeDtypeStruct((width, toks), BF16),
            heads,
            jax.ShapeDtypeStruct((toks, width), F32),
        ]
        + [block] * peers,
        scratch_shapes=[
            pltpu.VMEM((toks // QB, 3 * QB, QB), F32),
            pltpu.VMEM((width, toks), BF16),
        ],
        compiler_params=params(56),
        cost_estimate=cost(20e9, 20e6),
        name="attend",
    )(me, tokens, segr, segc, keyr, w_qkv, w_qkv, w_qkv, w_o, ga, gf)


def attend_back_kernel(
    segr_ref,
    segc_ref,
    q_ref,
    k_ref,
    v_ref,
    lse_ref,
    mixt_ref,
    gb_ref,
    attnt_ref,
    wo_ref,
    wq_ref,
    wk_ref,
    wv_ref,
    gin_ref,
    gwo_ref,
    gwq_ref,
    gwk_ref,
    gwv_ref,
    gatt_ref,
    bias_ref,
    dqt_ref,
    dk_ref,
    dv_ref,
    do_ref,
):
    p = pl.program_id(0)
    toks, width = gb_ref.shape
    count = toks // QB
    scale = HEAD**-0.5

    @pl.when(p == 0)
    def _():
        fill_bias(bias_ref, segr_ref[...], segc_ref[...], count)
        gatt_ref[...] = gin_ref[...]

    gb = gb_ref[...]
    do_ref[...] = mm(gb, wo_ref[...], NT).astype(BF16)
    dot_ = mm(wo_ref[...], gb, NT).astype(BF16).astype(F32)
    mixt = mixt_ref[...]
    gwo_ref[...] = mm(mixt, gb).astype(BF16)
    weighted = dot_ * mixt.astype(F32)
    delta = [
        jnp.sum(weighted[h * HEAD : (h + 1) * HEAD], axis=0, keepdims=True) for h in range(2)
    ]
    kt = k_ref[...].astype(F32).T.astype(BF16)
    dk_ref[...] = jnp.zeros_like(dk_ref)
    dv_ref[...] = jnp.zeros_like(dv_ref)
    for i in range(count):
        low, high = band(i)
        cols = slice(i * QB, (i + 1) * QB)
        q = q_ref[cols, :] * scale
        do = do_ref[cols, :]
        keys = k_ref[low:high, :]
        values = v_ref[low:high, :]
        dk_add, dv_add, dqs = [], [], []
        for h in range(2):
            qm, dom = head_mask(q, h), head_mask(do, h)
            s = mm(keys, qm, NT) + bias_ref[i, : high - low, :]
            pr = jnp.exp(s - lse_ref[0, h : h + 1, cols])
            dpr = mm(values, dom, NT)
            ds = (pr * (dpr - delta[h][:, cols])).astype(BF16)
            dv_add.append(mm(pr.astype(BF16), dom))
            dk_add.append(mm(ds, qm))
            dqs.append(mm(kt[h * HEAD : (h + 1) * HEAD, low:high], ds))
        dk_ref[low:high, :] += dk_add[0] + dk_add[1]
        dv_ref[low:high, :] += dv_add[0] + dv_add[1]
        dqt_ref[:, cols] = jnp.concatenate(dqs, axis=0) * scale
    grads = [
        dqt_ref[...].T.astype(BF16),
        dk_ref[...].astype(BF16),
        dv_ref[...].astype(BF16),
    ]
    attnt = attnt_ref[...]
    for grad, ref in zip(grads, (gwq_ref, gwk_ref, gwv_ref)):
        ref[...] = mm(attnt, grad).astype(BF16)
    joined = jnp.concatenate(grads, axis=1)
    weights = jnp.concatenate([wq_ref[...], wk_ref[...], wv_ref[...]], axis=1)
    gatt_ref[...] += mm(joined, weights, NT)


def attend_back(first, pairs, segr, segc, q, k, v, lse, mixt, gb, attnt, w_o, w_qkv, gin):
    toks, width = gb.shape
    pair_cols = pl.BlockSpec((toks, PAIR), lambda p: (0, first + p))
    weights = [
        pl.BlockSpec((width, PAIR), lambda p, part=part: (0, part * PAIRS + first + p))
        for part in range(3)
    ]
    grad_cols = pl.BlockSpec((width, PAIR), lambda p: (0, p))
    grad_w = jax.ShapeDtypeStruct((width, pairs * PAIR), BF16)
    return pl.pallas_call(
        attend_back_kernel,
        grid=(pairs,),
        in_specs=[
            whole((1, toks)),
            whole((toks, 1)),
            pair_cols,
            pair_cols,
            pair_cols,
            pl.BlockSpec((1, 2, toks), lambda p: (first + p, 0, 0)),
            pl.BlockSpec((PAIR, toks), lambda p: (first + p, 0)),
            whole((toks, width)),
            whole((width, toks)),
            pl.BlockSpec((PAIR, width), lambda p: (first + p, 0)),
            *weights,
            whole((toks, width)),
        ],
        out_specs=[
            pl.BlockSpec((PAIR, width), lambda p: (p, 0)),
            grad_cols,
            grad_cols,
            grad_cols,
            whole((toks, width)),
        ],
        out_shape=[
            jax.ShapeDtypeStruct((pairs * PAIR, width), BF16),
            grad_w,
            grad_w,
            grad_w,
            jax.ShapeDtypeStruct((toks, width), F32),
        ],
        scratch_shapes=[
            pltpu.VMEM((toks // QB, 3 * QB, QB), F32),
            pltpu.VMEM((PAIR, toks), F32),
            pltpu.VMEM((toks, PAIR), F32),
            pltpu.VMEM((toks, PAIR), F32),
            pltpu.VMEM((toks, PAIR), BF16),
        ],
        compiler_params=params(56),
        cost_estimate=cost(pairs * 5e9, 20e6),
        name="attend_back",
    )(segr, segc, q, k, v, lse, mixt, gb, attnt, w_o, w_qkv, w_qkv, w_qkv, gin)


def unit_rows(values):
    total = jnp.sum(values * values, axis=1, keepdims=True)
    return lax.rsqrt(jnp.maximum(total, NORM_FLOOR)), total


def unit_rows_back(values, inv, total, grad):
    passed = jnp.where(total > NORM_FLOOR, 1.0, jnp.where(total == NORM_FLOOR, 0.5, 0.0))
    inner = jnp.sum(grad * values, axis=1, keepdims=True)
    return inv * grad - passed * inv * inv * inv * inner * values


def gelu_and_slope(h):
    cdf = 0.5 + 0.5 * lax.erf(h * 0.7071067811865476)
    pdf = 0.3989422804014327 * jnp.exp(-0.5 * h * h)
    return h * cdf, cdf + h * pdf


def expert_kernel(peers, experts, me_ref, wr_ref, emb_ref, win_ref, wout_ref, *rest):
    x_refs, rest = rest[:peers], rest[peers:]
    g_refs, rest = rest[:peers], rest[peers:]
    gwin_ref, gwout_ref, gwr_ref, gemb_ref = rest[:4]
    rest = rest[4:]
    fout_refs, rest = rest[:peers], rest[peers:]
    gout_refs, rest = rest[:peers], rest[peers:]
    x_s, xt_s, g_s, act_s, gp_s, out_s, gin_s, acc_s = rest
    c = pl.program_id(0)
    rows = x_s.shape[0]
    cap = x_refs[0].shape[0]
    me = me_ref[0]
    step = min(QB, rows)

    def route(block):
        z = mm(block, wr_ref[...])
        inv, total = unit_rows(z)
        zn = z * inv
        einv, _ = unit_rows(emb_ref[...])
        en = emb_ref[...] * einv
        logits = mm(zn, en, NT, HIGHEST) / ROUTER_WARMTH
        lane = lax.broadcasted_iota(I32, logits.shape, 1)
        logits = jnp.where(lane < experts, logits, MASK_VALUE)
        w = jnp.exp(logits - jnp.max(logits, axis=1, keepdims=True))
        chances = w / jnp.sum(w, axis=1, keepdims=True)
        mine = lane == me
        gate = jnp.sum(jnp.where(mine, chances, 0.0), axis=1, keepdims=True)
        return z, inv, total, zn, en, chances, mine, gate

    @pl.when(c == 0)
    def _():
        for d in range(peers):
            x_s[d * cap : (d + 1) * cap, :] = x_refs[d][...]
            g_s[d * cap : (d + 1) * cap, :] = g_refs[d][...]
        for r in range(0, rows, step):
            block = x_s[r : r + step, :]
            xt_s[:, r : r + step] = block.T
            gate = route(block)[-1]
            g_s[r : r + step, :] = (gate * g_s[r : r + step, :].astype(F32)).astype(BF16)
        out_s[...] = jnp.zeros_like(out_s)
        gin_s[...] = jnp.zeros_like(gin_s)
        acc_s[...] = jnp.zeros_like(acc_s)

    w_in, w_out = win_ref[0], wout_ref[0]
    for r in range(0, rows, step):
        part = slice(r, r + step)
        h = mm(x_s[part, :], w_in)
        act, slope = gelu_and_slope(h)
        act_s[part, :] = act.astype(BF16)
        ga = mm(g_s[part, :], w_out, NT)
        gp_s[part, :] = (ga * slope).astype(BF16)
        prod = act * ga
        folded = prod[:, :LANES]
        for j in range(LANES, prod.shape[1], LANES):
            folded = folded + prod[:, j : j + LANES]
        acc_s[part, :] += folded
    act16, gp16 = act_s[...], gp_s[...]
    out_s[...] += mm(act16, w_out)
    gin_s[...] += mm(gp16, w_in, NT)
    gwout_ref[...] = mm(act16, g_s[...], TN).astype(BF16)
    gwin_ref[0] = mm(xt_s[...], gp16).astype(BF16)

    @pl.when(c == pl.num_programs(0) - 1)
    def _():
        gwr = jnp.zeros(gwr_ref.shape, F32)
        gen = jnp.zeros(gemb_ref.shape, F32)
        for r in range(0, rows, step):
            part = slice(r, r + step)
            z, inv, total, zn, en, chances, mine, gate = route(x_s[part, :])
            weight = jnp.sum(acc_s[part, :], axis=1, keepdims=True)
            dl = weight * (jnp.where(mine, 1.0, 0.0) - chances) / ROUTER_WARMTH
            gen = gen + mm(dl, zn, TN, HIGHEST)
            dz = unit_rows_back(z, inv, total, mm(dl, en, NN, HIGHEST))
            dz_top = dz.astype(BF16)
            dz_low = (dz - dz_top.astype(F32)).astype(BF16)
            back = gin_s[part, :].astype(BF16).astype(F32)
            back = back + mm(dz_top, wr_ref[...], NT) + mm(dz_low, wr_ref[...], NT)
            gin_s[part, :] = back
            xt = xt_s[:, part]
            gwr = gwr + mm(xt, dz_top) + mm(xt, dz_low)
            out_s[part, :] = gate * out_s[part, :].astype(BF16).astype(F32)
        for d in range(peers):
            gout_refs[d][...] = gin_s[d * cap : (d + 1) * cap, :].astype(BF16)
            fout_refs[d][...] = out_s[d * cap : (d + 1) * cap, :].astype(BF16)
        gwr_ref[...] = gwr
        einv, etotal = unit_rows(emb_ref[...])
        gemb_ref[...] = unit_rows_back(emb_ref[...], einv, etotal, gen)


def expert(me, wr, emb, w_in, w_out, xs, gs, experts, shards):
    peers = len(xs)
    cap, width = xs[0].shape
    hidden = w_in.shape[2]
    share = hidden // shards
    wide = 256 if share % 256 == 0 else 128
    per = share // wide
    rows = peers * cap
    block = jax.ShapeDtypeStruct((cap, width), BF16)
    return pl.pallas_call(
        functools.partial(expert_kernel, peers, experts),
        grid=(hidden // wide,),
        in_specs=[
            smem(),
            whole(wr.shape),
            whole(emb.shape),
            pl.BlockSpec((1, width, wide), lambda c: (0, 0, c)),
            pl.BlockSpec((1, wide, width), lambda c: (0, c, 0)),
        ]
        + [whole((cap, width))] * (2 * peers),
        out_specs=[
            pl.BlockSpec((1, width, wide), lambda c: (c // per, 0, c % per)),
            pl.BlockSpec((wide, width), lambda c: (c, 0)),
            whole((width, LANES)),
            whole(emb.shape),
        ]
        + [whole((cap, width))] * (2 * peers),
        out_shape=[
            jax.ShapeDtypeStruct((shards, width, share), BF16),
            jax.ShapeDtypeStruct((hidden, width), BF16),
            jax.ShapeDtypeStruct((width, LANES), F32),
            jax.ShapeDtypeStruct(emb.shape, F32),
        ]
        + [block] * (2 * peers),
        scratch_shapes=[
            pltpu.VMEM((rows, width), BF16),
            pltpu.VMEM((width, rows), BF16),
            pltpu.VMEM((rows, width), BF16),
            pltpu.VMEM((rows, wide), BF16),
            pltpu.VMEM((rows, wide), BF16),
            pltpu.VMEM((rows, width), F32),
            pltpu.VMEM((rows, width), F32),
            pltpu.VMEM((rows, LANES), F32),
        ],
        compiler_params=params(60),
        cost_estimate=cost(12 * rows * width * hidden, 50e6),
        name="expert",
    )(me, wr, emb, w_in, w_out, *xs, *gs)


def gather_rows(me, keys, rows_ref, peers):
    total = rows_ref.shape[0]
    cap = total // peers
    column = lax.broadcasted_iota(I32, (keys.shape[0], total), 1)
    target = ((column // cap) ^ me) * cap + column % cap
    return mm(ones_where(keys == target), rows_ref[...])


def stage_rows(block_refs, rows_ref):
    cap = block_refs[0].shape[0]

    @pl.when(pl.program_id(0) == 0)
    def _():
        for d, ref in enumerate(block_refs):
            rows_ref[d * cap : (d + 1) * cap, :] = ref[...]


def combine_back_kernel(peers, me_ref, keyc_ref, res_ref, cot_ref, gf_ref, *rest):
    gres_ref, gb_ref, gain_ref, rows_ref = rest[peers:]
    stage_rows(rest[:peers], rows_ref)
    dy = gather_rows(me_ref[0], keyc_ref[...], rows_ref, peers)
    x = res_ref[...]
    inv = lax.rsqrt(jnp.mean(x * x, axis=1, keepdims=True) + EPSILON)

    @pl.when(pl.program_id(0) == 0)
    def _():
        gain_ref[...] = jnp.zeros_like(gain_ref)

    gain_ref[...] += jnp.sum(dy * x * inv, axis=0, keepdims=True)
    dn = dy * gf_ref[...]
    dx = inv * dn - x * (inv * inv * inv * jnp.mean(x * dn, axis=1, keepdims=True))
    grad = cot_ref[...].astype(F32) + dx
    gres_ref[...] = grad
    gb_ref[...] = grad.astype(BF16)


def combine_back(me, keyc, res, cot, gf, blocks):
    toks, width = res.shape
    peers = len(blocks)
    cap = blocks[0].shape[0]
    tile = pl.BlockSpec((QB, width), lambda i: (i, 0))
    return pl.pallas_call(
        functools.partial(combine_back_kernel, peers),
        grid=(toks // QB,),
        in_specs=[smem(), pl.BlockSpec((QB, 1), lambda i: (i, 0)), tile, tile, whole((1, width))]
        + [whole((cap, width))] * peers,
        out_specs=[tile, tile, whole((1, width))],
        out_shape=[
            jax.ShapeDtypeStruct((toks, width), F32),
            jax.ShapeDtypeStruct((toks, width), BF16),
            jax.ShapeDtypeStruct((1, width), F32),
        ],
        scratch_shapes=[pltpu.VMEM((peers * cap, width), BF16)],
        compiler_params=params(40),
        cost_estimate=cost(2 * toks * peers * cap * width, 15e6),
        name="combine_back",
    )(me, keyc, res, cot, gf, *blocks)


def combine_kernel(peers, me_ref, keyc_ref, res_ref, *rest):
    out_ref, rows_ref = rest[peers:]
    stage_rows(rest[:peers], rows_ref)
    back = gather_rows(me_ref[0], keyc_ref[...], rows_ref, peers)
    out_ref[...] = (res_ref[...] + back).astype(BF16)


def combine(me, keyc, res, blocks):
    toks, width = res.shape
    peers = len(blocks)
    cap = blocks[0].shape[0]
    tile = pl.BlockSpec((QB, width), lambda i: (i, 0))
    return pl.pallas_call(
        functools.partial(combine_kernel, peers),
        grid=(toks // QB,),
        in_specs=[smem(), pl.BlockSpec((QB, 1), lambda i: (i, 0)), tile]
        + [whole((cap, width))] * peers,
        out_specs=tile,
        out_shape=jax.ShapeDtypeStruct((toks, width), BF16),
        scratch_shapes=[pltpu.VMEM((peers * cap, width), BF16)],
        compiler_params=params(40),
        cost_estimate=cost(2 * toks * peers * cap * width, 10e6),
        name="combine",
    )(me, keyc, res, *blocks)


def norm_back_kernel(gatt_ref, tok_ref, gres_ref, ga_ref, out_ref, gain_ref):
    dy = gatt_ref[...]
    x = tok_ref[...].astype(F32)
    inv = lax.rsqrt(jnp.mean(x * x, axis=1, keepdims=True) + EPSILON)

    @pl.when(pl.program_id(0) == 0)
    def _():
        gain_ref[...] = jnp.zeros_like(gain_ref)

    gain_ref[...] += jnp.sum(dy * x * inv, axis=0, keepdims=True)
    dn = dy * ga_ref[...]
    dx = inv * dn - x * (inv * inv * inv * jnp.mean(x * dn, axis=1, keepdims=True))
    out_ref[...] = gres_ref[...] + dx


def norm_back(gatt, tokens, gres, ga):
    toks, width = tokens.shape
    tile = pl.BlockSpec((QB, width), lambda i: (i, 0))
    return pl.pallas_call(
        norm_back_kernel,
        grid=(toks // QB,),
        in_specs=[tile, tile, tile, whole((1, width))],
        out_specs=[tile, whole((1, width))],
        out_shape=[
            jax.ShapeDtypeStruct((toks, width), F32),
            jax.ShapeDtypeStruct((1, width), F32),
        ],
        compiler_params=params(32),
        cost_estimate=cost(20 * toks * width, 12 * toks * width),
        name="norm_back",
    )(gatt, tokens, gres, ga)


def exchange(blocks):
    peers = len(blocks)
    return [blocks[0]] + [
        lax.ppermute(blocks[d], "expert", [(j, j ^ d) for j in range(peers)])
        for d in range(1, peers)
    ]


def halve(value, axis, bit):
    size = lax.axis_size(axis)
    half = value.shape[0] // 2
    up = (lax.axis_index(axis) >> bit) & 1
    keep = lax.dynamic_slice_in_dim(value, up * half, half, 0)
    send = lax.dynamic_slice_in_dim(value, (1 - up) * half, half, 0)
    got = lax.ppermute(send, axis, [(j, j ^ (1 << bit)) for j in range(size)])
    return (keep.astype(F32) + got.astype(F32)).astype(BF16)


def double(value, axis, bit):
    size = lax.axis_size(axis)
    up = (lax.axis_index(axis) >> bit) & 1
    got = lax.ppermute(value, axis, [(j, j ^ (1 << bit)) for j in range(size)])
    return jnp.where(
        up == 1, jnp.concatenate([got, value], 0), jnp.concatenate([value, got], 0)
    )


def total_over_all(value, flip):
    bits = list(range((lax.axis_size("expert") - 1).bit_length()))
    if flip:
        bits = bits[:1] + bits[1:][::-1]
    for bit in bits:
        value = halve(value, "expert", bit)
    groups = lax.axis_size("dp")
    total = value.astype(F32)
    for d in range(1, groups):
        total = total + lax.ppermute(value, "dp", [(j, j ^ d) for j in range(groups)]).astype(F32)
    value = total.astype(BF16)
    for bit in bits[::-1]:
        value = double(value, "expert", bit)
    return value


def sum_shared(parts):
    sizes = [part.shape[0] for part in parts]
    joined = jnp.concatenate(parts, axis=0)
    half = joined.shape[0] // 2
    total = jnp.concatenate(
        [total_over_all(joined[:half], False), total_over_all(joined[half:], True)], axis=0
    ).astype(F32)
    outs, at = [], 0
    for size in sizes:
        outs.append(total[at : at + size])
        at += size
    return outs


def on_device(
    tokens,
    segments,
    routes,
    cotangent,
    w_qkv,
    w_attn_out,
    gain_attn,
    gain_ffn,
    w_router,
    embed,
    w_in,
    w_out,
):
    toks, width = tokens.shape
    experts, rdim = embed.shape
    peers = lax.axis_size("expert")
    shards = lax.axis_size("dp")
    cap = 2 * toks // experts
    me = lax.axis_index("expert").astype(I32).reshape(1)
    ga, gf = gain_attn.reshape(1, width), gain_ffn.reshape(1, width)
    segr, segc = segments.reshape(1, toks), segments.reshape(toks, 1)
    wr = jnp.pad(w_router, ((0, 0), (0, LANES - rdim)))
    emb = jnp.pad(embed, ((0, LANES - experts), (0, LANES - rdim)))

    keyr, keyc, *g_blocks = place(me, routes, cotangent, peers, cap)
    g_rows = exchange(g_blocks)
    q, k, v, lse, mixt, attn_in, res, *x_blocks = attend(
        me, tokens, segr, segc, keyr, w_qkv, w_attn_out, ga, gf, peers, cap
    )
    x_rows = exchange(x_blocks)
    attnt = attn_in.T
    gwin, gwout, gwr, gemb, *outs = expert(
        me, wr, emb, w_in, w_out, x_rows, g_rows, experts, shards
    )
    fouts, gouts = outs[:peers], outs[peers:]
    grad_w_out = lax.psum_scatter(gwout, "dp", scatter_dimension=0, tiled=True)
    grad_w_in = lax.psum_scatter(gwin, "dp", scatter_dimension=0, tiled=True)
    gback = exchange(gouts)
    gres, gb, ggf = combine_back(me, keyc, res, cotangent, gf, gback)
    fback = exchange(fouts)
    out_tokens = combine(me, keyc, res, fback)

    half = PAIRS // 2
    gatt = jnp.zeros((toks, width), F32)
    sums = []
    for first in (0, half):
        gwo, gwq, gwk, gwv, gatt = attend_back(
            first, half, segr, segc, q, k, v, lse, mixt, gb, attnt, w_attn_out, w_qkv, gatt
        )
        sums.append(sum_shared([gwo.reshape(width, -1), gwq, gwk, gwv]))
    grad_tokens, gga = norm_back(gatt, tokens, gres, ga)
    small = lax.psum(
        jnp.concatenate([gga.reshape(-1), ggf.reshape(-1), gwr[:, :rdim].reshape(-1), gemb[:experts, :rdim].reshape(-1)]),
        ("dp", "expert"),
    )
    grad_gain_attn = small[:width]
    grad_gain_ffn = small[width : 2 * width]
    grad_router = small[2 * width : (2 + rdim) * width].reshape(width, rdim)
    grad_embed = small[(2 + rdim) * width :].reshape(experts, rdim)
    grad_w_qkv = jnp.concatenate([sums[s][1 + part] for part in range(3) for s in range(2)], axis=1)
    grad_w_attn_out = jnp.concatenate(
        [sums[s][0].reshape(-1, width) for s in range(2)], axis=0
    )
    return (
        out_tokens,
        grad_tokens,
        grad_w_qkv,
        grad_w_attn_out,
        grad_gain_attn,
        grad_gain_ffn,
        grad_router,
        grad_embed,
        grad_w_in.astype(F32),
        grad_w_out.astype(F32)[None],
    )


def solution(mesh):
    rows = P(("dp", "expert"), None)
    return jax.shard_map(
        on_device,
        mesh=mesh,
        in_specs=(
            rows,
            rows,
            rows,
            rows,
            P(),
            P(),
            P(),
            P(),
            P(),
            P(),
            P("expert", None, None),
            P("expert", None, None),
        ),
        out_specs=(
            rows,
            rows,
            P(),
            P(),
            P(),
            P(),
            P(),
            P(),
            P("expert", None, "dp"),
            P("expert", "dp", None),
        ),
        check_vma=False,
    )
```

```python
import functools

import jax
import jax.numpy as jnp
from jax import lax
from jax.experimental import pallas as pl
from jax.experimental.pallas import tpu as pltpu
from jax.sharding import PartitionSpec as P

HEADS = 12
HEAD = 64
PAIRS = HEADS // 2
PAIR = 2 * HEAD
QB = 256
LANES = 128
ROUTER_WARMTH = 0.3
NORM_FLOOR = 12.0
EPSILON = 1e-05
MASK_VALUE = -1e30
F32 = jnp.float32
BF16 = jnp.bfloat16
I32 = jnp.int32
NN = (((1,), (0,)), ((), ()))
NT = (((1,), (1,)), ((), ()))
TN = (((0,), (0,)), ((), ()))
HIGHEST = lax.Precision.HIGHEST
MIB = 1 << 20


def mm(a, b, dims=NN, precision=None):
    return lax.dot_general(a, b, dims, precision=precision, preferred_element_type=F32)


def params(mib):
    return pltpu.CompilerParams(vmem_limit_bytes=mib * MIB)


def cost(micros, nbytes=0):
    return pl.CostEstimate(
        flops=int(micros * 1.15e9), bytes_accessed=int(nbytes), transcendentals=0
    )


def whole(shape):
    return pl.BlockSpec(
        shape, lambda *_: (0,) * len(shape), pipeline_mode=pl.Buffered(buffer_count=1)
    )


def smem():
    return pl.BlockSpec(memory_space=pltpu.SMEM)


def norm_back(x, gain, dy):
    inv = lax.rsqrt(jnp.mean(x * x, axis=1, keepdims=True) + EPSILON)
    dn = dy * gain
    dx = inv * dn - x * (inv * inv * inv * jnp.mean(x * dn, axis=1, keepdims=True))
    return dx, jnp.sum(dy * x * inv, axis=0, keepdims=True)


def column_of(row):
    return jnp.broadcast_to(row.astype(F32), (8, row.shape[1])).T[:, :1].astype(row.dtype)


def ones_where(mask):
    return jnp.where(mask, 1.0, 0.0).astype(BF16)


def dispatch(key_row, rows, out_refs):
    at = 0
    for ref in out_refs:
        step = min(2 * QB, ref.shape[0])
        for r in range(0, ref.shape[0], step):
            slot = lax.broadcasted_iota(I32, (step, key_row.shape[1]), 0) + at
            ref[r : r + step, :] = mm(ones_where(key_row == slot), rows).astype(BF16)
            at += step


def place_kernel(peers, rr_ref, cot_ref, keyr_ref, g_ref):
    toks = cot_ref.shape[0]
    cap = g_ref.shape[0] // peers
    half = cap // 2
    rr = rr_ref[...]
    before = ones_where(
        lax.broadcasted_iota(I32, (toks, toks), 0) <= lax.broadcasted_iota(I32, (toks, toks), 1)
    )
    hot_row = jnp.where(lax.broadcasted_iota(I32, (peers, toks), 0) == rr, 1.0, 0.0)
    upto = mm(hot_row.astype(BF16), before)
    rank = (jnp.sum(hot_row * upto, axis=0, keepdims=True) - 1.0).astype(I32)
    keyr_ref[...] = rr * half + jnp.where(rank < half, rank, rank + (peers - 1) * half)
    dispatch(rr * cap + rank, cot_ref[...], (g_ref,))


def place(routes, cot, peers, slots):
    toks, width = cot.shape
    return pl.pallas_call(
        functools.partial(place_kernel, peers),
        out_shape=[
            jax.ShapeDtypeStruct((1, toks), I32),
            jax.ShapeDtypeStruct((slots, width), BF16),
        ],
        in_specs=[pl.BlockSpec(memory_space=pltpu.VMEM)] * 2,
        compiler_params=params(40),
        cost_estimate=cost(5),
        name="place",
    )(routes, cot)


def band(i):
    return max(0, i - 2) * QB, (i + 1) * QB


def fill_bias(bias_ref, segr, count):
    segc = column_of(segr)
    for i in range(count):
        low, high = band(i)
        keys = lax.broadcasted_iota(I32, (high - low, QB), 0) + low
        queries = lax.broadcasted_iota(I32, (high - low, QB), 1) + i * QB
        same = segc[low:high] == segr[:, i * QB : (i + 1) * QB]
        bias_ref[i, : high - low, :] = jnp.where((keys <= queries) & same, 0.0, MASK_VALUE)


def head_mask(values, h):
    lane = lax.broadcasted_iota(I32, values.shape, 1)
    return jnp.where((lane >= h * HEAD) & (lane < (h + 1) * HEAD), values, jnp.zeros_like(values))


def attend_kernel(
    tok_ref,
    segr_ref,
    keyr_ref,
    wq_ref,
    wk_ref,
    wv_ref,
    wo_ref,
    ga_ref,
    gf_ref,
    q_ref,
    k_ref,
    v_ref,
    lse_ref,
    mixt_ref,
    attn_ref,
    res_ref,
    xa_ref,
    xb_ref,
    bias_ref,
    mix_ref,
):
    p = pl.program_id(0)
    toks, width = tok_ref.shape
    count = toks // QB

    @pl.when(p == 0)
    def _():
        fill_bias(bias_ref, segr_ref[...], count)
        x = tok_ref[...].astype(F32)
        inv = lax.rsqrt(jnp.mean(x * x, axis=1, keepdims=True) + EPSILON)
        attn_ref[...] = (x * inv * ga_ref[...]).astype(BF16)

    attn_in = attn_ref[...]
    weights = jnp.concatenate([wq_ref[...], wk_ref[...], wv_ref[...]], axis=1)
    qkv = mm(attn_in, weights)
    q_ref[...] = qkv[:, :PAIR].astype(BF16)
    k_ref[...] = qkv[:, PAIR : 2 * PAIR].astype(BF16)
    v = qkv[:, 2 * PAIR :]
    v_ref[...] = v.astype(BF16)
    vt = v.T.astype(BF16)
    for i in range(count):
        low, high = band(i)
        cols = slice(i * QB, (i + 1) * QB)
        q = q_ref[cols, :] * HEAD**-0.5
        keys = k_ref[low:high, :]
        parts = []
        for h in range(2):
            s = mm(keys, head_mask(q, h), NT) + bias_ref[i, : high - low, :]
            top = jnp.max(s, axis=0, keepdims=True)
            w = jnp.exp(s - top)
            total = jnp.sum(w, axis=0, keepdims=True)
            lse_ref[0, h : h + 1, cols] = top + jnp.log(total)
            chances = (w * (1.0 / total)).astype(BF16)
            parts.append(mm(vt[h * HEAD : (h + 1) * HEAD, low:high], chances))
        mixt_ref[:, cols] = jnp.concatenate(parts, axis=0).astype(BF16)
    mix_ref[pl.ds(pl.multiple_of(p * PAIR, PAIR), PAIR), :] = mixt_ref[...]

    @pl.when(p == pl.num_programs(0) - 1)
    def _():
        res = tok_ref[...].astype(F32) + mm(mix_ref[...], wo_ref[...], TN)
        res_ref[...] = res
        inv = lax.rsqrt(jnp.mean(res * res, axis=1, keepdims=True) + EPSILON)
        ffn_in = (res * inv * gf_ref[...]).astype(BF16)
        dispatch(keyr_ref[...], ffn_in, (xa_ref, xb_ref))


def attend(tokens, segr, keyr, w_qkv, w_o, ga, gf):
    toks, width = tokens.shape
    pair_cols = pl.BlockSpec((toks, PAIR), lambda p: (0, p))
    heads = jax.ShapeDtypeStruct((toks, width), BF16)
    weights = [
        pl.BlockSpec((width, PAIR), lambda p, part=part: (0, part * PAIRS + p)) for part in range(3)
    ]
    return pl.pallas_call(
        attend_kernel,
        grid=(PAIRS,),
        in_specs=[
            whole((toks, width)),
            whole((1, toks)),
            whole((1, toks)),
            *weights,
            whole((width, width)),
            whole((1, width)),
            whole((1, width)),
        ],
        out_specs=[
            pair_cols,
            pair_cols,
            pair_cols,
            pl.BlockSpec((1, 2, toks), lambda p: (p, 0, 0)),
            pl.BlockSpec((PAIR, toks), lambda p: (p, 0)),
            whole((toks, width)),
            whole((toks, width)),
            whole((toks, width)),
            whole((toks, width)),
        ],
        out_shape=[
            heads,
            heads,
            heads,
            jax.ShapeDtypeStruct((PAIRS, 2, toks), F32),
            jax.ShapeDtypeStruct((width, toks), BF16),
            heads,
            jax.ShapeDtypeStruct((toks, width), F32),
            heads,
            heads,
        ],
        scratch_shapes=[
            pltpu.VMEM((toks // QB, 3 * QB, QB), F32),
            pltpu.VMEM((width, toks), BF16),
        ],
        compiler_params=params(56),
        cost_estimate=cost(42),
        name="attend",
    )(tokens, segr, keyr, w_qkv, w_qkv, w_qkv, w_o, ga, gf)


def attend_back_kernel(
    last,
    core_ref,
    segr_ref,
    q_ref,
    k_ref,
    v_ref,
    lse_ref,
    mixt_ref,
    gb_ref,
    attnt_ref,
    wo_ref,
    wq_ref,
    wk_ref,
    wv_ref,
    *rest,
):
    if last:
        gin_ref, tok_ref, gres_ref, ga_ref, send_ref, keep_ref, gtok_ref, gain_ref, gatt_ref = rest[:9]
    else:
        gin_ref, send_ref, keep_ref, gatt_ref = rest[:4]
    bias_ref, dqt_ref, dk_ref, dv_ref, do_ref = rest[-5:]
    p = pl.program_id(0)
    toks, width = gb_ref.shape
    count = toks // QB
    scale = HEAD**-0.5

    @pl.when(p == 0)
    def _():
        fill_bias(bias_ref, segr_ref[...], count)
        gatt_ref[...] = gin_ref[...]

    gb = gb_ref[...]
    do_ref[...] = mm(gb, wo_ref[...], NT).astype(BF16)
    dot_ = mm(wo_ref[...], gb, NT).astype(BF16).astype(F32)
    mixt = mixt_ref[...]
    gwo = mm(mixt, gb).astype(BF16)
    weighted = dot_ * mixt.astype(F32)
    delta = [
        jnp.sum(weighted[h * HEAD : (h + 1) * HEAD], axis=0, keepdims=True) for h in range(2)
    ]
    kt = k_ref[...].astype(F32).T.astype(BF16)
    dk_ref[...] = jnp.zeros_like(dk_ref)
    dv_ref[...] = jnp.zeros_like(dv_ref)
    for i in range(count):
        low, high = band(i)
        cols = slice(i * QB, (i + 1) * QB)
        q = q_ref[cols, :] * scale
        do = do_ref[cols, :]
        keys = k_ref[low:high, :]
        values = v_ref[low:high, :]
        dk_add, dv_add, dqs = [], [], []
        for h in range(2):
            qm, dom = head_mask(q, h), head_mask(do, h)
            s = mm(keys, qm, NT) + bias_ref[i, : high - low, :]
            pr = jnp.exp(s - lse_ref[0, h : h + 1, cols])
            dpr = mm(values, dom, NT)
            ds = (pr * (dpr - delta[h][:, cols])).astype(BF16)
            dv_add.append(mm(pr.astype(BF16), dom))
            dk_add.append(mm(ds, qm))
            dqs.append(mm(kt[h * HEAD : (h + 1) * HEAD, low:high], ds))
        dk_ref[low:high, :] += dk_add[0] + dk_add[1]
        dv_ref[low:high, :] += dv_add[0] + dv_add[1]
        dqt_ref[:, cols] = jnp.concatenate(dqs, axis=0) * scale
    grads = [
        dqt_ref[...].T.astype(BF16),
        dk_ref[...].astype(BF16),
        dv_ref[...].astype(BF16),
    ]
    joined = jnp.concatenate(grads, axis=1)
    gw = mm(attnt_ref[...], joined).astype(BF16)
    for turn, ref in enumerate((send_ref, keep_ref)):

        @pl.when(p == turn)
        def _(ref=ref):
            for part in range(3):
                ref[part] = gw[:, part * PAIR : (part + 1) * PAIR]
            for j in range(width // PAIR):
                ref[3, j * PAIR : (j + 1) * PAIR, :] = gwo[:, j * PAIR : (j + 1) * PAIR]

    weights = jnp.concatenate([wq_ref[...], wk_ref[...], wv_ref[...]], axis=1)
    gatt_ref[...] += mm(joined, weights, NT)

    if last:

        @pl.when(p == pl.num_programs(0) - 1)
        def _():
            gain = jnp.zeros(gain_ref.shape, F32)
            for i in range(count):
                part = slice(i * QB, (i + 1) * QB)
                dx, dgain = norm_back(tok_ref[part, :].astype(F32), ga_ref[...], gatt_ref[part, :])
                gtok_ref[part, :] = gres_ref[part, :] + dx
                gain = gain + dgain
            gain_ref[...] = gain


def attend_back(first, core, segr, q, k, v, lse, mixt, gb, attnt, w_o, w_qkv, gin, final):
    toks, width = gb.shape

    def pair(p, core_ref):
        return first + jnp.where(p == 0, 1 - core_ref[0], core_ref[0])

    def fixed(shape):
        return pl.BlockSpec(
            shape, lambda p, c: (0,) * len(shape), pipeline_mode=pl.Buffered(buffer_count=1)
        )

    pair_cols = pl.BlockSpec((toks, PAIR), lambda p, c: (0, pair(p, c)))
    weights = [
        pl.BlockSpec((width, PAIR), lambda p, c, part=part: (0, part * PAIRS + pair(p, c)))
        for part in range(3)
    ]
    full = fixed((toks, width))
    row = fixed((1, width))
    f32_full = jax.ShapeDtypeStruct((toks, width), F32)
    gw_spec = fixed((4, width, PAIR))
    gw_shape = jax.ShapeDtypeStruct((4, width, PAIR), BF16)
    scratch = [
        pltpu.VMEM((toks // QB, 3 * QB, QB), F32),
        pltpu.VMEM((PAIR, toks), F32),
        pltpu.VMEM((toks, PAIR), F32),
        pltpu.VMEM((toks, PAIR), F32),
        pltpu.VMEM((toks, PAIR), BF16),
    ]
    if final:
        out_specs = [gw_spec, gw_spec, full, row]
        out_shape = [gw_shape, gw_shape, f32_full, jax.ShapeDtypeStruct((1, width), F32)]
        scratch = [pltpu.VMEM((toks, width), F32)] + scratch
    else:
        out_specs, out_shape = [gw_spec, gw_spec, full], [gw_shape, gw_shape, f32_full]
    return pl.pallas_call(
        functools.partial(attend_back_kernel, bool(final)),
        grid_spec=pltpu.PrefetchScalarGridSpec(
            num_scalar_prefetch=1,
            grid=(2,),
            in_specs=[
                fixed((1, toks)),
                pair_cols,
                pair_cols,
                pair_cols,
                pl.BlockSpec((1, 2, toks), lambda p, c: (pair(p, c), 0, 0)),
                pl.BlockSpec((PAIR, toks), lambda p, c: (pair(p, c), 0)),
                full,
                fixed((width, toks)),
                pl.BlockSpec((PAIR, width), lambda p, c: (pair(p, c), 0)),
                *weights,
                full,
            ]
            + ([full, full, row] if final else []),
            out_specs=out_specs,
            scratch_shapes=scratch,
        ),
        out_shape=out_shape,
        compiler_params=params(56),
        cost_estimate=cost(19),
        name="attend_back",
    )(core, segr, q, k, v, lse, mixt, gb, attnt, w_o, w_qkv, w_qkv, w_qkv, gin, *final)


def unit_scale(values, axis):
    total = jnp.sum(values * values, axis=axis, keepdims=True)
    return lax.rsqrt(jnp.maximum(total, NORM_FLOOR)), total


def unit_back(values, inv, total, grad, axis):
    passed = jnp.where(total > NORM_FLOOR, 1.0, jnp.where(total == NORM_FLOOR, 0.5, 0.0))
    inner = jnp.sum(grad * values, axis=axis, keepdims=True)
    return inv * grad - passed * inv * inv * inv * inner * values


def gelu_and_slope(h):
    cdf = 0.5 + 0.5 * lax.erf(h * 0.7071067811865476)
    pdf = 0.3989422804014327 * jnp.exp(-0.5 * h * h)
    return h * cdf, cdf + h * pdf


def route(me, x, wrt, emb):
    z = mm(wrt, x, NT)
    inv, total = unit_scale(z, 0)
    zn = z * inv
    en = emb * unit_scale(emb, 1)[0]
    logits = mm(en, zn, NN, HIGHEST) / ROUTER_WARMTH
    w = jnp.exp(logits - jnp.max(logits, axis=0, keepdims=True))
    chances = w / jnp.sum(w, axis=0, keepdims=True)
    mine = jnp.where(lax.broadcasted_iota(I32, logits.shape, 0) == me, 1.0, 0.0)
    return z, inv, total, zn, en, chances, mine


def expert_kernel(grads, me_ref, wrt_ref, emb_ref, x_ref, win_ref, ga_ref, *rest):
    if grads:
        acta_ref, gpa_ref, xta_ref, gta_ref, gtb_ref, gw_ref, act_ref, *rest = rest
    else:
        act_ref, gp_ref, xt_ref, *rest = rest
    gout_ref, gwrt_ref, gemb_ref, gin_s, acc_s, gate_s, *rest = rest
    if grads:
        gp_ref, xt_ref = rest
    c = pl.program_id(0)
    rows, width = x_ref.shape
    me = me_ref[0]

    @pl.when(c == 0)
    def _():
        chances, mine = route(me, x_ref[...], wrt_ref[...], emb_ref[...])[-2:]
        gate = column_of(jnp.sum(chances * mine, axis=0, keepdims=True))
        gate_s[...] = jnp.broadcast_to(gate, (rows, LANES))
        for r in range(0, rows, QB):
            xt_ref[:, r : r + QB] = x_ref[r : r + QB, :].T
        gin_s[...] = jnp.zeros_like(gin_s)
        acc_s[...] = jnp.zeros_like(acc_s)

    w_in = win_ref[0]
    wide = w_in.shape[1]
    step = min(2 * QB, rows)
    for r in range(0, rows, step):
        part = slice(r, r + step)
        h = mm(x_ref[part, :], w_in)
        act, slope = gelu_and_slope(h)
        gate = jnp.concatenate([gate_s[part, :]] * (wide // LANES), axis=1)
        ga = ga_ref[part, :].astype(F32)
        act = act * gate
        act_ref[part, :] = act.astype(BF16)
        gp = (ga * (slope * gate)).astype(BF16)
        gp_ref[part, :] = gp
        prod = act * ga
        folded = prod[:, :LANES]
        for j in range(LANES, wide, LANES):
            folded = folded + prod[:, j : j + LANES]
        acc_s[part, :] += folded
        gin_s[part, :] += mm(gp, w_in, NT)
    if grads:
        gw_ref[0, 0] = (mm(xta_ref[...], gpa_ref[...]) + mm(xt_ref[...], gp_ref[...])).astype(BF16)
        gw_ref[0, 1] = (mm(gta_ref[...], acta_ref[...]) + mm(gtb_ref[...], act_ref[...])).astype(
            BF16
        )

    @pl.when(c == pl.num_programs(0) - 1)
    def _():
        x, wrt, emb = x_ref[...], wrt_ref[...], emb_ref[...]
        z, inv, total, zn, en, chances, mine = route(me, x, wrt, emb)
        weight = jnp.sum(acc_s[...].T, axis=0, keepdims=True)
        dl = weight * (mine - chances) / ROUTER_WARMTH
        gen = mm(dl, zn, NT, HIGHEST)
        dz = unit_back(z, inv, total, mm(en, dl, TN, HIGHEST), 0)
        dz_top = dz.astype(BF16)
        dz_low = (dz - dz_top.astype(F32)).astype(BF16)
        gwrt_ref[...] = mm(dz_top, x) + mm(dz_low, x)
        einv, etotal = unit_scale(emb, 1)
        gemb_ref[...] = unit_back(emb, einv, etotal, gen, 1)
        dz_top, dz_low = dz_top.astype(F32).T.astype(BF16), dz_low.astype(F32).T.astype(BF16)
        for r in range(0, rows, QB):
            part = slice(r, r + QB)
            back = gin_s[part, :].astype(BF16).astype(F32)
            back = back + mm(dz_top[part], wrt) + mm(dz_low[part], wrt)
            gout_ref[part, :] = back.astype(BF16)


def expert(me, wrt, emb, x, w_in, ga, wide, other=None):
    rows, width = x.shape
    hidden = w_in.shape[2]
    steps = hidden // wide
    grads = other is not None
    cols = pl.BlockSpec((rows, wide), lambda c: (0, c))
    hid = jax.ShapeDtypeStruct((rows, hidden), BF16)
    xt_spec = whole((width, rows))
    operands = [me, wrt, emb, x, w_in, ga]
    in_specs = [
        smem(),
        whole(wrt.shape),
        whole(emb.shape),
        whole((rows, width)),
        pl.BlockSpec((1, width, wide), lambda c: (0, 0, c)),
        cols,
    ]
    scratch = [
        pltpu.VMEM((rows, width), F32),
        pltpu.VMEM((rows, LANES), F32),
        pltpu.VMEM((rows, LANES), F32),
    ]
    if grads:
        operands += list(other)
        in_specs += [cols, cols, xt_spec, xt_spec, xt_spec]
        out_specs = [pl.BlockSpec((1, 2, width, wide), lambda c: (c, 0, 0, 0)), cols]
        out_shape = [jax.ShapeDtypeStruct((steps, 2, width, wide), BF16), hid]
        scratch += [pltpu.VMEM((rows, wide), BF16), pltpu.VMEM((width, rows), BF16)]
    else:
        out_specs = [cols, cols, xt_spec]
        out_shape = [hid, hid, jax.ShapeDtypeStruct((width, rows), BF16)]
    out_specs += [whole((rows, width)), whole(wrt.shape), whole(emb.shape)]
    out_shape += [
        jax.ShapeDtypeStruct((rows, width), BF16),
        jax.ShapeDtypeStruct(wrt.shape, F32),
        jax.ShapeDtypeStruct(emb.shape, F32),
    ]
    return pl.pallas_call(
        functools.partial(expert_kernel, grads),
        grid=(steps,),
        in_specs=in_specs,
        out_specs=out_specs,
        out_shape=out_shape,
        scratch_shapes=scratch,
        compiler_params=params(60),
        cost_estimate=cost(45 if grads else 24),
        name="expert",
    )(*operands)


def grad_act_kernel(g_ref, wout_ref, out_ref, gt_ref):
    g = g_ref[...].reshape(out_ref.shape[0], g_ref.shape[-1])

    @pl.when(pl.program_id(0) == 0)
    def _():
        gt_ref[...] = g.T

    out_ref[...] = mm(g, wout_ref[0], NT).astype(BF16)


def grad_act(g, half, w_out, wide):
    peers, _, slots, width = g.shape
    rows = peers * slots
    hidden = w_out.shape[1]
    return pl.pallas_call(
        grad_act_kernel,
        grid=(hidden // wide,),
        in_specs=[
            pl.BlockSpec((peers, 1, slots, width), lambda c: (0, half, 0, 0)),
            pl.BlockSpec((1, wide, width), lambda c: (0, c, 0)),
        ],
        out_specs=[pl.BlockSpec((rows, wide), lambda c: (0, c)), whole((width, rows))],
        out_shape=[
            jax.ShapeDtypeStruct((rows, hidden), BF16),
            jax.ShapeDtypeStruct((width, rows), BF16),
        ],
        compiler_params=params(40),
        cost_estimate=cost(7),
        name="grad_act",
    )(g, w_out)


def expert_out_kernel(acta_ref, actb_ref, wout_ref, outa_ref, outb_ref, acc_ref):
    c = pl.program_id(0)
    rows = acta_ref.shape[0]

    @pl.when(c == 0)
    def _():
        acc_ref[...] = jnp.zeros_like(acc_ref)

    w_out = wout_ref[0]
    acc_ref[:rows, :] += mm(acta_ref[...], w_out)
    acc_ref[rows:, :] += mm(actb_ref[...], w_out)

    @pl.when(c == pl.num_programs(0) - 1)
    def _():
        outa_ref[...] = acc_ref[:rows, :].astype(BF16)
        outb_ref[...] = acc_ref[rows:, :].astype(BF16)


def expert_out_of(acta, actb, w_out, wide):
    rows, hidden = acta.shape
    width = w_out.shape[2]
    block = jax.ShapeDtypeStruct((rows, width), BF16)
    cols = pl.BlockSpec((rows, wide), lambda c: (0, c))
    return pl.pallas_call(
        expert_out_kernel,
        grid=(hidden // wide,),
        in_specs=[cols, cols, pl.BlockSpec((1, wide, width), lambda c: (0, c, 0))],
        out_specs=[whole((rows, width))] * 2,
        out_shape=[block] * 2,
        scratch_shapes=[pltpu.VMEM((2 * rows, width), F32)],
        compiler_params=params(50),
        cost_estimate=cost(14),
        name="expert_out",
    )(acta, actb, w_out)


def expert_sums_kernel(sum_ref, win_ref, wout_ref):
    win_ref[0] = sum_ref[0].astype(F32)
    wout_ref[0] = sum_ref[1].astype(F32).T


def expert_sums(total):
    _, width, share = total.shape
    wide = LANES
    return pl.pallas_call(
        expert_sums_kernel,
        grid=(share // wide,),
        in_specs=[pl.BlockSpec((2, width, wide), lambda k: (0, 0, k))],
        out_specs=[
            pl.BlockSpec((1, width, wide), lambda k: (0, 0, k)),
            pl.BlockSpec((1, wide, width), lambda k: (0, k, 0)),
        ],
        out_shape=[
            jax.ShapeDtypeStruct((1, width, share), F32),
            jax.ShapeDtypeStruct((1, share, width), F32),
        ],
        compiler_params=params(32),
        cost_estimate=cost(3),
        name="expert_sums",
    )(total)


def gather_rows(key_row, row_refs):
    keys = column_of(key_row)
    total, at = None, 0
    for ref in row_refs:
        column = lax.broadcasted_iota(I32, (keys.shape[0], ref.shape[0]), 1) + at
        part = mm(ones_where(keys == column), ref[...])
        total = part if total is None else total + part
        at += ref.shape[0]
    return total


def combine_back_kernel(
    keyr_ref, res_ref, cot_ref, gf_ref, ra_ref, rb_ref, gres_ref, gb_ref, gain_ref
):
    dy = gather_rows(keyr_ref[...], (ra_ref, rb_ref))

    @pl.when(pl.program_id(0) == 0)
    def _():
        gain_ref[...] = jnp.zeros_like(gain_ref)

    dx, dgain = norm_back(res_ref[...], gf_ref[...], dy)
    gain_ref[...] += dgain
    grad = cot_ref[...].astype(F32) + dx
    gres_ref[...] = grad
    gb_ref[...] = grad.astype(BF16)


def combine_back(keyr, res, cot, gf, rows):
    toks, width = res.shape
    tile = pl.BlockSpec((QB, width), lambda i: (i, 0))
    return pl.pallas_call(
        combine_back_kernel,
        grid=(toks // QB,),
        in_specs=[
            pl.BlockSpec((1, QB), lambda i: (0, i)),
            tile,
            tile,
            whole((1, width)),
            *[whole(r.shape) for r in rows],
        ],
        out_specs=[tile, tile, whole((1, width))],
        out_shape=[
            jax.ShapeDtypeStruct((toks, width), F32),
            jax.ShapeDtypeStruct((toks, width), BF16),
            jax.ShapeDtypeStruct((1, width), F32),
        ],
        compiler_params=params(40),
        cost_estimate=cost(8),
        name="combine_back",
    )(keyr, res, cot, gf, *rows)


def combine_kernel(keyr_ref, res_ref, ra_ref, rb_ref, out_ref):
    out_ref[...] = (res_ref[...] + gather_rows(keyr_ref[...], (ra_ref, rb_ref))).astype(BF16)


def combine(keyr, res, rows):
    toks, width = res.shape
    tile = pl.BlockSpec((QB, width), lambda i: (i, 0))
    return pl.pallas_call(
        combine_kernel,
        grid=(toks // QB,),
        in_specs=[
            pl.BlockSpec((1, QB), lambda i: (0, i)),
            tile,
            *[whole(r.shape) for r in rows],
        ],
        out_specs=tile,
        out_shape=jax.ShapeDtypeStruct((toks, width), BF16),
        compiler_params=params(40),
        cost_estimate=cost(5),
        name="combine",
    )(keyr, res, *rows)


def shared_sums_kernel(
    me_ref, mine_ref, other_ref, mine_tail, other_tail, qkv_ref, o_ref, small_ref
):
    pair, part = pl.program_id(0), pl.program_id(1)
    chips, extra = mine_tail.shape[:2]
    quarter = chips // 4
    chip = me_ref[0] >> 1
    is_mine = (me_ref[0] & 1) == pair % 2

    def piece(ref, index):
        blocks = [ref[(index * quarter + t) ^ chip] for t in range(quarter)]
        return jnp.concatenate(blocks, axis=0).astype(F32)

    for ref, chosen in ((mine_ref, is_mine), (other_ref, jnp.logical_not(is_mine))):

        @pl.when(chosen)
        def _(ref=ref):
            qkv_ref[...] = piece(ref, part)

        @pl.when(chosen & (part == 0))
        def _(ref=ref):
            block = piece(ref, 3)
            for j in range(block.shape[0] // PAIR):
                o_ref[:, j * PAIR : (j + 1) * PAIR] = block[j * PAIR : (j + 1) * PAIR]

    @pl.when((pair == 0) & (part == 0))
    def _():
        for t in range(chips):
            both = mine_tail[t ^ chip].astype(F32) + other_tail[t ^ chip].astype(F32)
            small_ref[t * extra : (t + 1) * extra, :] = both


def shared_sums(me, mine, other, width):
    chips = mine.shape[0]
    rows = 4 * width // chips
    count = PAIRS // 2 * rows
    extra = mine.shape[1] - count
    block = pl.BlockSpec((chips, rows, PAIR), lambda pair, part: (0, pair // 2, 0))
    tail = pl.BlockSpec((chips, extra, PAIR), lambda pair, part: (0, count // extra, 0))
    return pl.pallas_call(
        shared_sums_kernel,
        grid=(PAIRS, 3),
        in_specs=[smem(), block, block, tail, tail],
        out_specs=[
            pl.BlockSpec((width, PAIR), lambda pair, part: (0, part * PAIRS + pair)),
            pl.BlockSpec((PAIR, width), lambda pair, part: (pair, 0)),
            whole((chips * extra, PAIR)),
        ],
        out_shape=[
            jax.ShapeDtypeStruct((width, 3 * width), F32),
            jax.ShapeDtypeStruct((width, width), F32),
            jax.ShapeDtypeStruct((chips * extra, PAIR), F32),
        ],
        compiler_params=params(32),
        cost_estimate=cost(8),
        name="shared_sums",
    )(me, mine, other, mine, other)


def exchange(rows):
    peers = lax.axis_size("expert")
    width = rows.shape[1]
    out = lax.all_to_all(
        rows.reshape(peers, -1, width), "expert", split_axis=0, concat_axis=0, tiled=True
    )
    return out.reshape(-1, width)


def core_groups():
    return [[core + 2 * chip for chip in range(lax.axis_size("expert") // 2)] for core in range(2)]


def swap_cores(value):
    peers = lax.axis_size("expert")
    return lax.ppermute(value, "expert", [(j, j ^ 1) for j in range(peers)])


def sum_blocks(blocks):
    return jnp.sum(blocks.astype(F32), axis=0).astype(BF16)


def sum_over_chips(blocks):
    return sum_blocks(
        lax.all_to_all(blocks, "expert", 0, 0, axis_index_groups=core_groups(), tiled=True)
    )


def finish_sums(shares):
    peers = lax.axis_size("expert")
    groups = lax.axis_size("dp")
    joined = jnp.concatenate(shares, axis=0)
    blocks = joined.reshape(groups, joined.shape[0] // groups, -1)
    total = sum_blocks(lax.all_to_all(blocks, "dp", 0, 0, tiled=True))
    total = lax.all_gather(total, "dp", axis=0, tiled=True)
    pieces = [total] + [
        lax.ppermute(total, "expert", [(j, j ^ (2 * d)) for j in range(peers)])
        for d in range(1, peers // 2)
    ]
    mine = jnp.stack(pieces)
    return mine, swap_cores(mine)


def on_device(
    tokens,
    segments,
    routes,
    cotangent,
    w_qkv,
    w_attn_out,
    gain_attn,
    gain_ffn,
    w_router,
    embed,
    w_in,
    w_out,
):
    toks, width = tokens.shape
    experts, rdim = embed.shape
    peers = lax.axis_size("expert")
    shards = lax.axis_size("dp")
    chips = peers // 2
    wide = w_in.shape[2] // shards
    me = lax.axis_index("expert").astype(I32).reshape(1)
    core = me & 1
    ga, gf = gain_attn.reshape(1, width), gain_ffn.reshape(1, width)
    segr = segments.reshape(1, toks)
    wrt = w_router.T
    hold = lax.optimization_barrier

    keyr, g_slots = place(routes.reshape(1, toks), cotangent, peers, 2 * toks)
    g_rows = exchange(g_slots).reshape(peers, 2, toks // peers, width)
    q, k, v, lse, mixt, attn_in, res, xa_slots, xb_slots = attend(
        tokens, segr, keyr, w_qkv, w_attn_out, ga, gf
    )
    x_a = exchange(xa_slots)
    gact_a, gt_a = grad_act(g_rows, 0, w_out, wide)
    gact_b, gt_b = grad_act(g_rows, 1, w_out, wide)
    x_a, xb_slots, gact_b, gt_b = hold((x_a, xb_slots, gact_b, gt_b))
    x_b = exchange(xb_slots)
    act_a, gp_a, xt_a, gout_a, gwr_a, gemb_a = expert(me, wrt, embed, x_a, w_in, gact_a, wide)
    gback_a = exchange(gout_a)
    gw, act_b, gout_b, gwr_b, gemb_b = expert(
        me, wrt, embed, x_b, w_in, gact_b, wide, (act_a, gp_a, xt_a, gt_a, gt_b)
    )
    expert_total = lax.psum_scatter(gw, "dp", scatter_dimension=0, tiled=True)[0]
    gout_b, gback_a = hold((gout_b, gback_a))
    gback_b = exchange(gout_b)
    attnt = attn_in.T
    fout_a, fout_b = expert_out_of(act_a, act_b, w_out, wide)
    gback_b, fout_a, fout_b, attnt = hold((gback_b, fout_a, fout_b, attnt))
    gres, gb, ggf = combine_back(keyr, res, cotangent, gf, (gback_a, gback_b))

    gatt = jnp.zeros((toks, width), F32)
    fback, both, shares = [], [], []
    for turn in range(PAIRS // 2):
        final = (tokens, gres, ga) if turn + 1 == PAIRS // 2 else ()
        send, keep, gatt, *gga = attend_back(
            2 * turn, core, segr, q, k, v, lse, mixt, gb, attnt, w_attn_out, w_qkv, gatt, final
        )
        got = swap_cores(send)
        both.append((keep.astype(F32) + got.astype(F32)).astype(BF16).reshape(chips, -1, PAIR))
        if turn == 0:
            fback.append(exchange(fout_a))
            gatt, fout_b, *fback = hold((gatt, fout_b, *fback))
        elif not final:
            fback.append(exchange(fout_b))
            gatt, both, fback = hold((gatt, both, fback))
            shares.append(sum_over_chips(jnp.concatenate(both, axis=1)))
            both = []
    grad_tokens = gatt
    gemb = (gemb_a + gemb_b).reshape(-1)
    small = jnp.concatenate(
        [
            gga[0].reshape(-1, LANES),
            ggf.reshape(-1, LANES),
            (gwr_a + gwr_b).reshape(-1, LANES),
            jnp.pad(gemb, (0, -experts * rdim % LANES)).reshape(-1, LANES),
        ],
        axis=0,
    )
    small = jnp.pad(small, ((0, -small.shape[0] % (16 * chips)), (0, 0))).astype(BF16)
    small = small.reshape(chips, -1, LANES)
    shares.append(sum_over_chips(jnp.concatenate([*both, small], axis=1)))
    mine, others = finish_sums(shares)
    grad_w_qkv, grad_w_attn_out, small = shared_sums(me, mine, others, width)
    small = small.reshape(-1)
    grad_gain_attn = small[:width]
    grad_gain_ffn = small[width : 2 * width]
    grad_router = small[2 * width : (2 + rdim) * width].reshape(rdim, width).T
    at = (2 + rdim) * width
    grad_embed = small[at : at + experts * rdim].reshape(experts, rdim)
    out_tokens = combine(keyr, res, fback)
    grad_w_in, grad_w_out = expert_sums(expert_total)
    return (
        out_tokens,
        grad_tokens,
        grad_w_qkv,
        grad_w_attn_out,
        grad_gain_attn,
        grad_gain_ffn,
        grad_router,
        grad_embed,
        grad_w_in,
        grad_w_out,
    )


def solution(mesh):
    rows = P(("dp", "expert"), None)
    return jax.shard_map(
        on_device,
        mesh=mesh,
        in_specs=(
            rows,
            rows,
            rows,
            rows,
            P(),
            P(),
            P(),
            P(),
            P(),
            P(),
            P("expert", None, None),
            P("expert", None, None),
        ),
        out_specs=(
            rows,
            rows,
            P(),
            P(),
            P(),
            P(),
            P(),
            P(),
            P("expert", None, "dp"),
            P("expert", "dp", None),
        ),
        check_vma=False,
    )
```

```python
import functools
import math

import jax
import jax.numpy as jnp
from jax import lax
from jax.experimental import pallas as pl
from jax.experimental.pallas import tpu as pltpu
from jax.sharding import PartitionSpec as P

HEADS = 12
HEAD = 64
PAIRS = HEADS // 2
PAIR = 2 * HEAD
QB = 256
LANES = 128
ROUTER_WARMTH = 0.3
NORM_FLOOR = 12.0
EPSILON = 1e-05
MASK_VALUE = -1e30
F32 = jnp.float32
BF16 = jnp.bfloat16
I32 = jnp.int32
NN = (((1,), (0,)), ((), ()))
NT = (((1,), (1,)), ((), ()))
TN = (((0,), (0,)), ((), ()))
HIGHEST = lax.Precision.HIGHEST
MIB = 1 << 20


def mm(a, b, dims=NN, precision=None):
    return lax.dot_general(a, b, dims, precision=precision, preferred_element_type=F32)


def params():
    return pltpu.CompilerParams(vmem_limit_bytes=62 * MIB)


def cost(micros, nbytes=0):
    return pl.CostEstimate(
        flops=int(micros * 1.15e9), bytes_accessed=int(nbytes), transcendentals=0
    )


def whole(shape):
    return pl.BlockSpec(
        shape, lambda *_: (0,) * len(shape), pipeline_mode=pl.Buffered(buffer_count=1)
    )


def smem():
    return pl.BlockSpec(memory_space=pltpu.SMEM)


def norm_back(x, gain, dy):
    inv = lax.rsqrt(jnp.mean(x * x, axis=1, keepdims=True) + EPSILON)
    dn = dy * gain
    dx = inv * dn - x * (inv * inv * inv * jnp.mean(x * dn, axis=1, keepdims=True))
    return dx, jnp.sum(dy * x * inv, axis=0, keepdims=True)


def column_of(row):
    return jnp.broadcast_to(row.astype(F32), (8, row.shape[1])).T[:, :1].astype(row.dtype)


def ones_where(mask):
    return jnp.where(mask, 1.0, 0.0).astype(BF16)


def dispatch(key_row, rows, out_refs):
    at = 0
    for ref in out_refs:
        step = min(2 * QB, ref.shape[0])
        for r in range(0, ref.shape[0], step):
            slot = lax.broadcasted_iota(I32, (step, key_row.shape[1]), 0) + at
            ref[r : r + step, :] = mm(ones_where(key_row == slot), rows).astype(BF16)
            at += step


def place_kernel(peers, rr_ref, cot_ref, keyr_ref, keyn_ref, g_ref):
    toks = cot_ref.shape[0]
    cap = g_ref.shape[0] // peers
    half = cap // 2
    rr = rr_ref[...]
    before = ones_where(
        lax.broadcasted_iota(I32, (toks, toks), 0) <= lax.broadcasted_iota(I32, (toks, toks), 1)
    )
    hot_row = jnp.where(lax.broadcasted_iota(I32, (peers, toks), 0) == rr, 1.0, 0.0)
    upto = mm(hot_row.astype(BF16), before)
    rank = (jnp.sum(hot_row * upto, axis=0, keepdims=True) - 1.0).astype(I32)
    keyr_ref[...] = rr * half + jnp.where(rank < half, rank, rank + (peers - 1) * half)
    keyn_ref[...] = rr * cap + rank
    dispatch(keyn_ref[...], cot_ref[...], (g_ref,))


def place(routes, cot, peers, slots):
    toks, width = cot.shape
    return pl.pallas_call(
        functools.partial(place_kernel, peers),
        out_shape=[
            jax.ShapeDtypeStruct((1, toks), I32),
            jax.ShapeDtypeStruct((1, toks), I32),
            jax.ShapeDtypeStruct((slots, width), BF16),
        ],
        in_specs=[pl.BlockSpec(memory_space=pltpu.VMEM)] * 2,
        compiler_params=params(),
        cost_estimate=cost(5),
        name="place",
    )(routes, cot)


def band(i):
    return max(0, i - 2) * QB, (i + 1) * QB


def fill_bias(bias_ref, segr, count):
    segc = column_of(segr)
    for i in range(count):
        low, high = band(i)
        keys = lax.broadcasted_iota(I32, (high - low, QB), 0) + low
        queries = lax.broadcasted_iota(I32, (high - low, QB), 1) + i * QB
        same = segc[low:high] == segr[:, i * QB : (i + 1) * QB]
        bias_ref[i, : high - low, :] = jnp.where((keys <= queries) & same, 0.0, MASK_VALUE)


def head_mask(values, h):
    lane = lax.broadcasted_iota(I32, values.shape, 1)
    return jnp.where((lane >= h * HEAD) & (lane < (h + 1) * HEAD), values, jnp.zeros_like(values))


def attend_kernel(
    tok_ref,
    segr_ref,
    keyr_ref,
    wq_ref,
    wk_ref,
    wv_ref,
    wo_ref,
    ga_ref,
    gf_ref,
    q_ref,
    k_ref,
    v_ref,
    lse_ref,
    mixt_ref,
    attn_ref,
    res_ref,
    xa_ref,
    xb_ref,
    bias_ref,
    mix_ref,
):
    p = pl.program_id(0)
    toks, width = tok_ref.shape
    count = toks // QB

    @pl.when(p == 0)
    def _():
        fill_bias(bias_ref, segr_ref[...], count)
        x = tok_ref[...].astype(F32)
        inv = lax.rsqrt(jnp.mean(x * x, axis=1, keepdims=True) + EPSILON)
        attn_ref[...] = (x * inv * ga_ref[...]).astype(BF16)

    attn_in = attn_ref[...]
    weights = jnp.concatenate([wq_ref[...], wk_ref[...], wv_ref[...]], axis=1)
    qkv = mm(attn_in, weights)
    q_ref[...] = qkv[:, :PAIR].astype(BF16)
    k_ref[...] = qkv[:, PAIR : 2 * PAIR].astype(BF16)
    v = qkv[:, 2 * PAIR :]
    v_ref[...] = v.astype(BF16)
    vt = v.T.astype(BF16)
    for i in range(count):
        low, high = band(i)
        cols = slice(i * QB, (i + 1) * QB)
        q = q_ref[cols, :] * HEAD**-0.5
        keys = k_ref[low:high, :]
        parts = []
        for h in range(2):
            s = mm(keys, head_mask(q, h), NT) + bias_ref[i, : high - low, :]
            top = jnp.max(s, axis=0, keepdims=True)
            w = jnp.exp(s - top)
            total = jnp.sum(w, axis=0, keepdims=True)
            lse_ref[0, h : h + 1, cols] = top + jnp.log(total)
            chances = (w * (1.0 / total)).astype(BF16)
            parts.append(mm(vt[h * HEAD : (h + 1) * HEAD, low:high], chances))
        mixt_ref[:, cols] = jnp.concatenate(parts, axis=0).astype(BF16)
    mix_ref[pl.ds(pl.multiple_of(p * PAIR, PAIR), PAIR), :] = mixt_ref[...]

    @pl.when(p == pl.num_programs(0) - 1)
    def _():
        res = tok_ref[...].astype(F32) + mm(mix_ref[...], wo_ref[...], TN)
        res_ref[...] = res
        inv = lax.rsqrt(jnp.mean(res * res, axis=1, keepdims=True) + EPSILON)
        ffn_in = (res * inv * gf_ref[...]).astype(BF16)
        dispatch(keyr_ref[...], ffn_in, (xa_ref, xb_ref))


def attend(tokens, segr, keyr, w_qkv, w_o, ga, gf):
    toks, width = tokens.shape
    pair_cols = pl.BlockSpec((toks, PAIR), lambda p: (0, p))
    heads = jax.ShapeDtypeStruct((toks, width), BF16)
    weights = [
        pl.BlockSpec((width, PAIR), lambda p, part=part: (0, part * PAIRS + p)) for part in range(3)
    ]
    return pl.pallas_call(
        attend_kernel,
        grid=(PAIRS,),
        in_specs=[
            whole((toks, width)),
            whole((1, toks)),
            whole((1, toks)),
            *weights,
            whole((width, width)),
            whole((1, width)),
            whole((1, width)),
        ],
        out_specs=[
            pair_cols,
            pair_cols,
            pair_cols,
            pl.BlockSpec((1, 2, toks), lambda p: (p, 0, 0)),
            pl.BlockSpec((PAIR, toks), lambda p: (p, 0)),
            whole((toks, width)),
            whole((toks, width)),
            whole((toks, width)),
            whole((toks, width)),
        ],
        out_shape=[
            heads,
            heads,
            heads,
            jax.ShapeDtypeStruct((PAIRS, 2, toks), F32),
            jax.ShapeDtypeStruct((width, toks), BF16),
            heads,
            jax.ShapeDtypeStruct((toks, width), F32),
            heads,
            heads,
        ],
        scratch_shapes=[
            pltpu.VMEM((toks // QB, 3 * QB, QB), F32),
            pltpu.VMEM((width, toks), BF16),
        ],
        compiler_params=params(),
        cost_estimate=cost(42),
        name="attend",
    )(tokens, segr, keyr, w_qkv, w_qkv, w_qkv, w_o, ga, gf)


def attend_back_kernel(
    core_ref,
    segr_ref,
    q_ref,
    k_ref,
    v_ref,
    lse_ref,
    mixt_ref,
    gb_ref,
    attnt_ref,
    wo_ref,
    send_ref,
    keep_ref,
    gqkv_ref,
    bias_ref,
    dqt_ref,
    dk_ref,
    dv_ref,
    do_ref,
):
    p = pl.program_id(0)
    toks, width = gb_ref.shape
    count = toks // QB
    scale = HEAD**-0.5

    @pl.when(p == 0)
    def _():
        fill_bias(bias_ref, segr_ref[...], count)

    gb = gb_ref[...]
    do_ref[...] = mm(gb, wo_ref[...], NT).astype(BF16)
    dot_ = mm(wo_ref[...], gb, NT).astype(BF16).astype(F32)
    mixt = mixt_ref[...]
    gwo = mm(mixt, gb).astype(BF16)
    weighted = dot_ * mixt.astype(F32)
    delta = [
        jnp.sum(weighted[h * HEAD : (h + 1) * HEAD], axis=0, keepdims=True) for h in range(2)
    ]
    kt = k_ref[...].astype(F32).T.astype(BF16)
    dk_ref[...] = jnp.zeros_like(dk_ref)
    dv_ref[...] = jnp.zeros_like(dv_ref)
    for i in range(count):
        low, high = band(i)
        cols = slice(i * QB, (i + 1) * QB)
        q = q_ref[cols, :] * scale
        do = do_ref[cols, :]
        keys = k_ref[low:high, :]
        values = v_ref[low:high, :]
        dk_add, dv_add, dqs = [], [], []
        for h in range(2):
            qm, dom = head_mask(q, h), head_mask(do, h)
            s = mm(keys, qm, NT) + bias_ref[i, : high - low, :]
            pr = jnp.exp(s - lse_ref[0, h : h + 1, cols])
            dpr = mm(values, dom, NT)
            ds = (pr * (dpr - delta[h][:, cols])).astype(BF16)
            dv_add.append(mm(pr.astype(BF16), dom))
            dk_add.append(mm(ds, qm))
            dqs.append(mm(kt[h * HEAD : (h + 1) * HEAD, low:high], ds))
        dk_ref[low:high, :] += dk_add[0] + dk_add[1]
        dv_ref[low:high, :] += dv_add[0] + dv_add[1]
        dqt_ref[:, cols] = jnp.concatenate(dqs, axis=0) * scale
    grads = [
        dqt_ref[...].T.astype(BF16),
        dk_ref[...].astype(BF16),
        dv_ref[...].astype(BF16),
    ]
    for part in range(3):
        gqkv_ref[part] = grads[part]
    gw = mm(attnt_ref[...], jnp.concatenate(grads, axis=1)).astype(BF16)
    for turn, ref in enumerate((send_ref, keep_ref)):

        @pl.when(p == turn)
        def _(ref=ref):
            for part in range(3):
                ref[part] = gw[:, part * PAIR : (part + 1) * PAIR]
            for j in range(width // PAIR):
                ref[3, j * PAIR : (j + 1) * PAIR, :] = gwo[:, j * PAIR : (j + 1) * PAIR]


def attend_back(first, core, segr, q, k, v, lse, mixt, gb, attnt, w_o):
    toks, width = gb.shape

    def pair(p, core_ref):
        return jnp.where(p == 0, 1 - core_ref[0], core_ref[0])

    def fixed(shape):
        return pl.BlockSpec(
            shape, lambda p, c: (0,) * len(shape), pipeline_mode=pl.Buffered(buffer_count=1)
        )

    pair_cols = pl.BlockSpec((toks, PAIR), lambda p, c: (0, first + pair(p, c)))
    gw_spec = fixed((4, width, PAIR))
    gw_shape = jax.ShapeDtypeStruct((4, width, PAIR), BF16)
    return pl.pallas_call(
        attend_back_kernel,
        grid_spec=pltpu.PrefetchScalarGridSpec(
            num_scalar_prefetch=1,
            grid=(2,),
            in_specs=[
                fixed((1, toks)),
                pair_cols,
                pair_cols,
                pair_cols,
                pl.BlockSpec((1, 2, toks), lambda p, c: (first + pair(p, c), 0, 0)),
                pl.BlockSpec((PAIR, toks), lambda p, c: (first + pair(p, c), 0)),
                fixed((toks, width)),
                fixed((width, toks)),
                pl.BlockSpec((PAIR, width), lambda p, c: (first + pair(p, c), 0)),
            ],
            out_specs=[
                gw_spec,
                gw_spec,
                pl.BlockSpec((3, toks, PAIR), lambda p, c: (0, 0, pair(p, c))),
            ],
            scratch_shapes=[
                pltpu.VMEM((toks // QB, 3 * QB, QB), F32),
                pltpu.VMEM((PAIR, toks), F32),
                pltpu.VMEM((toks, PAIR), F32),
                pltpu.VMEM((toks, PAIR), F32),
                pltpu.VMEM((toks, PAIR), BF16),
            ],
        ),
        out_shape=[gw_shape, gw_shape, jax.ShapeDtypeStruct((3, toks, 2 * PAIR), BF16)],
        compiler_params=params(),
        cost_estimate=cost(10 if first + 2 == PAIRS else 2),
        name="attend_back",
    )(core, segr, q, k, v, lse, mixt, gb, attnt, w_o)


def grad_tokens_kernel(tok_ref, gres_ref, ga_ref, w_ref, *rest):
    *g_refs, out_ref = rest
    grads = [ref[part] for part in range(3) for ref in g_refs]
    dy = mm(jnp.concatenate(grads, axis=1), w_ref[...], NT)
    dx, _ = norm_back(tok_ref[...].astype(F32), ga_ref[...], dy)
    out_ref[...] = gres_ref[...] + dx


def grad_tokens_of(tokens, gres, ga, w_qkv, grads):
    toks, width = tokens.shape
    rows = 2 * QB
    tile = pl.BlockSpec((rows, width), lambda i: (i, 0))
    return pl.pallas_call(
        grad_tokens_kernel,
        grid=(toks // rows,),
        in_specs=[tile, tile, whole((1, width)), whole(w_qkv.shape)]
        + [pl.BlockSpec((3, rows, 2 * PAIR), lambda i: (0, i, 0))] * len(grads),
        out_specs=tile,
        out_shape=jax.ShapeDtypeStruct((toks, width), F32),
        compiler_params=params(),
        cost_estimate=cost(9),
        name="grad_tokens",
    )(tokens, gres, ga, w_qkv, *grads)


def unit_scale(values, axis):
    total = jnp.sum(values * values, axis=axis, keepdims=True)
    return lax.rsqrt(jnp.maximum(total, NORM_FLOOR)), total


def unit_back(values, inv, total, grad, axis):
    passed = jnp.where(total > NORM_FLOOR, 1.0, jnp.where(total == NORM_FLOOR, 0.5, 0.0))
    inner = jnp.sum(grad * values, axis=axis, keepdims=True)
    return inv * grad - passed * inv * inv * inv * inner * values


def gelu_and_slope(h):
    cdf = 0.5 + 0.5 * lax.erf(h * 0.7071067811865476)
    pdf = 0.3989422804014327 * jnp.exp(-0.5 * h * h)
    return h * cdf, cdf + h * pdf


def route(me, x, wrt, emb):
    z = mm(wrt, x, NT)
    inv, total = unit_scale(z, 0)
    zn = z * inv
    en = emb * unit_scale(emb, 1)[0]
    logits = mm(en, zn, NN, HIGHEST) / ROUTER_WARMTH
    w = jnp.exp(logits - jnp.max(logits, axis=0, keepdims=True))
    chances = w / jnp.sum(w, axis=0, keepdims=True)
    mine = jnp.where(lax.broadcasted_iota(I32, logits.shape, 0) == me, 1.0, 0.0)
    return z, inv, total, zn, en, chances, mine


def expert_kernel(
    me_ref,
    wrt_ref,
    emb_ref,
    x_ref,
    win_ref,
    ga_ref,
    act_ref,
    gp_ref,
    xt_ref,
    gout_ref,
    gwrt_ref,
    gemb_ref,
    w_s,
    gp_s,
    acc_s,
    gate_s,
):
    c = pl.program_id(0)
    rows, width = x_ref.shape
    me = me_ref[0]

    @pl.when(c == 0)
    def _():
        chances, mine = route(me, x_ref[...], wrt_ref[...], emb_ref[...])[-2:]
        gate = column_of(jnp.sum(chances * mine, axis=0, keepdims=True))
        gate_s[...] = jnp.broadcast_to(gate, (rows, LANES))
        acc_s[...] = jnp.zeros_like(acc_s)
        for r in range(0, rows, QB):
            xt_ref[:, r : r + QB] = x_ref[r : r + QB, :].T

    w_in = win_ref[0]
    wide = w_in.shape[1]
    chunk = pl.ds(pl.multiple_of(c * wide, LANES), wide)
    w_s[:, chunk] = w_in
    step = min(2 * QB, rows)
    for r in range(0, rows, step):
        part = slice(r, r + step)
        h = mm(x_ref[part, :], w_in)
        act, slope = gelu_and_slope(h)
        gate = jnp.concatenate([gate_s[part, :]] * (wide // LANES), axis=1)
        ga = ga_ref[part, :].astype(F32)
        act = act * gate
        act_ref[part, :] = act.astype(BF16)
        gp = (ga * (slope * gate)).astype(BF16)
        gp_s[part, chunk] = gp
        gp_ref[part, :] = gp
        prod = act * ga
        folded = prod[:, :LANES]
        for j in range(LANES, wide, LANES):
            folded = folded + prod[:, j : j + LANES]
        acc_s[part, :] += folded

    @pl.when(c == pl.num_programs(0) - 1)
    def _():
        x, wrt, emb = x_ref[...], wrt_ref[...], emb_ref[...]
        z, inv, total, zn, en, chances, mine = route(me, x, wrt, emb)
        weight = jnp.sum(acc_s[...].T, axis=0, keepdims=True)
        dl = weight * (mine - chances) / ROUTER_WARMTH
        gen = mm(dl, zn, NT, HIGHEST)
        dz = unit_back(z, inv, total, mm(en, dl, TN, HIGHEST), 0)
        dz_top = dz.astype(BF16)
        dz_low = (dz - dz_top.astype(F32)).astype(BF16)
        gwrt_ref[...] = mm(dz_top, x) + mm(dz_low, x)
        einv, etotal = unit_scale(emb, 1)
        gemb_ref[...] = unit_back(emb, einv, etotal, gen, 1)
        dz_top, dz_low = dz_top.astype(F32).T.astype(BF16), dz_low.astype(F32).T.astype(BF16)
        for r in range(0, rows, step):
            part = slice(r, r + step)
            back = mm(gp_s[part, :], w_s[...], NT).astype(BF16).astype(F32)
            back = back + mm(dz_top[part], wrt) + mm(dz_low[part], wrt)
            gout_ref[part, :] = back.astype(BF16)


def expert(me, wrt, emb, x, w_in, ga, wide):
    rows, width = x.shape
    hidden = w_in.shape[2]
    cols = pl.BlockSpec((rows, wide), lambda c: (0, c))
    hid = jax.ShapeDtypeStruct((rows, hidden), BF16)
    return pl.pallas_call(
        expert_kernel,
        grid=(hidden // wide,),
        in_specs=[
            smem(),
            whole(wrt.shape),
            whole(emb.shape),
            whole((rows, width)),
            pl.BlockSpec((1, width, wide), lambda c: (0, 0, c)),
            cols,
        ],
        out_specs=[
            cols,
            cols,
            whole((width, rows)),
            whole((rows, width)),
            whole(wrt.shape),
            whole(emb.shape),
        ],
        out_shape=[
            hid,
            hid,
            jax.ShapeDtypeStruct((width, rows), BF16),
            jax.ShapeDtypeStruct((rows, width), BF16),
            jax.ShapeDtypeStruct(wrt.shape, F32),
            jax.ShapeDtypeStruct(emb.shape, F32),
        ],
        scratch_shapes=[
            pltpu.VMEM((width, hidden), BF16),
            pltpu.VMEM((rows, hidden), BF16),
            pltpu.VMEM((rows, LANES), F32),
            pltpu.VMEM((rows, LANES), F32),
        ],
        compiler_params=params(),
        cost_estimate=cost(23),
        name="expert",
    )(me, wrt, emb, x, w_in, ga)


def expert_grads_kernel(lefta_ref, leftb_ref, righta_ref, rightb_ref, out_ref, left_s):
    rows = lefta_ref.shape[1]

    @pl.when(pl.program_id(0) == 0)
    def _():
        left_s[:, :rows] = lefta_ref[...]
        left_s[:, rows:] = leftb_ref[...]

    right = jnp.concatenate([righta_ref[...], rightb_ref[...]], axis=0)
    out_ref[0] = mm(left_s[...], right).astype(BF16)


def expert_grads(lefts, rights, wide):
    width, rows = lefts[0].shape
    steps = rights[0].shape[1] // wide
    return pl.pallas_call(
        expert_grads_kernel,
        grid=(steps,),
        in_specs=[whole((width, rows))] * 2 + [pl.BlockSpec((rows, wide), lambda c: (0, c))] * 2,
        out_specs=pl.BlockSpec((1, width, wide), lambda c: (c, 0, 0)),
        out_shape=jax.ShapeDtypeStruct((steps, width, wide), BF16),
        scratch_shapes=[pltpu.VMEM((width, 2 * rows), BF16)],
        compiler_params=params(),
        cost_estimate=cost(5),
        name="expert_grads",
    )(*lefts, *rights)


def grad_act_kernel(g_ref, wout_ref, out_ref, gt_ref):
    g = g_ref[...].reshape(out_ref.shape[0], g_ref.shape[-1])

    @pl.when(pl.program_id(0) == 0)
    def _():
        gt_ref[...] = g.T

    out_ref[...] = mm(g, wout_ref[0], NT).astype(BF16)


def grad_act(g, half, w_out, wide):
    peers, _, slots, width = g.shape
    rows = peers * slots
    hidden = w_out.shape[1]
    return pl.pallas_call(
        grad_act_kernel,
        grid=(hidden // wide,),
        in_specs=[
            pl.BlockSpec((peers, 1, slots, width), lambda c: (0, half, 0, 0)),
            pl.BlockSpec((1, wide, width), lambda c: (0, c, 0)),
        ],
        out_specs=[pl.BlockSpec((rows, wide), lambda c: (0, c)), whole((width, rows))],
        out_shape=[
            jax.ShapeDtypeStruct((rows, hidden), BF16),
            jax.ShapeDtypeStruct((width, rows), BF16),
        ],
        compiler_params=params(),
        cost_estimate=cost(7),
        name="grad_act",
    )(g, w_out)


def expert_out_kernel(acta_ref, actb_ref, wout_ref, out_ref, acc_ref):
    c = pl.program_id(0)
    rows = acta_ref.shape[0]
    peers, _, slots, width = out_ref.shape

    @pl.when(c == 0)
    def _():
        acc_ref[...] = jnp.zeros_like(acc_ref)

    w_out = wout_ref[0]
    acc_ref[:rows, :] += mm(acta_ref[...], w_out)
    acc_ref[rows:, :] += mm(actb_ref[...], w_out)

    @pl.when(c == pl.num_programs(0) - 1)
    def _():
        for h in range(2):
            part = acc_ref[h * rows : (h + 1) * rows, :].astype(BF16)
            out_ref[:, h] = part.reshape(peers, slots, width)


def expert_out_of(acta, actb, w_out, wide, peers):
    rows, hidden = acta.shape
    width = w_out.shape[2]
    shape = (peers, 2, rows // peers, width)
    cols = pl.BlockSpec((rows, wide), lambda c: (0, c))
    return pl.pallas_call(
        expert_out_kernel,
        grid=(hidden // wide,),
        in_specs=[cols, cols, pl.BlockSpec((1, wide, width), lambda c: (0, c, 0))],
        out_specs=whole(shape),
        out_shape=jax.ShapeDtypeStruct(shape, BF16),
        scratch_shapes=[pltpu.VMEM((2 * rows, width), F32)],
        compiler_params=params(),
        cost_estimate=cost(14),
        name="expert_out",
    )(acta, actb, w_out)


def expert_sums_kernel(in_ref, out_ref, win_ref, wout_ref):
    win_ref[0] = in_ref[...].astype(F32)
    wout_ref[0] = out_ref[...].astype(F32).T


def expert_sums(grad_in, grad_out):
    width, share = grad_in.shape
    block = pl.BlockSpec((width, LANES), lambda k: (0, k))
    return pl.pallas_call(
        expert_sums_kernel,
        grid=(share // LANES,),
        in_specs=[block, block],
        out_specs=[
            pl.BlockSpec((1, width, LANES), lambda k: (0, 0, k)),
            pl.BlockSpec((1, LANES, width), lambda k: (0, k, 0)),
        ],
        out_shape=[
            jax.ShapeDtypeStruct((1, width, share), F32),
            jax.ShapeDtypeStruct((1, share, width), F32),
        ],
        compiler_params=params(),
        cost_estimate=cost(3),
        name="expert_sums",
    )(grad_in, grad_out)


def gather_rows(key_row, row_refs):
    keys = column_of(key_row)
    total, at = None, 0
    for ref in row_refs:
        column = lax.broadcasted_iota(I32, (keys.shape[0], ref.shape[0]), 1) + at
        part = mm(ones_where(keys == column), ref[...])
        total = part if total is None else total + part
        at += ref.shape[0]
    return total


def combine_back_kernel(
    keyr_ref, res_ref, cot_ref, gf_ref, ra_ref, rb_ref, gres_ref, gb_ref, gain_ref
):
    dy = gather_rows(keyr_ref[...], (ra_ref, rb_ref))

    @pl.when(pl.program_id(0) == 0)
    def _():
        gain_ref[...] = jnp.zeros_like(gain_ref)

    dx, dgain = norm_back(res_ref[...], gf_ref[...], dy)
    gain_ref[...] += dgain
    grad = cot_ref[...].astype(F32) + dx
    gres_ref[...] = grad
    gb_ref[...] = grad.astype(BF16)


def combine_back(keyr, res, cot, gf, rows):
    toks, width = res.shape
    tile = pl.BlockSpec((QB, width), lambda i: (i, 0))
    return pl.pallas_call(
        combine_back_kernel,
        grid=(toks // QB,),
        in_specs=[
            pl.BlockSpec((1, QB), lambda i: (0, i)),
            tile,
            tile,
            whole((1, width)),
            *[whole(r.shape) for r in rows],
        ],
        out_specs=[tile, tile, whole((1, width))],
        out_shape=[
            jax.ShapeDtypeStruct((toks, width), F32),
            jax.ShapeDtypeStruct((toks, width), BF16),
            jax.ShapeDtypeStruct((1, width), F32),
        ],
        compiler_params=params(),
        cost_estimate=cost(100),
        name="combine_back",
    )(keyr, res, cot, gf, *rows)


def combine_kernel(keyn_ref, res_ref, rows_ref, out_ref):
    out_ref[...] = (res_ref[...] + gather_rows(keyn_ref[...], (rows_ref,))).astype(BF16)


def combine(keyn, res, rows):
    toks, width = res.shape
    tile = pl.BlockSpec((QB, width), lambda i: (i, 0))
    return pl.pallas_call(
        combine_kernel,
        grid=(toks // QB,),
        in_specs=[
            pl.BlockSpec((1, QB), lambda i: (0, i)),
            tile,
            whole(rows.shape),
        ],
        out_specs=tile,
        out_shape=jax.ShapeDtypeStruct((toks, width), BF16),
        compiler_params=params(),
        cost_estimate=cost(5),
        name="combine",
    )(keyn, res, rows)


def shared_sums_kernel(count, experts, rows, extra, me_ref, w_ref, ga_ref, *rest):
    blocks, rest = rest[: 2 * count], rest[2 * count :]
    qkv_ref, o_ref, gain_ref, gain_ffn_ref, router_ref, embed_ref = rest[:6]
    held, small_s, sems = rest[6:]
    i = pl.program_id(0)
    width = o_ref.shape[1]
    chip, core = me_ref[0] >> 1, me_ref[0] & 1
    grain = math.gcd(rows, PAIR)

    @pl.when(i == 0)
    def _():
        copies = []
        for n, ref in enumerate(blocks):
            side = core if n < count else 1 - core
            copies.append(
                pltpu.make_async_copy(ref, held.at[side, (n % count) ^ chip], sems.at[n])
            )
        for copy in copies:
            copy.start()
        for copy in copies:
            copy.wait()

    def piece(side, two, row):
        base = two * rows + (two // 2) * extra
        pieces = []
        for t in range(0, PAIR, grain):
            at = pl.multiple_of(base + (row + t) % rows, math.gcd(grain, extra))
            pieces.append(held[side, (row + t) // rows, pl.ds(at, grain), :])
        return jnp.concatenate(pieces, axis=0).astype(F32)

    for pair in range(PAIRS):
        for part in range(3):
            at = (part * PAIRS + pair) * PAIR
            qkv_ref[:, at : at + PAIR] = piece(pair % 2, pair // 2, part * width + i * PAIR)
    for two in range(PAIRS // 2):

        @pl.when(i // 2 == two)
        def _(two=two):
            for j in range(width // PAIR):
                o_ref[:, j * PAIR : (j + 1) * PAIR] = piece(i % 2, two, 3 * width + j * PAIR)

    folded = jnp.zeros((PAIR, LANES), F32)
    for at in range(0, qkv_ref.shape[1], LANES):
        folded += qkv_ref[:, at : at + LANES] * w_ref[:, at : at + LANES].astype(F32)
    gain = jnp.sum(folded.T, axis=0, keepdims=True) / ga_ref[...]
    gain_ref[pl.ds(pl.multiple_of(i * PAIR, PAIR), PAIR)] = gain[0]

    @pl.when(i == 0)
    def _():
        for t in range(count):
            part = slice(2 * rows, 2 * rows + extra)
            small_s[t * extra : (t + 1) * extra, :] = held[0, t, part, :].astype(F32)
        rdim = router_ref.shape[0]
        for j in range(width // LANES):
            lanes = slice(j * LANES, (j + 1) * LANES)
            gain_ffn_ref[lanes] = small_s[j, :]
            at = 8 + j * rdim
            router_ref[:, lanes] = small_s[at : at + rdim, :]
        at = 8 + width // LANES * rdim
        embed_ref[...] = small_s[at : at + experts, :rdim]


def shared_sums(me, blocks, rows, extra, w_qkv, ga, experts, rdim):
    width = w_qkv.shape[0]
    count = len(blocks) // 2
    lanes = pl.BlockSpec((1, PAIR), lambda i: (0, i))
    return pl.pallas_call(
        functools.partial(shared_sums_kernel, count, experts, rows, extra),
        grid=(width // PAIR,),
        in_specs=[smem(), pl.BlockSpec((PAIR, 3 * width), lambda i: (i, 0)), lanes]
        + [pl.BlockSpec(memory_space=pl.ANY)] * (2 * count),
        out_specs=[
            pl.BlockSpec((PAIR, 3 * width), lambda i: (i, 0)),
            pl.BlockSpec((PAIR, width), lambda i: (i, 0)),
            pl.BlockSpec((width,), lambda i: (0,)),
            pl.BlockSpec((width,), lambda i: (0,)),
            whole((rdim, width)),
            whole((experts, rdim)),
        ],
        out_shape=[
            jax.ShapeDtypeStruct((width, 3 * width), F32),
            jax.ShapeDtypeStruct((width, width), F32),
            jax.ShapeDtypeStruct((width,), F32),
            jax.ShapeDtypeStruct((width,), F32),
            jax.ShapeDtypeStruct((rdim, width), F32),
            jax.ShapeDtypeStruct((experts, rdim), F32),
        ],
        scratch_shapes=[
            pltpu.VMEM((2, count, *blocks[0].shape), BF16),
            pltpu.VMEM((count * extra, LANES), F32),
            pltpu.SemaphoreType.DMA((2 * count,)),
        ],
        compiler_params=params(),
        cost_estimate=cost(2),
        name="shared_sums",
    )(me, w_qkv, ga, *blocks)


def exchange(rows):
    peers = lax.axis_size("expert")
    width = rows.shape[1]
    out = lax.all_to_all(
        rows.reshape(peers, -1, width), "expert", split_axis=0, concat_axis=0, tiled=True
    )
    return out.reshape(-1, width)


def core_groups():
    return [[core + 2 * chip for chip in range(lax.axis_size("expert") // 2)] for core in range(2)]


def swap_cores(value):
    peers = lax.axis_size("expert")
    return lax.ppermute(value, "expert", [(j, j ^ 1) for j in range(peers)])


def sum_blocks(blocks):
    return jnp.sum(blocks.astype(F32), axis=0).astype(BF16)


def sum_over_chips(blocks):
    return sum_blocks(
        lax.all_to_all(blocks, "expert", 0, 0, axis_index_groups=core_groups(), tiled=True)
    )


def xor_permute(value, axis, d):
    return lax.ppermute(value, axis, [(j, j ^ d) for j in range(lax.axis_size(axis))])


def on_device(
    tokens,
    segments,
    routes,
    cotangent,
    w_qkv,
    w_attn_out,
    gain_attn,
    gain_ffn,
    w_router,
    embed,
    w_in,
    w_out,
):
    toks, width = tokens.shape
    experts, rdim = embed.shape
    peers = lax.axis_size("expert")
    shards = lax.axis_size("dp")
    chips = peers // 2
    share = w_in.shape[2] // shards
    me = lax.axis_index("expert").astype(I32).reshape(1)
    core = me & 1
    ga, gf = gain_attn.reshape(1, width), gain_ffn.reshape(1, width)
    segr = segments.reshape(1, toks)
    wrt = w_router.T
    hold = lax.optimization_barrier

    keyr, keyn, g_slots = place(routes.reshape(1, toks), cotangent, peers, 2 * toks)
    g_rows = exchange(g_slots).reshape(peers, 2, toks // peers, width)
    q, k, v, lse, mixt, attn_in, res, xa_slots, xb_slots = attend(
        tokens, segr, keyr, w_qkv, w_attn_out, ga, gf
    )
    x_a = exchange(xa_slots)
    gact_a, gt_a = grad_act(g_rows, 0, w_out, share)
    gact_b, gt_b = grad_act(g_rows, 1, w_out, share)
    x_a, xb_slots, gact_b, gt_b, attn_in = hold((x_a, xb_slots, gact_b, gt_b, attn_in))
    x_b = exchange(xb_slots)
    act_a, gp_a, xt_a, gout_a, gwr_a, gemb_a = expert(me, wrt, embed, x_a, w_in, gact_a, share)
    gback_a = exchange(gout_a)
    act_b, gp_b, xt_b, gout_b, gwr_b, gemb_b = expert(me, wrt, embed, x_b, w_in, gact_b, share)
    gout_b, gback_a = hold((gout_b, gback_a))
    gback_b = exchange(gout_b)
    gw_one = expert_grads((gt_a, gt_b), (act_a, act_b), share)
    total_one = lax.psum_scatter(gw_one, "dp", scatter_dimension=0, tiled=True)[0]
    gw_one, late_gp = hold((gw_one, gp_b))
    gw_two = expert_grads((xt_a, xt_b), (gp_a, late_gp), share)
    total_two = lax.psum_scatter(gw_two, "dp", scatter_dimension=0, tiled=True)[0]
    attnt = attn_in.T
    gback_b, gw_two, attnt = hold((gback_b, gw_two, attnt))
    gres, gb, ggf = combine_back(keyr, res, cotangent, gf, (gback_a, gback_b))

    small = jnp.concatenate(
        [
            jnp.pad(ggf.reshape(-1, LANES), ((0, 8 - width // LANES), (0, 0))),
            *jnp.split(gwr_a + gwr_b, width // LANES, axis=1),
            jnp.pad(gemb_a + gemb_b, ((0, 0), (0, LANES - rdim))),
        ],
        axis=0,
    )
    rows = 4 * width // chips
    extra = -(-small.shape[0] // (16 * chips)) * 16
    small = jnp.pad(small, ((0, chips * extra - small.shape[0]), (0, 0)))
    small = (small + swap_cores(small)).astype(BF16).reshape(chips, extra, LANES)
    both, grads = [], []
    for turn in range(PAIRS // 2):
        send, keep, grad = attend_back(
            2 * turn, core, segr, q, k, v, lse, mixt, gb, attnt, w_attn_out
        )
        grads.append(grad)
        got = swap_cores(send)
        both.append((keep.astype(F32) + got.astype(F32)).astype(BF16).reshape(chips, -1, PAIR))
        if turn == 0:
            (gb, grad) = hold((gb, grad))
        elif turn == 1:
            gb, both, small, grad = hold((gb, both, small, grad))
            share_one = sum_over_chips(jnp.concatenate([*both, small], axis=1))
    last, late_act = hold((both[-1], act_b))
    share_two = sum_over_chips(last)
    fout = expert_out_of(act_a, late_act, w_out, share, peers)
    share_two, share_one, fout, total_one = hold((share_two, share_one, fout, total_one))
    blocks = jnp.concatenate([share_one, share_two], axis=0).reshape(shards, -1, LANES)
    blocks = lax.all_to_all(blocks, "dp", 0, 0, tiled=True)
    blocks, fout = hold((blocks, fout))
    fback = exchange(fout.reshape(2 * toks, width))
    total = lax.all_gather(sum_blocks(blocks), "dp", axis=0, tiled=True)
    pieces = [total] + [xor_permute(total, "expert", d) for d in range(2, peers, 2)]
    grad_tokens = grad_tokens_of(tokens, gres, ga, w_qkv, grads)
    out_tokens = combine(keyn, res, fback)
    pieces, grad_tokens, out_tokens = hold((pieces, grad_tokens, out_tokens))
    blocks = pieces + [swap_cores(piece) for piece in pieces]
    grad_w_qkv, grad_w_attn_out, grad_gain_attn, grad_gain_ffn, grad_router, grad_embed = (
        shared_sums(me, blocks, rows, extra, w_qkv, ga, experts, rdim)
    )
    grad_w_qkv, total_two = hold((grad_w_qkv, total_two))
    grad_w_in, grad_w_out = expert_sums(total_two, total_one)
    return (
        out_tokens,
        grad_tokens,
        grad_w_qkv,
        grad_w_attn_out,
        grad_gain_attn,
        grad_gain_ffn,
        grad_router.T,
        grad_embed,
        grad_w_in,
        grad_w_out,
    )


def solution(mesh):
    rows = P(("dp", "expert"), None)
    return jax.shard_map(
        on_device,
        mesh=mesh,
        in_specs=(
            rows,
            rows,
            rows,
            rows,
            P(),
            P(),
            P(),
            P(),
            P(),
            P(),
            P("expert", None, None),
            P("expert", None, None),
        ),
        out_specs=(
            rows,
            rows,
            P(),
            P(),
            P(),
            P(),
            P(),
            P(),
            P("expert", None, "dp"),
            P("expert", "dp", None),
        ),
        check_vma=False,
    )
```

```python
import functools
import math

import jax
import jax.numpy as jnp
from jax import lax
from jax.experimental import pallas as pl
from jax.experimental.pallas import tpu as pltpu
from jax.sharding import PartitionSpec as P

HEADS = 12
HEAD = 64
PAIRS = HEADS // 2
PAIR = 2 * HEAD
QB = 256
LANES = 128
ROUTER_WARMTH = 0.3
NORM_FLOOR = 12.0
EPSILON = 1e-05
MASK_VALUE = -1e30
F32 = jnp.float32
BF16 = jnp.bfloat16
I32 = jnp.int32
NN = (((1,), (0,)), ((), ()))
NT = (((1,), (1,)), ((), ()))
TN = (((0,), (0,)), ((), ()))
HIGHEST = lax.Precision.HIGHEST
MIB = 1 << 20


def mm(a, b, dims=NN, precision=None):
    return lax.dot_general(a, b, dims, precision=precision, preferred_element_type=F32)


def params():
    return pltpu.CompilerParams(vmem_limit_bytes=62 * MIB)


def cost(micros, nbytes=0):
    return pl.CostEstimate(
        flops=int(micros * 1.15e9), bytes_accessed=int(nbytes), transcendentals=0
    )


def whole(shape):
    return pl.BlockSpec(
        shape, lambda *_: (0,) * len(shape), pipeline_mode=pl.Buffered(buffer_count=1)
    )


def smem():
    return pl.BlockSpec(memory_space=pltpu.SMEM)


def norm_back(x, gain, dy):
    inv = lax.rsqrt(jnp.mean(x * x, axis=1, keepdims=True) + EPSILON)
    dn = dy * gain
    dx = inv * dn - x * (inv * inv * inv * jnp.mean(x * dn, axis=1, keepdims=True))
    return dx, jnp.sum(dy * x * inv, axis=0, keepdims=True)


def column_of(row):
    return jnp.broadcast_to(row.astype(F32), (8, row.shape[1])).T[:, :1].astype(row.dtype)


def ones_where(mask):
    return jnp.where(mask, 1.0, 0.0).astype(BF16)


def dispatch(key_row, rows, out_refs):
    at = 0
    for ref in out_refs:
        step = min(2 * QB, ref.shape[0])
        for r in range(0, ref.shape[0], step):
            slot = lax.broadcasted_iota(I32, (step, key_row.shape[1]), 0) + at
            ref[r : r + step, :] = mm(ones_where(key_row == slot), rows).astype(BF16)
            at += step


def place_kernel(peers, rr_ref, cot_ref, keyr_ref, keyn_ref, g_ref):
    toks = cot_ref.shape[0]
    cap = g_ref.shape[0] // peers
    half = cap // 2
    rr = rr_ref[...]
    before = ones_where(
        lax.broadcasted_iota(I32, (toks, toks), 0) <= lax.broadcasted_iota(I32, (toks, toks), 1)
    )
    hot_row = jnp.where(lax.broadcasted_iota(I32, (peers, toks), 0) == rr, 1.0, 0.0)
    upto = mm(hot_row.astype(BF16), before)
    rank = (jnp.sum(hot_row * upto, axis=0, keepdims=True) - 1.0).astype(I32)
    keyr_ref[...] = rr * half + jnp.where(rank < half, rank, rank + (peers - 1) * half)
    keyn_ref[...] = rr * cap + rank
    dispatch(keyn_ref[...], cot_ref[...], (g_ref,))


def place(routes, cot, peers, slots):
    toks, width = cot.shape
    return pl.pallas_call(
        functools.partial(place_kernel, peers),
        out_shape=[
            jax.ShapeDtypeStruct((1, toks), I32),
            jax.ShapeDtypeStruct((1, toks), I32),
            jax.ShapeDtypeStruct((slots, width), BF16),
        ],
        in_specs=[pl.BlockSpec(memory_space=pltpu.VMEM)] * 2,
        compiler_params=params(),
        cost_estimate=cost(5),
        name="place",
    )(routes, cot)


def band(i):
    return max(0, i - 2) * QB, (i + 1) * QB


def fill_bias(bias_ref, segr, count):
    segc = column_of(segr)
    for i in range(count):
        low, high = band(i)
        keys = lax.broadcasted_iota(I32, (high - low, QB), 0) + low
        queries = lax.broadcasted_iota(I32, (high - low, QB), 1) + i * QB
        same = segc[low:high] == segr[:, i * QB : (i + 1) * QB]
        bias_ref[i, : high - low, :] = jnp.where((keys <= queries) & same, 0.0, MASK_VALUE)


def head_mask(values, h):
    lane = lax.broadcasted_iota(I32, values.shape, 1)
    return jnp.where((lane >= h * HEAD) & (lane < (h + 1) * HEAD), values, jnp.zeros_like(values))


def attend_kernel(
    tok_ref,
    segr_ref,
    keyr_ref,
    wq_ref,
    wk_ref,
    wv_ref,
    wo_ref,
    ga_ref,
    gf_ref,
    q_ref,
    k_ref,
    v_ref,
    lse_ref,
    mixt_ref,
    attn_ref,
    res_ref,
    xa_ref,
    xb_ref,
    bias_ref,
    mix_ref,
):
    p = pl.program_id(0)
    toks, width = tok_ref.shape
    count = toks // QB
    both = q_ref.shape[1]

    @pl.when(p == 0)
    def _():
        segr = segr_ref[...]
        segc = column_of(segr)
        for i in range(count):
            low, high = band(i)
            keys = lax.broadcasted_iota(I32, (QB, high - low), 1) + low
            queries = lax.broadcasted_iota(I32, (QB, high - low), 0) + i * QB
            same = segr[:, low:high] == segc[i * QB : (i + 1) * QB]
            bias_ref[i, :, : high - low] = jnp.where((keys <= queries) & same, 0.0, MASK_VALUE)
        x = tok_ref[...].astype(F32)
        inv = lax.rsqrt(jnp.mean(x * x, axis=1, keepdims=True) + EPSILON)
        attn_ref[...] = (x * inv * ga_ref[...]).astype(BF16)

    attn_in = attn_ref[...]
    q_ref[...] = mm(attn_in, wq_ref[...]).astype(BF16)
    k_ref[...] = mm(attn_in, wk_ref[...]).astype(BF16)
    v_ref[...] = mm(attn_in, wv_ref[...]).astype(BF16)
    lane = lax.broadcasted_iota(I32, (QB, PAIR), 1)
    for i in range(count):
        low, high = band(i)
        cols = slice(i * QB, (i + 1) * QB)
        for pair in range(both // PAIR):
            lanes = slice(pair * PAIR, (pair + 1) * PAIR)
            q = q_ref[cols, lanes] * HEAD**-0.5
            keys = k_ref[low:high, lanes]
            values = v_ref[low:high, lanes]
            parts, sums = [], []
            for h in range(2):
                s = mm(head_mask(q, h), keys, NT) + bias_ref[i, :, : high - low]
                top = jnp.max(s, axis=1, keepdims=True)
                w = jnp.exp(s - top)
                total = jnp.sum(w, axis=1, keepdims=True)
                sums.append(top + jnp.log(total))
                parts.append(mm((w * (1.0 / total)).astype(BF16), values))
            mixed = jnp.where(lane < HEAD, parts[0], parts[1])
            lse_ref[pair, :, cols] = jnp.where(lane == 0, sums[0], sums[1]).T[:2]
            mixt_ref[lanes, cols] = mixed.T.astype(BF16)
            at = pl.ds(pl.multiple_of(p * both + pair * PAIR, PAIR), PAIR)
            mix_ref[cols, at] = mixed.astype(BF16)

    @pl.when(p == pl.num_programs(0) - 1)
    def _():
        res = tok_ref[...].astype(F32) + mm(mix_ref[...], wo_ref[...])
        res_ref[...] = res
        inv = lax.rsqrt(jnp.mean(res * res, axis=1, keepdims=True) + EPSILON)
        ffn_in = (res * inv * gf_ref[...]).astype(BF16)
        dispatch(keyr_ref[...], ffn_in, (xa_ref, xb_ref))


def attend(tokens, segr, keyr, w_qkv, w_o, ga, gf):
    toks, width = tokens.shape
    both = 2 * PAIR
    pair_cols = pl.BlockSpec((toks, both), lambda p: (0, p))
    heads = jax.ShapeDtypeStruct((toks, width), BF16)
    weights = [
        pl.BlockSpec((width, both), lambda p, part=part: (0, part * PAIRS // 2 + p))
        for part in range(3)
    ]
    return pl.pallas_call(
        attend_kernel,
        grid=(PAIRS // 2,),
        in_specs=[
            whole((toks, width)),
            whole((1, toks)),
            whole((1, toks)),
            *weights,
            whole((width, width)),
            whole((1, width)),
            whole((1, width)),
        ],
        out_specs=[
            pair_cols,
            pair_cols,
            pair_cols,
            pl.BlockSpec((2, 2, toks), lambda p: (p, 0, 0)),
            pl.BlockSpec((both, toks), lambda p: (p, 0)),
            whole((toks, width)),
            whole((toks, width)),
            whole((toks, width)),
            whole((toks, width)),
        ],
        out_shape=[
            heads,
            heads,
            heads,
            jax.ShapeDtypeStruct((PAIRS, 2, toks), F32),
            jax.ShapeDtypeStruct((width, toks), BF16),
            heads,
            jax.ShapeDtypeStruct((toks, width), F32),
            heads,
            heads,
        ],
        scratch_shapes=[
            pltpu.VMEM((toks // QB, QB, 3 * QB), F32),
            pltpu.VMEM((toks, width), BF16),
        ],
        compiler_params=params(),
        cost_estimate=cost(42),
        name="attend",
    )(tokens, segr, keyr, w_qkv, w_qkv, w_qkv, w_o, ga, gf)


def attend_back_kernel(
    core_ref,
    segr_ref,
    q_ref,
    k_ref,
    v_ref,
    lse_ref,
    mixt_ref,
    gb_ref,
    attnt_ref,
    wo_ref,
    send_ref,
    keep_ref,
    gqkv_ref,
    bias_ref,
    dqt_ref,
    dk_ref,
    dv_ref,
    do_ref,
):
    toks, width = gb_ref.shape
    both = q_ref.shape[1]
    count = toks // QB
    scale = HEAD**-0.5
    fill_bias(bias_ref, segr_ref[...], count)
    gb = gb_ref[...]
    grad_out = mm(gb, wo_ref[...], NT)
    do_ref[...] = grad_out.astype(BF16)
    mixt = mixt_ref[...]
    gwo = mm(mixt, gb).astype(BF16)
    weighted = grad_out.astype(BF16).astype(F32).T * mixt.astype(F32)
    delta = [
        jnp.sum(weighted[h * HEAD : (h + 1) * HEAD], axis=0, keepdims=True)
        for h in range(both // HEAD)
    ]
    kt = k_ref[...].astype(F32).T.astype(BF16)
    dk_ref[...] = jnp.zeros_like(dk_ref)
    dv_ref[...] = jnp.zeros_like(dv_ref)
    for i in range(count):
        low, high = band(i)
        cols = slice(i * QB, (i + 1) * QB)
        for pair in range(both // PAIR):
            lanes = slice(pair * PAIR, (pair + 1) * PAIR)
            q = q_ref[cols, lanes] * scale
            do = do_ref[cols, lanes]
            keys = k_ref[low:high, lanes]
            values = v_ref[low:high, lanes]
            dk_add, dv_add = [], []
            for h in range(2):
                head = slice((2 * pair + h) * HEAD, (2 * pair + h + 1) * HEAD)
                qm, dom = head_mask(q, h), head_mask(do, h)
                s = mm(keys, qm, NT) + bias_ref[i, : high - low, :]
                pr = jnp.exp(s - lse_ref[pair, h : h + 1, cols])
                dpr = mm(values, dom, NT)
                ds = (pr * (dpr - delta[2 * pair + h][:, cols])).astype(BF16)
                dv_add.append(mm(pr.astype(BF16), dom))
                dk_add.append(mm(ds, qm))
                dqt_ref[head, cols] = mm(kt[head, low:high], ds) * scale
            dk_ref[low:high, lanes] += dk_add[0] + dk_add[1]
            dv_ref[low:high, lanes] += dv_add[0] + dv_add[1]
    grads = [
        dqt_ref[...].T.astype(BF16),
        dk_ref[...].astype(BF16),
        dv_ref[...].astype(BF16),
    ]
    for part in range(3):
        gqkv_ref[part] = grads[part]
    gw = mm(attnt_ref[...], jnp.concatenate(grads, axis=1)).astype(BF16)
    for core in range(2):

        @pl.when(core_ref[0] == core)
        def _(core=core):
            for pair, ref in ((1 - core, send_ref), (core, keep_ref)):
                for part in range(3):
                    at = part * both + pair * PAIR
                    ref[part] = gw[:, at : at + PAIR]
                for j in range(width // PAIR):
                    ref[3, j * PAIR : (j + 1) * PAIR, :] = gwo[
                        pair * PAIR : (pair + 1) * PAIR, j * PAIR : (j + 1) * PAIR
                    ]


def attend_back(turn, core, segr, q, k, v, lse, mixt, gb, attnt, w_o):
    toks, width = gb.shape
    both = 2 * PAIR
    pair_cols = pl.BlockSpec((toks, both), lambda p: (0, turn))
    gw_shape = jax.ShapeDtypeStruct((4, width, PAIR), BF16)
    return pl.pallas_call(
        attend_back_kernel,
        grid=(1,),
        in_specs=[
            smem(),
            whole((1, toks)),
            pair_cols,
            pair_cols,
            pair_cols,
            pl.BlockSpec((2, 2, toks), lambda p: (turn, 0, 0)),
            pl.BlockSpec((both, toks), lambda p: (turn, 0)),
            whole((toks, width)),
            whole((width, toks)),
            pl.BlockSpec((both, width), lambda p: (turn, 0)),
        ],
        out_specs=[whole((4, width, PAIR)), whole((4, width, PAIR)), whole((3, toks, both))],
        out_shape=[gw_shape, gw_shape, jax.ShapeDtypeStruct((3, toks, both), BF16)],
        scratch_shapes=[
            pltpu.VMEM((toks // QB, 3 * QB, QB), F32),
            pltpu.VMEM((both, toks), F32),
            pltpu.VMEM((toks, both), F32),
            pltpu.VMEM((toks, both), F32),
            pltpu.VMEM((toks, both), BF16),
        ],
        compiler_params=params(),
        cost_estimate=cost(10 if turn + 1 == PAIRS // 2 else 2),
        name="attend_back",
    )(core, segr, q, k, v, lse, mixt, gb, attnt, w_o)


def grad_tokens_kernel(tok_ref, gres_ref, ga_ref, w_ref, *rest):
    *g_refs, out_ref = rest
    grads = [ref[part] for part in range(3) for ref in g_refs]
    dy = mm(jnp.concatenate(grads, axis=1), w_ref[...], NT)
    dx, _ = norm_back(tok_ref[...].astype(F32), ga_ref[...], dy)
    out_ref[...] = gres_ref[...] + dx


def grad_tokens_of(tokens, gres, ga, w_qkv, grads):
    toks, width = tokens.shape
    rows = 2 * QB
    tile = pl.BlockSpec((rows, width), lambda i: (i, 0))
    return pl.pallas_call(
        grad_tokens_kernel,
        grid=(toks // rows,),
        in_specs=[tile, tile, whole((1, width)), whole(w_qkv.shape)]
        + [pl.BlockSpec((3, rows, 2 * PAIR), lambda i: (0, i, 0))] * len(grads),
        out_specs=tile,
        out_shape=jax.ShapeDtypeStruct((toks, width), F32),
        compiler_params=params(),
        cost_estimate=cost(9),
        name="grad_tokens",
    )(tokens, gres, ga, w_qkv, *grads)


def unit_scale(values, axis):
    total = jnp.sum(values * values, axis=axis, keepdims=True)
    return lax.rsqrt(jnp.maximum(total, NORM_FLOOR)), total


def unit_back(values, inv, total, grad, axis):
    passed = jnp.where(total > NORM_FLOOR, 1.0, jnp.where(total == NORM_FLOOR, 0.5, 0.0))
    inner = jnp.sum(grad * values, axis=axis, keepdims=True)
    return inv * grad - passed * inv * inv * inv * inner * values


def gelu_and_slope(h):
    cdf = 0.5 + 0.5 * lax.erf(h * 0.7071067811865476)
    pdf = 0.3989422804014327 * jnp.exp(-0.5 * h * h)
    return h * cdf, cdf + h * pdf


def route(me, x, wrt, emb):
    z = mm(wrt, x, NT)
    inv, total = unit_scale(z, 0)
    zn = z * inv
    en = emb * unit_scale(emb, 1)[0]
    logits = mm(en, zn, NN, HIGHEST) / ROUTER_WARMTH
    w = jnp.exp(logits - jnp.max(logits, axis=0, keepdims=True))
    chances = w / jnp.sum(w, axis=0, keepdims=True)
    mine = jnp.where(lax.broadcasted_iota(I32, logits.shape, 0) == me, 1.0, 0.0)
    return z, inv, total, zn, en, chances, mine


def expert_kernel(
    me_ref,
    wrt_ref,
    emb_ref,
    x_ref,
    win_ref,
    ga_ref,
    act_ref,
    gp_ref,
    xt_ref,
    gout_ref,
    gwrt_ref,
    gemb_ref,
    w_s,
    gp_s,
    acc_s,
    gate_s,
):
    c = pl.program_id(0)
    rows, width = x_ref.shape
    me = me_ref[0]

    @pl.when(c == 0)
    def _():
        chances, mine = route(me, x_ref[...], wrt_ref[...], emb_ref[...])[-2:]
        gate = column_of(jnp.sum(chances * mine, axis=0, keepdims=True))
        gate_s[...] = jnp.broadcast_to(gate, (rows, LANES))
        acc_s[...] = jnp.zeros_like(acc_s)
        for r in range(0, rows, QB):
            xt_ref[:, r : r + QB] = x_ref[r : r + QB, :].T

    w_in = win_ref[0]
    wide = w_in.shape[1]
    chunk = pl.ds(pl.multiple_of(c * wide, LANES), wide)
    w_s[:, chunk] = w_in
    step = min(2 * QB, rows)
    for r in range(0, rows, step):
        part = slice(r, r + step)
        h = mm(x_ref[part, :], w_in)
        act, slope = gelu_and_slope(h)
        gate = jnp.concatenate([gate_s[part, :]] * (wide // LANES), axis=1)
        ga = ga_ref[part, :].astype(F32)
        act = act * gate
        act_ref[part, :] = act.astype(BF16)
        gp = (ga * (slope * gate)).astype(BF16)
        gp_s[part, chunk] = gp
        gp_ref[part, :] = gp
        prod = act * ga
        folded = prod[:, :LANES]
        for j in range(LANES, wide, LANES):
            folded = folded + prod[:, j : j + LANES]
        acc_s[part, :] += folded

    @pl.when(c == pl.num_programs(0) - 1)
    def _():
        x, wrt, emb = x_ref[...], wrt_ref[...], emb_ref[...]
        z, inv, total, zn, en, chances, mine = route(me, x, wrt, emb)
        weight = jnp.sum(acc_s[...].T, axis=0, keepdims=True)
        dl = weight * (mine - chances) / ROUTER_WARMTH
        gen = mm(dl, zn, NT, HIGHEST)
        dz = unit_back(z, inv, total, mm(en, dl, TN, HIGHEST), 0)
        dz_top = dz.astype(BF16)
        dz_low = (dz - dz_top.astype(F32)).astype(BF16)
        gwrt_ref[...] = mm(dz_top, x) + mm(dz_low, x)
        einv, etotal = unit_scale(emb, 1)
        gemb_ref[...] = unit_back(emb, einv, etotal, gen, 1)
        dz_top, dz_low = dz_top.astype(F32).T.astype(BF16), dz_low.astype(F32).T.astype(BF16)
        for r in range(0, rows, step):
            part = slice(r, r + step)
            back = mm(gp_s[part, :], w_s[...], NT).astype(BF16).astype(F32)
            back = back + mm(dz_top[part], wrt) + mm(dz_low[part], wrt)
            gout_ref[part, :] = back.astype(BF16)


def expert(me, wrt, emb, x, w_in, ga, wide):
    rows, width = x.shape
    hidden = w_in.shape[2]
    cols = pl.BlockSpec((rows, wide), lambda c: (0, c))
    hid = jax.ShapeDtypeStruct((rows, hidden), BF16)
    return pl.pallas_call(
        expert_kernel,
        grid=(hidden // wide,),
        in_specs=[
            smem(),
            whole(wrt.shape),
            whole(emb.shape),
            whole((rows, width)),
            pl.BlockSpec((1, width, wide), lambda c: (0, 0, c)),
            cols,
        ],
        out_specs=[
            cols,
            cols,
            whole((width, rows)),
            whole((rows, width)),
            whole(wrt.shape),
            whole(emb.shape),
        ],
        out_shape=[
            hid,
            hid,
            jax.ShapeDtypeStruct((width, rows), BF16),
            jax.ShapeDtypeStruct((rows, width), BF16),
            jax.ShapeDtypeStruct(wrt.shape, F32),
            jax.ShapeDtypeStruct(emb.shape, F32),
        ],
        scratch_shapes=[
            pltpu.VMEM((width, hidden), BF16),
            pltpu.VMEM((rows, hidden), BF16),
            pltpu.VMEM((rows, LANES), F32),
            pltpu.VMEM((rows, LANES), F32),
        ],
        compiler_params=params(),
        cost_estimate=cost(23),
        name="expert",
    )(me, wrt, emb, x, w_in, ga)


def early_grads_kernel(
    gta_ref, gtb_ref, xta_ref, xtb_ref, acta_ref, actb_ref, gpa_ref, gpb_ref, out_ref, gt_s, xt_s
):
    rows = gta_ref.shape[1]
    width = gta_ref.shape[0]

    @pl.when(pl.program_id(0) == 0)
    def _():
        gt_s[:, :rows] = gta_ref[...]
        gt_s[:, rows:] = gtb_ref[...]
        xt_s[:, :rows] = xta_ref[...]
        xt_s[:, rows:] = xtb_ref[...]

    act = jnp.concatenate([acta_ref[...], actb_ref[...]], axis=0)
    out_ref[0, :width] = mm(gt_s[...], act).astype(BF16)
    gp = jnp.concatenate([gpa_ref[...], gpb_ref[...]], axis=0)
    out_ref[0, width:] = mm(xt_s[...], gp).astype(BF16)


def early_grads(gts, xts, acts, gps, wide):
    width, rows = gts[0].shape
    third = width // 3
    steps = acts[0].shape[1] // wide
    return pl.pallas_call(
        early_grads_kernel,
        grid=(steps,),
        in_specs=[whole((width, rows))] * 2
        + [whole((third, rows))] * 2
        + [pl.BlockSpec((rows, wide), lambda c: (0, c))] * 4,
        out_specs=pl.BlockSpec((1, width + third, wide), lambda c: (c, 0, 0)),
        out_shape=jax.ShapeDtypeStruct((steps, width + third, wide), BF16),
        scratch_shapes=[
            pltpu.VMEM((width, 2 * rows), BF16),
            pltpu.VMEM((third, 2 * rows), BF16),
        ],
        compiler_params=params(),
        cost_estimate=cost(10),
        name="early_grads",
    )(*gts, *xts, *acts, *gps)


def late_grads_kernel(xta_ref, xtb_ref, gpa_ref, gpb_ref, out_ref, xt_s):
    width, rows = xta_ref.shape
    third = width // 3

    @pl.when(pl.program_id(0) == 0)
    def _():
        xt_s[:, :rows] = xta_ref[third:, :]
        xt_s[:, rows:] = xtb_ref[third:, :]

    gp = jnp.concatenate([gpa_ref[...], gpb_ref[...]], axis=0)
    out_ref[0] = mm(xt_s[...], gp).astype(BF16)


def late_grads(xts, gps, wide):
    width, rows = xts[0].shape
    left = width - width // 3
    steps = gps[0].shape[1] // wide
    return pl.pallas_call(
        late_grads_kernel,
        grid=(steps,),
        in_specs=[whole((width, rows))] * 2 + [pl.BlockSpec((rows, wide), lambda c: (0, c))] * 2,
        out_specs=pl.BlockSpec((1, left, wide), lambda c: (c, 0, 0)),
        out_shape=jax.ShapeDtypeStruct((steps, left, wide), BF16),
        scratch_shapes=[pltpu.VMEM((left, 2 * rows), BF16)],
        compiler_params=params(),
        cost_estimate=cost(10),
        name="late_grads",
    )(*xts, *gps)


def grad_act_kernel(g_ref, wout_ref, out_ref, gt_ref):
    g = g_ref[...].reshape(out_ref.shape[0], g_ref.shape[-1])

    @pl.when(pl.program_id(0) == 0)
    def _():
        gt_ref[...] = g.T

    out_ref[...] = mm(g, wout_ref[0], NT).astype(BF16)


def grad_act(g, half, w_out, wide):
    peers, _, slots, width = g.shape
    rows = peers * slots
    hidden = w_out.shape[1]
    return pl.pallas_call(
        grad_act_kernel,
        grid=(hidden // wide,),
        in_specs=[
            pl.BlockSpec((peers, 1, slots, width), lambda c: (0, half, 0, 0)),
            pl.BlockSpec((1, wide, width), lambda c: (0, c, 0)),
        ],
        out_specs=[pl.BlockSpec((rows, wide), lambda c: (0, c)), whole((width, rows))],
        out_shape=[
            jax.ShapeDtypeStruct((rows, hidden), BF16),
            jax.ShapeDtypeStruct((width, rows), BF16),
        ],
        compiler_params=params(),
        cost_estimate=cost(7),
        name="grad_act",
    )(g, w_out)


def expert_out_kernel(acta_ref, actb_ref, wout_ref, out_ref, acc_ref):
    c = pl.program_id(0)
    rows = acta_ref.shape[0]
    peers, _, slots, width = out_ref.shape

    @pl.when(c == 0)
    def _():
        acc_ref[...] = jnp.zeros_like(acc_ref)

    w_out = wout_ref[0]
    acc_ref[:rows, :] += mm(acta_ref[...], w_out)
    acc_ref[rows:, :] += mm(actb_ref[...], w_out)

    @pl.when(c == pl.num_programs(0) - 1)
    def _():
        for h in range(2):
            part = acc_ref[h * rows : (h + 1) * rows, :].astype(BF16)
            out_ref[:, h] = part.reshape(peers, slots, width)


def expert_out_of(acta, actb, w_out, wide, peers):
    rows, hidden = acta.shape
    width = w_out.shape[2]
    shape = (peers, 2, rows // peers, width)
    cols = pl.BlockSpec((rows, wide), lambda c: (0, c))
    return pl.pallas_call(
        expert_out_kernel,
        grid=(hidden // wide,),
        in_specs=[cols, cols, pl.BlockSpec((1, wide, width), lambda c: (0, c, 0))],
        out_specs=whole(shape),
        out_shape=jax.ShapeDtypeStruct(shape, BF16),
        scratch_shapes=[pltpu.VMEM((2 * rows, width), F32)],
        compiler_params=params(),
        cost_estimate=cost(14),
        name="expert_out",
    )(acta, actb, w_out)


def expert_sums_kernel(early_ref, late_ref, win_ref, wout_ref):
    width = wout_ref.shape[2]
    third = width // 3
    win_ref[0, :third] = early_ref[width:].astype(F32)
    win_ref[0, third:] = late_ref[...].astype(F32)
    wout_ref[0] = early_ref[:width].astype(F32).T


def expert_sums(early, late):
    share = early.shape[1]
    width = early.shape[0] * 3 // 4
    return pl.pallas_call(
        expert_sums_kernel,
        grid=(share // LANES,),
        in_specs=[
            pl.BlockSpec((early.shape[0], LANES), lambda k: (0, k)),
            pl.BlockSpec((late.shape[0], LANES), lambda k: (0, k)),
        ],
        out_specs=[
            pl.BlockSpec((1, width, LANES), lambda k: (0, 0, k)),
            pl.BlockSpec((1, LANES, width), lambda k: (0, k, 0)),
        ],
        out_shape=[
            jax.ShapeDtypeStruct((1, width, share), F32),
            jax.ShapeDtypeStruct((1, share, width), F32),
        ],
        compiler_params=params(),
        cost_estimate=cost(3),
        name="expert_sums",
    )(early, late)


def gather_rows(key_row, row_refs):
    keys = column_of(key_row)
    total, at = None, 0
    for ref in row_refs:
        column = lax.broadcasted_iota(I32, (keys.shape[0], ref.shape[0]), 1) + at
        part = mm(ones_where(keys == column), ref[...])
        total = part if total is None else total + part
        at += ref.shape[0]
    return total


def combine_back_kernel(
    keyr_ref, res_ref, cot_ref, gf_ref, ra_ref, rb_ref, gres_ref, gb_ref, gain_ref
):
    dy = gather_rows(keyr_ref[...], (ra_ref, rb_ref))

    @pl.when(pl.program_id(0) == 0)
    def _():
        gain_ref[...] = jnp.zeros_like(gain_ref)

    dx, dgain = norm_back(res_ref[...], gf_ref[...], dy)
    gain_ref[...] += dgain
    grad = cot_ref[...].astype(F32) + dx
    gres_ref[...] = grad
    gb_ref[...] = grad.astype(BF16)


def combine_back(keyr, res, cot, gf, rows):
    toks, width = res.shape
    tile = pl.BlockSpec((QB, width), lambda i: (i, 0))
    return pl.pallas_call(
        combine_back_kernel,
        grid=(toks // QB,),
        in_specs=[
            pl.BlockSpec((1, QB), lambda i: (0, i)),
            tile,
            tile,
            whole((1, width)),
            *[whole(r.shape) for r in rows],
        ],
        out_specs=[tile, tile, whole((1, width))],
        out_shape=[
            jax.ShapeDtypeStruct((toks, width), F32),
            jax.ShapeDtypeStruct((toks, width), BF16),
            jax.ShapeDtypeStruct((1, width), F32),
        ],
        compiler_params=params(),
        cost_estimate=cost(100),
        name="combine_back",
    )(keyr, res, cot, gf, *rows)


def combine_kernel(keyn_ref, res_ref, rows_ref, out_ref):
    out_ref[...] = (res_ref[...] + gather_rows(keyn_ref[...], (rows_ref,))).astype(BF16)


def combine(keyn, res, rows):
    toks, width = res.shape
    tile = pl.BlockSpec((QB, width), lambda i: (i, 0))
    return pl.pallas_call(
        combine_kernel,
        grid=(toks // QB,),
        in_specs=[
            pl.BlockSpec((1, QB), lambda i: (0, i)),
            tile,
            whole(rows.shape),
        ],
        out_specs=tile,
        out_shape=jax.ShapeDtypeStruct((toks, width), BF16),
        compiler_params=params(),
        cost_estimate=cost(5),
        name="combine",
    )(keyn, res, rows)


def shared_sums_kernel(count, experts, rows, extra, me_ref, w_ref, ga_ref, *rest):
    blocks, rest = rest[: 2 * count], rest[2 * count :]
    qkv_ref, o_ref, gain_ref, gain_ffn_ref, router_ref, embed_ref = rest[:6]
    held, small_s, sems = rest[6:]
    i = pl.program_id(0)
    width = o_ref.shape[1]
    chip, core = me_ref[0] >> 1, me_ref[0] & 1
    grain = math.gcd(rows, PAIR)

    @pl.when(i == 0)
    def _():
        copies = []
        for n, ref in enumerate(blocks):
            side = core if n < count else 1 - core
            copies.append(
                pltpu.make_async_copy(ref, held.at[side, (n % count) ^ chip], sems.at[n])
            )
        for copy in copies:
            copy.start()
        for copy in copies:
            copy.wait()

    def piece(side, two, row):
        base = two * rows + (two // 2) * extra
        pieces = []
        for t in range(0, PAIR, grain):
            at = pl.multiple_of(base + (row + t) % rows, math.gcd(grain, extra))
            pieces.append(held[side, (row + t) // rows, pl.ds(at, grain), :])
        return jnp.concatenate(pieces, axis=0).astype(F32)

    for pair in range(PAIRS):
        for part in range(3):
            at = (part * PAIRS + pair) * PAIR
            qkv_ref[:, at : at + PAIR] = piece(pair % 2, pair // 2, part * width + i * PAIR)
    for two in range(PAIRS // 2):

        @pl.when(i // 2 == two)
        def _(two=two):
            for j in range(width // PAIR):
                o_ref[:, j * PAIR : (j + 1) * PAIR] = piece(i % 2, two, 3 * width + j * PAIR)

    folded = jnp.zeros((PAIR, LANES), F32)
    for at in range(0, qkv_ref.shape[1], LANES):
        folded += qkv_ref[:, at : at + LANES] * w_ref[:, at : at + LANES].astype(F32)
    gain = jnp.sum(folded.T, axis=0, keepdims=True) / ga_ref[...]
    gain_ref[pl.ds(pl.multiple_of(i * PAIR, PAIR), PAIR)] = gain[0]

    @pl.when(i == 0)
    def _():
        for t in range(count):
            part = slice(2 * rows, 2 * rows + extra)
            small_s[t * extra : (t + 1) * extra, :] = held[0, t, part, :].astype(F32)
        rdim = router_ref.shape[0]
        for j in range(width // LANES):
            lanes = slice(j * LANES, (j + 1) * LANES)
            gain_ffn_ref[lanes] = small_s[j, :]
            at = 8 + j * rdim
            router_ref[:, lanes] = small_s[at : at + rdim, :]
        at = 8 + width // LANES * rdim
        embed_ref[...] = small_s[at : at + experts, :rdim]


def shared_sums(me, blocks, rows, extra, w_qkv, ga, experts, rdim):
    width = w_qkv.shape[0]
    count = len(blocks) // 2
    lanes = pl.BlockSpec((1, PAIR), lambda i: (0, i))
    return pl.pallas_call(
        functools.partial(shared_sums_kernel, count, experts, rows, extra),
        grid=(width // PAIR,),
        in_specs=[smem(), pl.BlockSpec((PAIR, 3 * width), lambda i: (i, 0)), lanes]
        + [pl.BlockSpec(memory_space=pl.ANY)] * (2 * count),
        out_specs=[
            pl.BlockSpec((PAIR, 3 * width), lambda i: (i, 0)),
            pl.BlockSpec((PAIR, width), lambda i: (i, 0)),
            pl.BlockSpec((width,), lambda i: (0,)),
            pl.BlockSpec((width,), lambda i: (0,)),
            whole((rdim, width)),
            whole((experts, rdim)),
        ],
        out_shape=[
            jax.ShapeDtypeStruct((width, 3 * width), F32),
            jax.ShapeDtypeStruct((width, width), F32),
            jax.ShapeDtypeStruct((width,), F32),
            jax.ShapeDtypeStruct((width,), F32),
            jax.ShapeDtypeStruct((rdim, width), F32),
            jax.ShapeDtypeStruct((experts, rdim), F32),
        ],
        scratch_shapes=[
            pltpu.VMEM((2, count, *blocks[0].shape), BF16),
            pltpu.VMEM((count * extra, LANES), F32),
            pltpu.SemaphoreType.DMA((2 * count,)),
        ],
        compiler_params=params(),
        cost_estimate=cost(2),
        name="shared_sums",
    )(me, w_qkv, ga, *blocks)


def exchange(rows):
    peers = lax.axis_size("expert")
    width = rows.shape[1]
    out = lax.all_to_all(
        rows.reshape(peers, -1, width), "expert", split_axis=0, concat_axis=0, tiled=True
    )
    return out.reshape(-1, width)


def core_groups():
    return [[core + 2 * chip for chip in range(lax.axis_size("expert") // 2)] for core in range(2)]


def swap_cores(value):
    peers = lax.axis_size("expert")
    return lax.ppermute(value, "expert", [(j, j ^ 1) for j in range(peers)])


def sum_blocks(blocks):
    return jnp.sum(blocks.astype(F32), axis=0).astype(BF16)


def sum_over_chips(blocks):
    return sum_blocks(
        lax.all_to_all(blocks, "expert", 0, 0, axis_index_groups=core_groups(), tiled=True)
    )


def xor_permute(value, axis, d):
    return lax.ppermute(value, axis, [(j, j ^ d) for j in range(lax.axis_size(axis))])


def gather_over_dp(part, beside):
    groups = lax.axis_size("dp")
    me = lax.axis_index("dp")
    parts = [part] + [xor_permute(part, "dp", d) for d in range(1, groups)]
    parts, beside = lax.optimization_barrier((parts, beside))
    parts = jnp.stack(parts)
    for bit in range((groups - 1).bit_length()):
        split = parts.reshape(-1, 2, 1 << bit, *part.shape)
        parts = jnp.where((me >> bit) & 1 == 1, split[:, ::-1], split)
    return parts.reshape(-1, part.shape[1]), beside


def on_device(
    tokens,
    segments,
    routes,
    cotangent,
    w_qkv,
    w_attn_out,
    gain_attn,
    gain_ffn,
    w_router,
    embed,
    w_in,
    w_out,
):
    toks, width = tokens.shape
    experts, rdim = embed.shape
    peers = lax.axis_size("expert")
    shards = lax.axis_size("dp")
    chips = peers // 2
    share = w_in.shape[2] // shards
    me = lax.axis_index("expert").astype(I32).reshape(1)
    core = me & 1
    ga, gf = gain_attn.reshape(1, width), gain_ffn.reshape(1, width)
    segr = segments.reshape(1, toks)
    wrt = w_router.T
    hold = lax.optimization_barrier

    keyr, keyn, g_slots = place(routes.reshape(1, toks), cotangent, peers, 2 * toks)
    g_rows = exchange(g_slots).reshape(peers, 2, toks // peers, width)
    q, k, v, lse, mixt, attn_in, res, xa_slots, xb_slots = attend(
        tokens, segr, keyr, w_qkv, w_attn_out, ga, gf
    )
    x_a = exchange(xa_slots)
    gact_a, gt_a = grad_act(g_rows, 0, w_out, share)
    gact_b, gt_b = grad_act(g_rows, 1, w_out, share)
    x_a, xb_slots, gact_b, gt_b, attn_in = hold((x_a, xb_slots, gact_b, gt_b, attn_in))
    x_b = exchange(xb_slots)
    act_a, gp_a, xt_a, gout_a, gwr_a, gemb_a = expert(me, wrt, embed, x_a, w_in, gact_a, share)
    gback_a = exchange(gout_a)
    act_b, gp_b, xt_b, gout_b, gwr_b, gemb_b = expert(me, wrt, embed, x_b, w_in, gact_b, share)
    gout_b, gback_a = hold((gout_b, gback_a))
    gback_b = exchange(gout_b)
    early = early_grads((gt_a, gt_b), (xt_a, xt_b), (act_a, act_b), (gp_a, gp_b), share)
    early_sum = lax.psum_scatter(early, "dp", scatter_dimension=0, tiled=True)[0]
    attnt = attn_in.T
    gback_b, early, attnt = hold((gback_b, early, attnt))
    gres, gb, ggf = combine_back(keyr, res, cotangent, gf, (gback_a, gback_b))

    small = jnp.concatenate(
        [
            jnp.pad(ggf.reshape(-1, LANES), ((0, 8 - width // LANES), (0, 0))),
            *jnp.split(gwr_a + gwr_b, width // LANES, axis=1),
            jnp.pad(gemb_a + gemb_b, ((0, 0), (0, LANES - rdim))),
        ],
        axis=0,
    )
    rows = 4 * width // chips
    extra = -(-small.shape[0] // (16 * chips)) * 16
    small = jnp.pad(small, ((0, chips * extra - small.shape[0]), (0, 0)))
    small = (small + swap_cores(small)).astype(BF16).reshape(chips, extra, LANES)
    both, grads = [], []
    for turn in range(PAIRS // 2):
        send, keep, grad = attend_back(
            turn, core, segr, q, k, v, lse, mixt, gb, attnt, w_attn_out
        )
        grads.append(grad)
        got = swap_cores(send)
        both.append((keep.astype(F32) + got.astype(F32)).astype(BF16).reshape(chips, -1, PAIR))
        if turn == 0:
            (gb, grad) = hold((gb, grad))
        elif turn == 1:
            gb, both, small, grad = hold((gb, both, small, grad))
            share_one = sum_over_chips(jnp.concatenate([*both, small], axis=1))
    last, late_act, share_one = hold((both[-1], act_b, share_one))
    share_two = sum_over_chips(last)
    fout = expert_out_of(act_a, late_act, w_out, share, peers)
    share_two, fout, late_gp, late_res = hold((share_two, fout, gp_b, gres))
    blocks = jnp.concatenate([share_one, share_two], axis=0).reshape(shards, -1, LANES)
    blocks = lax.all_to_all(blocks, "dp", 0, 0, tiled=True)
    late = late_grads((xt_a, xt_b), (gp_a, late_gp), share)
    grad_tokens = grad_tokens_of(tokens, late_res, ga, w_qkv, grads)
    blocks, fout, late, grad_tokens, early_sum = hold(
        (blocks, fout, late, grad_tokens, early_sum)
    )
    fback = exchange(fout.reshape(2 * toks, width))
    total, fback = gather_over_dp(sum_blocks(blocks), fback)
    late_sum = lax.psum_scatter(late, "dp", scatter_dimension=0, tiled=True)[0]
    pieces = [total] + [xor_permute(total, "expert", d) for d in range(2, peers, 2)]
    out_tokens = combine(keyn, res, fback)
    pieces, out_tokens = hold((pieces, out_tokens))
    blocks = pieces + [swap_cores(piece) for piece in pieces]
    grad_w_qkv, grad_w_attn_out, grad_gain_attn, grad_gain_ffn, grad_router, grad_embed = (
        shared_sums(me, blocks, rows, extra, w_qkv, ga, experts, rdim)
    )
    grad_w_qkv, late_sum = hold((grad_w_qkv, late_sum))
    grad_w_in, grad_w_out = expert_sums(early_sum, late_sum)
    return (
        out_tokens,
        grad_tokens,
        grad_w_qkv,
        grad_w_attn_out,
        grad_gain_attn,
        grad_gain_ffn,
        grad_router.T,
        grad_embed,
        grad_w_in,
        grad_w_out,
    )


def solution(mesh):
    rows = P(("dp", "expert"), None)
    return jax.shard_map(
        on_device,
        mesh=mesh,
        in_specs=(
            rows,
            rows,
            rows,
            rows,
            P(),
            P(),
            P(),
            P(),
            P(),
            P(),
            P("expert", None, None),
            P("expert", None, None),
        ),
        out_specs=(
            rows,
            rows,
            P(),
            P(),
            P(),
            P(),
            P(),
            P(),
            P("expert", None, "dp"),
            P("expert", "dp", None),
        ),
        check_vma=False,
    )
```

```python
import functools
import math

import jax
import jax.numpy as jnp
from jax import lax
from jax.experimental import pallas as pl
from jax.experimental.pallas import tpu as pltpu
from jax.sharding import PartitionSpec as P

HEADS = 12
HEAD = 64
PAIRS = HEADS // 2
PAIR = 2 * HEAD
QB = 256
LANES = 128
ROUTER_WARMTH = 0.3
NORM_FLOOR = 12.0
EPSILON = 1e-05
MASK_VALUE = -1e30
F32 = jnp.float32
BF16 = jnp.bfloat16
I32 = jnp.int32
NN = (((1,), (0,)), ((), ()))
NT = (((1,), (1,)), ((), ()))
TN = (((0,), (0,)), ((), ()))
HIGHEST = lax.Precision.HIGHEST
MIB = 1 << 20


def mm(a, b, dims=NN, precision=None):
    return lax.dot_general(a, b, dims, precision=precision, preferred_element_type=F32)


def params():
    return pltpu.CompilerParams(vmem_limit_bytes=62 * MIB)


def cost(micros, nbytes=0):
    return pl.CostEstimate(
        flops=int(micros * 1.15e9), bytes_accessed=int(nbytes), transcendentals=0
    )


def whole(shape):
    return pl.BlockSpec(
        shape, lambda *_: (0,) * len(shape), pipeline_mode=pl.Buffered(buffer_count=1)
    )


def smem():
    return pl.BlockSpec(memory_space=pltpu.SMEM)


def norm_back(x, gain, dy):
    inv = lax.rsqrt(jnp.mean(x * x, axis=1, keepdims=True) + EPSILON)
    dn = dy * gain
    dx = inv * dn - x * (inv * inv * inv * jnp.mean(x * dn, axis=1, keepdims=True))
    return dx, jnp.sum(dy * x * inv, axis=0, keepdims=True)


def column_of(row):
    return jnp.broadcast_to(row.astype(F32), (8, row.shape[1])).T[:, :1].astype(row.dtype)


def ones_where(mask):
    return jnp.where(mask, 1.0, 0.0).astype(BF16)


def dispatch(key_row, rows, out_refs):
    at = 0
    for ref in out_refs:
        step = min(2 * QB, ref.shape[0])
        for r in range(0, ref.shape[0], step):
            slot = lax.broadcasted_iota(I32, (step, key_row.shape[1]), 0) + at
            ref[r : r + step, :] = mm(ones_where(key_row == slot), rows).astype(BF16)
            at += step


def place_kernel(peers, rr_ref, cot_ref, keyr_ref, keyn_ref, g_ref):
    toks = cot_ref.shape[0]
    cap = g_ref.shape[0] // peers
    half = cap // 2
    rr = rr_ref[...]
    before = ones_where(
        lax.broadcasted_iota(I32, (toks, toks), 0) <= lax.broadcasted_iota(I32, (toks, toks), 1)
    )
    hot_row = jnp.where(lax.broadcasted_iota(I32, (peers, toks), 0) == rr, 1.0, 0.0)
    upto = mm(hot_row.astype(BF16), before)
    rank = (jnp.sum(hot_row * upto, axis=0, keepdims=True) - 1.0).astype(I32)
    keyr_ref[...] = rr * half + jnp.where(rank < half, rank, rank + (peers - 1) * half)
    keyn_ref[...] = rr * cap + rank
    dispatch(keyn_ref[...], cot_ref[...], (g_ref,))


def place(routes, cot, peers, slots):
    toks, width = cot.shape
    return pl.pallas_call(
        functools.partial(place_kernel, peers),
        out_shape=[
            jax.ShapeDtypeStruct((1, toks), I32),
            jax.ShapeDtypeStruct((1, toks), I32),
            jax.ShapeDtypeStruct((slots, width), BF16),
        ],
        in_specs=[pl.BlockSpec(memory_space=pltpu.VMEM)] * 2,
        compiler_params=params(),
        cost_estimate=cost(5),
        name="place",
    )(routes, cot)


def band(i):
    return max(0, i - 2) * QB, (i + 1) * QB


def fill_bias(bias_ref, segr, count):
    segc = column_of(segr)
    for i in range(count):
        low, high = band(i)
        keys = lax.broadcasted_iota(I32, (high - low, QB), 0) + low
        queries = lax.broadcasted_iota(I32, (high - low, QB), 1) + i * QB
        same = segc[low:high] == segr[:, i * QB : (i + 1) * QB]
        bias_ref[i, : high - low, :] = jnp.where((keys <= queries) & same, 0.0, MASK_VALUE)


def head_mask(values, h):
    lane = lax.broadcasted_iota(I32, values.shape, 1)
    return jnp.where((lane >= h * HEAD) & (lane < (h + 1) * HEAD), values, jnp.zeros_like(values))


def attend_kernel(
    tok_ref,
    segr_ref,
    keyr_ref,
    wq_ref,
    wk_ref,
    wv_ref,
    wo_ref,
    ga_ref,
    gf_ref,
    q_ref,
    k_ref,
    v_ref,
    lse_ref,
    mixt_ref,
    attn_ref,
    res_ref,
    xa_ref,
    xb_ref,
    bias_ref,
    mix_ref,
):
    p = pl.program_id(0)
    toks, width = tok_ref.shape
    count = toks // QB
    both = q_ref.shape[1]

    @pl.when(p == 0)
    def _():
        segr = segr_ref[...]
        segc = column_of(segr)
        for i in range(count):
            low, high = band(i)
            keys = lax.broadcasted_iota(I32, (QB, high - low), 1) + low
            queries = lax.broadcasted_iota(I32, (QB, high - low), 0) + i * QB
            same = segr[:, low:high] == segc[i * QB : (i + 1) * QB]
            bias_ref[i, :, : high - low] = jnp.where((keys <= queries) & same, 0.0, MASK_VALUE)
        x = tok_ref[...].astype(F32)
        inv = lax.rsqrt(jnp.mean(x * x, axis=1, keepdims=True) + EPSILON)
        attn_ref[...] = (x * inv * ga_ref[...]).astype(BF16)

    attn_in = attn_ref[...]
    q_ref[...] = mm(attn_in, wq_ref[...]).astype(BF16)
    k_ref[...] = mm(attn_in, wk_ref[...]).astype(BF16)
    v_ref[...] = mm(attn_in, wv_ref[...]).astype(BF16)
    lane = lax.broadcasted_iota(I32, (QB, PAIR), 1)
    for i in range(count):
        low, high = band(i)
        cols = slice(i * QB, (i + 1) * QB)
        for pair in range(both // PAIR):
            lanes = slice(pair * PAIR, (pair + 1) * PAIR)
            q = q_ref[cols, lanes] * HEAD**-0.5
            keys = k_ref[low:high, lanes]
            values = v_ref[low:high, lanes]
            parts, sums = [], []
            for h in range(2):
                s = mm(head_mask(q, h), keys, NT) + bias_ref[i, :, : high - low]
                top = jnp.max(s, axis=1, keepdims=True)
                w = jnp.exp(s - top)
                total = jnp.sum(w, axis=1, keepdims=True)
                sums.append(top + jnp.log(total))
                parts.append(mm((w * (1.0 / total)).astype(BF16), values))
            mixed = jnp.where(lane < HEAD, parts[0], parts[1])
            lse_ref[pair, :, cols] = jnp.where(lane == 0, sums[0], sums[1]).T[:2]
            mixt_ref[lanes, cols] = mixed.T.astype(BF16)
            at = pl.ds(pl.multiple_of(p * both + pair * PAIR, PAIR), PAIR)
            mix_ref[cols, at] = mixed.astype(BF16)

    @pl.when(p == pl.num_programs(0) - 1)
    def _():
        res = tok_ref[...].astype(F32) + mm(mix_ref[...], wo_ref[...])
        res_ref[...] = res
        inv = lax.rsqrt(jnp.mean(res * res, axis=1, keepdims=True) + EPSILON)
        ffn_in = (res * inv * gf_ref[...]).astype(BF16)
        dispatch(keyr_ref[...], ffn_in, (xa_ref, xb_ref))


def attend(tokens, segr, keyr, w_qkv, w_o, ga, gf):
    toks, width = tokens.shape
    both = 2 * PAIR
    pair_cols = pl.BlockSpec((toks, both), lambda p: (0, p))
    heads = jax.ShapeDtypeStruct((toks, width), BF16)
    weights = [
        pl.BlockSpec((width, both), lambda p, part=part: (0, part * PAIRS // 2 + p))
        for part in range(3)
    ]
    return pl.pallas_call(
        attend_kernel,
        grid=(PAIRS // 2,),
        in_specs=[
            whole((toks, width)),
            whole((1, toks)),
            whole((1, toks)),
            *weights,
            whole((width, width)),
            whole((1, width)),
            whole((1, width)),
        ],
        out_specs=[
            pair_cols,
            pair_cols,
            pair_cols,
            pl.BlockSpec((2, 2, toks), lambda p: (p, 0, 0)),
            pl.BlockSpec((both, toks), lambda p: (p, 0)),
            whole((toks, width)),
            whole((toks, width)),
            whole((toks, width)),
            whole((toks, width)),
        ],
        out_shape=[
            heads,
            heads,
            heads,
            jax.ShapeDtypeStruct((PAIRS, 2, toks), F32),
            jax.ShapeDtypeStruct((width, toks), BF16),
            heads,
            jax.ShapeDtypeStruct((toks, width), F32),
            heads,
            heads,
        ],
        scratch_shapes=[
            pltpu.VMEM((toks // QB, QB, 3 * QB), F32),
            pltpu.VMEM((toks, width), BF16),
        ],
        compiler_params=params(),
        cost_estimate=cost(42),
        name="attend",
    )(tokens, segr, keyr, w_qkv, w_qkv, w_qkv, w_o, ga, gf)


def attend_back_kernel(
    core_ref,
    segr_ref,
    q_ref,
    k_ref,
    v_ref,
    lse_ref,
    mixt_ref,
    gb_ref,
    attnt_ref,
    wo_ref,
    send_ref,
    keep_ref,
    gqkv_ref,
    bias_ref,
    dqt_ref,
    dk_ref,
    dv_ref,
    do_ref,
):
    toks, width = gb_ref.shape
    both = q_ref.shape[1]
    count = toks // QB
    scale = HEAD**-0.5
    fill_bias(bias_ref, segr_ref[...], count)
    gb = gb_ref[...]
    grad_out = mm(gb, wo_ref[...], NT)
    do_ref[...] = grad_out.astype(BF16)
    mixt = mixt_ref[...]
    gwo = mm(mixt, gb).astype(BF16)
    weighted = grad_out.astype(BF16).astype(F32).T * mixt.astype(F32)
    delta = [
        jnp.sum(weighted[h * HEAD : (h + 1) * HEAD], axis=0, keepdims=True)
        for h in range(both // HEAD)
    ]
    kt = k_ref[...].astype(F32).T.astype(BF16)
    dk_ref[...] = jnp.zeros_like(dk_ref)
    dv_ref[...] = jnp.zeros_like(dv_ref)
    for i in range(count):
        low, high = band(i)
        cols = slice(i * QB, (i + 1) * QB)
        for pair in range(both // PAIR):
            lanes = slice(pair * PAIR, (pair + 1) * PAIR)
            q = q_ref[cols, lanes] * scale
            do = do_ref[cols, lanes]
            keys = k_ref[low:high, lanes]
            values = v_ref[low:high, lanes]
            dk_add, dv_add = [], []
            for h in range(2):
                head = slice((2 * pair + h) * HEAD, (2 * pair + h + 1) * HEAD)
                qm, dom = head_mask(q, h), head_mask(do, h)
                s = mm(keys, qm, NT) + bias_ref[i, : high - low, :]
                pr = jnp.exp(s - lse_ref[pair, h : h + 1, cols])
                dpr = mm(values, dom, NT)
                ds = (pr * (dpr - delta[2 * pair + h][:, cols])).astype(BF16)
                dv_add.append(mm(pr.astype(BF16), dom))
                dk_add.append(mm(ds, qm))
                dqt_ref[head, cols] = mm(kt[head, low:high], ds) * scale
            dk_ref[low:high, lanes] += dk_add[0] + dk_add[1]
            dv_ref[low:high, lanes] += dv_add[0] + dv_add[1]
    grads = [
        dqt_ref[...].T.astype(BF16),
        dk_ref[...].astype(BF16),
        dv_ref[...].astype(BF16),
    ]
    for part in range(3):
        gqkv_ref[part] = grads[part]
    gw = mm(attnt_ref[...], jnp.concatenate(grads, axis=1)).astype(BF16)
    for core in range(2):

        @pl.when(core_ref[0] == core)
        def _(core=core):
            for pair, ref in ((1 - core, send_ref), (core, keep_ref)):
                for part in range(3):
                    at = part * both + pair * PAIR
                    ref[part] = gw[:, at : at + PAIR]
                for j in range(width // PAIR):
                    ref[3, j * PAIR : (j + 1) * PAIR, :] = gwo[
                        pair * PAIR : (pair + 1) * PAIR, j * PAIR : (j + 1) * PAIR
                    ]


def attend_back(turn, core, segr, q, k, v, lse, mixt, gb, attnt, w_o):
    toks, width = gb.shape
    both = 2 * PAIR
    pair_cols = pl.BlockSpec((toks, both), lambda p: (0, turn))
    gw_shape = jax.ShapeDtypeStruct((4, width, PAIR), BF16)
    return pl.pallas_call(
        attend_back_kernel,
        grid=(1,),
        in_specs=[
            smem(),
            whole((1, toks)),
            pair_cols,
            pair_cols,
            pair_cols,
            pl.BlockSpec((2, 2, toks), lambda p: (turn, 0, 0)),
            pl.BlockSpec((both, toks), lambda p: (turn, 0)),
            whole((toks, width)),
            whole((width, toks)),
            pl.BlockSpec((both, width), lambda p: (turn, 0)),
        ],
        out_specs=[whole((4, width, PAIR)), whole((4, width, PAIR)), whole((3, toks, both))],
        out_shape=[gw_shape, gw_shape, jax.ShapeDtypeStruct((3, toks, both), BF16)],
        scratch_shapes=[
            pltpu.VMEM((toks // QB, 3 * QB, QB), F32),
            pltpu.VMEM((both, toks), F32),
            pltpu.VMEM((toks, both), F32),
            pltpu.VMEM((toks, both), F32),
            pltpu.VMEM((toks, both), BF16),
        ],
        compiler_params=params(),
        cost_estimate=cost(10 if turn + 1 == PAIRS // 2 else 2),
        name="attend_back",
    )(core, segr, q, k, v, lse, mixt, gb, attnt, w_o)


def grad_tokens_kernel(tok_ref, gres_ref, ga_ref, w_ref, *rest):
    *g_refs, out_ref = rest
    grads = [ref[part] for part in range(3) for ref in g_refs]
    dy = mm(jnp.concatenate(grads, axis=1), w_ref[...], NT)
    dx, _ = norm_back(tok_ref[...].astype(F32), ga_ref[...], dy)
    out_ref[...] = gres_ref[...] + dx


def grad_tokens_of(tokens, gres, ga, w_qkv, grads):
    toks, width = tokens.shape
    rows = 2 * QB
    tile = pl.BlockSpec((rows, width), lambda i: (i, 0))
    return pl.pallas_call(
        grad_tokens_kernel,
        grid=(toks // rows,),
        in_specs=[tile, tile, whole((1, width)), whole(w_qkv.shape)]
        + [pl.BlockSpec((3, rows, 2 * PAIR), lambda i: (0, i, 0))] * len(grads),
        out_specs=tile,
        out_shape=jax.ShapeDtypeStruct((toks, width), F32),
        compiler_params=params(),
        cost_estimate=cost(9),
        name="grad_tokens",
    )(tokens, gres, ga, w_qkv, *grads)


def unit_scale(values, axis):
    total = jnp.sum(values * values, axis=axis, keepdims=True)
    return lax.rsqrt(jnp.maximum(total, NORM_FLOOR)), total


def unit_back(values, inv, total, grad, axis):
    passed = jnp.where(total > NORM_FLOOR, 1.0, jnp.where(total == NORM_FLOOR, 0.5, 0.0))
    inner = jnp.sum(grad * values, axis=axis, keepdims=True)
    return inv * grad - passed * inv * inv * inv * inner * values


def gelu_and_slope(h):
    cdf = 0.5 + 0.5 * lax.erf(h * 0.7071067811865476)
    pdf = 0.3989422804014327 * jnp.exp(-0.5 * h * h)
    return h * cdf, cdf + h * pdf


def route(me, x, wrt, emb):
    z = mm(wrt, x, NT)
    inv, total = unit_scale(z, 0)
    zn = z * inv
    en = emb * unit_scale(emb, 1)[0]
    logits = mm(en, zn, NN, HIGHEST) / ROUTER_WARMTH
    w = jnp.exp(logits - jnp.max(logits, axis=0, keepdims=True))
    chances = w / jnp.sum(w, axis=0, keepdims=True)
    mine = jnp.where(lax.broadcasted_iota(I32, logits.shape, 0) == me, 1.0, 0.0)
    return z, inv, total, zn, en, chances, mine


def expert_kernel(
    me_ref,
    wrt_ref,
    emb_ref,
    x_ref,
    win_ref,
    ga_ref,
    act_ref,
    gp_ref,
    xt_ref,
    gout_ref,
    gwrt_ref,
    gemb_ref,
    w_s,
    gp_s,
    acc_s,
    gate_s,
):
    c = pl.program_id(0)
    rows, width = x_ref.shape
    me = me_ref[0]

    @pl.when(c == 0)
    def _():
        chances, mine = route(me, x_ref[...], wrt_ref[...], emb_ref[...])[-2:]
        gate = column_of(jnp.sum(chances * mine, axis=0, keepdims=True))
        gate_s[...] = jnp.broadcast_to(gate, (rows, LANES))
        acc_s[...] = jnp.zeros_like(acc_s)
        for r in range(0, rows, QB):
            xt_ref[:, r : r + QB] = x_ref[r : r + QB, :].T

    w_in = win_ref[0]
    wide = w_in.shape[1]
    chunk = pl.ds(pl.multiple_of(c * wide, LANES), wide)
    w_s[:, chunk] = w_in
    step = min(2 * QB, rows)
    for r in range(0, rows, step):
        part = slice(r, r + step)
        h = mm(x_ref[part, :], w_in)
        act, slope = gelu_and_slope(h)
        gate = jnp.concatenate([gate_s[part, :]] * (wide // LANES), axis=1)
        ga = ga_ref[part, :].astype(F32)
        act = act * gate
        act_ref[part, :] = act.astype(BF16)
        gp = (ga * (slope * gate)).astype(BF16)
        gp_s[part, chunk] = gp
        gp_ref[part, :] = gp
        prod = act * ga
        folded = prod[:, :LANES]
        for j in range(LANES, wide, LANES):
            folded = folded + prod[:, j : j + LANES]
        acc_s[part, :] += folded

    @pl.when(c == pl.num_programs(0) - 1)
    def _():
        x, wrt, emb = x_ref[...], wrt_ref[...], emb_ref[...]
        z, inv, total, zn, en, chances, mine = route(me, x, wrt, emb)
        weight = jnp.sum(acc_s[...].T, axis=0, keepdims=True)
        dl = weight * (mine - chances) / ROUTER_WARMTH
        gen = mm(dl, zn, NT, HIGHEST)
        dz = unit_back(z, inv, total, mm(en, dl, TN, HIGHEST), 0)
        dz_top = dz.astype(BF16)
        dz_low = (dz - dz_top.astype(F32)).astype(BF16)
        gwrt_ref[...] = mm(dz_top, x) + mm(dz_low, x)
        einv, etotal = unit_scale(emb, 1)
        gemb_ref[...] = unit_back(emb, einv, etotal, gen, 1)
        dz_top, dz_low = dz_top.astype(F32).T.astype(BF16), dz_low.astype(F32).T.astype(BF16)
        for r in range(0, rows, step):
            part = slice(r, r + step)
            back = mm(gp_s[part, :], w_s[...], NT).astype(BF16).astype(F32)
            back = back + mm(dz_top[part], wrt) + mm(dz_low[part], wrt)
            gout_ref[part, :] = back.astype(BF16)


def expert(me, wrt, emb, x, w_in, ga, wide):
    rows, width = x.shape
    hidden = w_in.shape[2]
    cols = pl.BlockSpec((rows, wide), lambda c: (0, c))
    hid = jax.ShapeDtypeStruct((rows, hidden), BF16)
    return pl.pallas_call(
        expert_kernel,
        grid=(hidden // wide,),
        in_specs=[
            smem(),
            whole(wrt.shape),
            whole(emb.shape),
            whole((rows, width)),
            pl.BlockSpec((1, width, wide), lambda c: (0, 0, c)),
            cols,
        ],
        out_specs=[
            cols,
            cols,
            whole((width, rows)),
            whole((rows, width)),
            whole(wrt.shape),
            whole(emb.shape),
        ],
        out_shape=[
            hid,
            hid,
            jax.ShapeDtypeStruct((width, rows), BF16),
            jax.ShapeDtypeStruct((rows, width), BF16),
            jax.ShapeDtypeStruct(wrt.shape, F32),
            jax.ShapeDtypeStruct(emb.shape, F32),
        ],
        scratch_shapes=[
            pltpu.VMEM((width, hidden), BF16),
            pltpu.VMEM((rows, hidden), BF16),
            pltpu.VMEM((rows, LANES), F32),
            pltpu.VMEM((rows, LANES), F32),
        ],
        compiler_params=params(),
        cost_estimate=cost(23),
        name="expert",
    )(me, wrt, emb, x, w_in, ga)


def early_grads_kernel(
    gta_ref, gtb_ref, xta_ref, xtb_ref, acta_ref, actb_ref, gpa_ref, gpb_ref, out_ref, gt_s, xt_s
):
    rows = gta_ref.shape[1]
    width = gta_ref.shape[0]

    @pl.when(pl.program_id(0) == 0)
    def _():
        gt_s[:, :rows] = gta_ref[...]
        gt_s[:, rows:] = gtb_ref[...]
        xt_s[:, :rows] = xta_ref[...]
        xt_s[:, rows:] = xtb_ref[...]

    act = jnp.concatenate([acta_ref[...], actb_ref[...]], axis=0)
    out_ref[0, :width] = mm(gt_s[...], act).astype(BF16)
    gp = jnp.concatenate([gpa_ref[...], gpb_ref[...]], axis=0)
    out_ref[0, width:] = mm(xt_s[...], gp).astype(BF16)


def early_grads(gts, xts, acts, gps, wide):
    width, rows = gts[0].shape
    third = width // 3
    steps = acts[0].shape[1] // wide
    return pl.pallas_call(
        early_grads_kernel,
        grid=(steps,),
        in_specs=[whole((width, rows))] * 2
        + [whole((third, rows))] * 2
        + [pl.BlockSpec((rows, wide), lambda c: (0, c))] * 4,
        out_specs=pl.BlockSpec((1, width + third, wide), lambda c: (c, 0, 0)),
        out_shape=jax.ShapeDtypeStruct((steps, width + third, wide), BF16),
        scratch_shapes=[
            pltpu.VMEM((width, 2 * rows), BF16),
            pltpu.VMEM((third, 2 * rows), BF16),
        ],
        compiler_params=params(),
        cost_estimate=cost(10),
        name="early_grads",
    )(*gts, *xts, *acts, *gps)


def late_grads_kernel(xta_ref, xtb_ref, gpa_ref, gpb_ref, out_ref, xt_s):
    width, rows = xta_ref.shape
    third = width // 3

    @pl.when(pl.program_id(0) == 0)
    def _():
        xt_s[:, :rows] = xta_ref[third:, :]
        xt_s[:, rows:] = xtb_ref[third:, :]

    gp = jnp.concatenate([gpa_ref[...], gpb_ref[...]], axis=0)
    out_ref[0] = mm(xt_s[...], gp).astype(BF16)


def late_grads(xts, gps, wide):
    width, rows = xts[0].shape
    left = width - width // 3
    steps = gps[0].shape[1] // wide
    return pl.pallas_call(
        late_grads_kernel,
        grid=(steps,),
        in_specs=[whole((width, rows))] * 2 + [pl.BlockSpec((rows, wide), lambda c: (0, c))] * 2,
        out_specs=pl.BlockSpec((1, left, wide), lambda c: (c, 0, 0)),
        out_shape=jax.ShapeDtypeStruct((steps, left, wide), BF16),
        scratch_shapes=[pltpu.VMEM((left, 2 * rows), BF16)],
        compiler_params=params(),
        cost_estimate=cost(10),
        name="late_grads",
    )(*xts, *gps)


def grad_act_kernel(g_ref, wout_ref, out_ref, gt_ref):
    g = g_ref[...].reshape(out_ref.shape[0], g_ref.shape[-1])

    @pl.when(pl.program_id(0) == 0)
    def _():
        gt_ref[...] = g.T

    out_ref[...] = mm(g, wout_ref[0], NT).astype(BF16)


def grad_act(g, half, w_out, wide):
    peers, _, slots, width = g.shape
    rows = peers * slots
    hidden = w_out.shape[1]
    return pl.pallas_call(
        grad_act_kernel,
        grid=(hidden // wide,),
        in_specs=[
            pl.BlockSpec((peers, 1, slots, width), lambda c: (0, half, 0, 0)),
            pl.BlockSpec((1, wide, width), lambda c: (0, c, 0)),
        ],
        out_specs=[pl.BlockSpec((rows, wide), lambda c: (0, c)), whole((width, rows))],
        out_shape=[
            jax.ShapeDtypeStruct((rows, hidden), BF16),
            jax.ShapeDtypeStruct((width, rows), BF16),
        ],
        compiler_params=params(),
        cost_estimate=cost(7),
        name="grad_act",
    )(g, w_out)


def expert_out_kernel(acta_ref, actb_ref, wout_ref, out_ref, acc_ref):
    c = pl.program_id(0)
    rows = acta_ref.shape[0]
    peers, _, slots, width = out_ref.shape

    @pl.when(c == 0)
    def _():
        acc_ref[...] = jnp.zeros_like(acc_ref)

    w_out = wout_ref[0]
    acc_ref[:rows, :] += mm(acta_ref[...], w_out)
    acc_ref[rows:, :] += mm(actb_ref[...], w_out)

    @pl.when(c == pl.num_programs(0) - 1)
    def _():
        for h in range(2):
            part = acc_ref[h * rows : (h + 1) * rows, :].astype(BF16)
            out_ref[:, h] = part.reshape(peers, slots, width)


def expert_out_of(acta, actb, w_out, wide, peers):
    rows, hidden = acta.shape
    width = w_out.shape[2]
    shape = (peers, 2, rows // peers, width)
    cols = pl.BlockSpec((rows, wide), lambda c: (0, c))
    return pl.pallas_call(
        expert_out_kernel,
        grid=(hidden // wide,),
        in_specs=[cols, cols, pl.BlockSpec((1, wide, width), lambda c: (0, c, 0))],
        out_specs=whole(shape),
        out_shape=jax.ShapeDtypeStruct(shape, BF16),
        scratch_shapes=[pltpu.VMEM((2 * rows, width), F32)],
        compiler_params=params(),
        cost_estimate=cost(14),
        name="expert_out",
    )(acta, actb, w_out)


def expert_sums_kernel(early_ref, late_ref, win_ref, wout_ref):
    width = wout_ref.shape[2]
    third = width // 3
    win_ref[0, :third] = early_ref[width:].astype(F32)
    win_ref[0, third:] = late_ref[...].astype(F32)
    wout_ref[0] = early_ref[:width].astype(F32).T


def expert_sums(early, late):
    share = early.shape[1]
    width = early.shape[0] * 3 // 4
    return pl.pallas_call(
        expert_sums_kernel,
        grid=(share // LANES,),
        in_specs=[
            pl.BlockSpec((early.shape[0], LANES), lambda k: (0, k)),
            pl.BlockSpec((late.shape[0], LANES), lambda k: (0, k)),
        ],
        out_specs=[
            pl.BlockSpec((1, width, LANES), lambda k: (0, 0, k)),
            pl.BlockSpec((1, LANES, width), lambda k: (0, k, 0)),
        ],
        out_shape=[
            jax.ShapeDtypeStruct((1, width, share), F32),
            jax.ShapeDtypeStruct((1, share, width), F32),
        ],
        compiler_params=params(),
        cost_estimate=cost(3),
        name="expert_sums",
    )(early, late)


def gather_rows(key_row, row_refs):
    keys = column_of(key_row)
    total, at = None, 0
    for ref in row_refs:
        column = lax.broadcasted_iota(I32, (keys.shape[0], ref.shape[0]), 1) + at
        part = mm(ones_where(keys == column), ref[...])
        total = part if total is None else total + part
        at += ref.shape[0]
    return total


def combine_back_kernel(
    keyr_ref, res_ref, cot_ref, gf_ref, ra_ref, rb_ref, gres_ref, gb_ref, gain_ref
):
    dy = gather_rows(keyr_ref[...], (ra_ref, rb_ref))

    @pl.when(pl.program_id(0) == 0)
    def _():
        gain_ref[...] = jnp.zeros_like(gain_ref)

    dx, dgain = norm_back(res_ref[...], gf_ref[...], dy)
    gain_ref[...] += dgain
    grad = cot_ref[...].astype(F32) + dx
    gres_ref[...] = grad
    gb_ref[...] = grad.astype(BF16)


def combine_back(keyr, res, cot, gf, rows):
    toks, width = res.shape
    tile = pl.BlockSpec((QB, width), lambda i: (i, 0))
    return pl.pallas_call(
        combine_back_kernel,
        grid=(toks // QB,),
        in_specs=[
            pl.BlockSpec((1, QB), lambda i: (0, i)),
            tile,
            tile,
            whole((1, width)),
            *[whole(r.shape) for r in rows],
        ],
        out_specs=[tile, tile, whole((1, width))],
        out_shape=[
            jax.ShapeDtypeStruct((toks, width), F32),
            jax.ShapeDtypeStruct((toks, width), BF16),
            jax.ShapeDtypeStruct((1, width), F32),
        ],
        compiler_params=params(),
        cost_estimate=cost(100),
        name="combine_back",
    )(keyr, res, cot, gf, *rows)


def combine_kernel(keyn_ref, res_ref, rows_ref, out_ref):
    out_ref[...] = (res_ref[...] + gather_rows(keyn_ref[...], (rows_ref,))).astype(BF16)


def combine(keyn, res, rows):
    toks, width = res.shape
    tile = pl.BlockSpec((QB, width), lambda i: (i, 0))
    return pl.pallas_call(
        combine_kernel,
        grid=(toks // QB,),
        in_specs=[
            pl.BlockSpec((1, QB), lambda i: (0, i)),
            tile,
            whole(rows.shape),
        ],
        out_specs=tile,
        out_shape=jax.ShapeDtypeStruct((toks, width), BF16),
        compiler_params=params(),
        cost_estimate=cost(5),
        name="combine",
    )(keyn, res, rows)


def shared_sums_kernel(count, experts, rows, extra, me_ref, w_ref, ga_ref, *rest):
    blocks, rest = rest[: 2 * count], rest[2 * count :]
    qkv_ref, o_ref, gain_ref, gain_ffn_ref, router_ref, embed_ref = rest[:6]
    held, small_s, sems = rest[6:]
    i = pl.program_id(0)
    width = o_ref.shape[1]
    chip, core = me_ref[0] >> 1, me_ref[0] & 1
    grain = math.gcd(rows, PAIR)

    @pl.when(i == 0)
    def _():
        copies = []
        for n, ref in enumerate(blocks):
            side = core if n < count else 1 - core
            copies.append(
                pltpu.make_async_copy(ref, held.at[side, (n % count) ^ chip], sems.at[n])
            )
        for copy in copies:
            copy.start()
        for copy in copies:
            copy.wait()

    def piece(side, two, row):
        base = two * rows + (two // 2) * extra
        pieces = []
        for t in range(0, PAIR, grain):
            at = pl.multiple_of(base + (row + t) % rows, math.gcd(grain, extra))
            pieces.append(held[side, (row + t) // rows, pl.ds(at, grain), :])
        return jnp.concatenate(pieces, axis=0).astype(F32)

    for pair in range(PAIRS):
        for part in range(3):
            at = (part * PAIRS + pair) * PAIR
            qkv_ref[:, at : at + PAIR] = piece(pair % 2, pair // 2, part * width + i * PAIR)
    for two in range(PAIRS // 2):

        @pl.when(i // 2 == two)
        def _(two=two):
            for j in range(width // PAIR):
                o_ref[:, j * PAIR : (j + 1) * PAIR] = piece(i % 2, two, 3 * width + j * PAIR)

    folded = jnp.zeros((PAIR, LANES), F32)
    for at in range(0, qkv_ref.shape[1], LANES):
        folded += qkv_ref[:, at : at + LANES] * w_ref[:, at : at + LANES].astype(F32)
    gain = jnp.sum(folded.T, axis=0, keepdims=True) / ga_ref[...]
    gain_ref[pl.ds(pl.multiple_of(i * PAIR, PAIR), PAIR)] = gain[0]

    @pl.when(i == 0)
    def _():
        for t in range(count):
            part = slice(2 * rows, 2 * rows + extra)
            small_s[t * extra : (t + 1) * extra, :] = held[0, t, part, :].astype(F32)
        rdim = router_ref.shape[0]
        for j in range(width // LANES):
            lanes = slice(j * LANES, (j + 1) * LANES)
            gain_ffn_ref[lanes] = small_s[j, :]
            at = 8 + j * rdim
            router_ref[:, lanes] = small_s[at : at + rdim, :]
        at = 8 + width // LANES * rdim
        embed_ref[...] = small_s[at : at + experts, :rdim]


def shared_sums(me, blocks, rows, extra, w_qkv, ga, experts, rdim):
    width = w_qkv.shape[0]
    count = len(blocks) // 2
    lanes = pl.BlockSpec((1, PAIR), lambda i: (0, i))
    return pl.pallas_call(
        functools.partial(shared_sums_kernel, count, experts, rows, extra),
        grid=(width // PAIR,),
        in_specs=[smem(), pl.BlockSpec((PAIR, 3 * width), lambda i: (i, 0)), lanes]
        + [pl.BlockSpec(memory_space=pl.ANY)] * (2 * count),
        out_specs=[
            pl.BlockSpec((PAIR, 3 * width), lambda i: (i, 0)),
            pl.BlockSpec((PAIR, width), lambda i: (i, 0)),
            pl.BlockSpec((width,), lambda i: (0,)),
            pl.BlockSpec((width,), lambda i: (0,)),
            whole((rdim, width)),
            whole((experts, rdim)),
        ],
        out_shape=[
            jax.ShapeDtypeStruct((width, 3 * width), F32),
            jax.ShapeDtypeStruct((width, width), F32),
            jax.ShapeDtypeStruct((width,), F32),
            jax.ShapeDtypeStruct((width,), F32),
            jax.ShapeDtypeStruct((rdim, width), F32),
            jax.ShapeDtypeStruct((experts, rdim), F32),
        ],
        scratch_shapes=[
            pltpu.VMEM((2, count, *blocks[0].shape), BF16),
            pltpu.VMEM((count * extra, LANES), F32),
            pltpu.SemaphoreType.DMA((2 * count,)),
        ],
        compiler_params=params(),
        cost_estimate=cost(2),
        name="shared_sums",
    )(me, w_qkv, ga, *blocks)


def exchange(rows):
    peers = lax.axis_size("expert")
    width = rows.shape[1]
    out = lax.all_to_all(
        rows.reshape(peers, -1, width), "expert", split_axis=0, concat_axis=0, tiled=True
    )
    return out.reshape(-1, width)


def core_groups():
    return [[core + 2 * chip for chip in range(lax.axis_size("expert") // 2)] for core in range(2)]


def swap_cores(value):
    peers = lax.axis_size("expert")
    return lax.ppermute(value, "expert", [(j, j ^ 1) for j in range(peers)])


def sum_blocks(blocks):
    return jnp.sum(blocks.astype(F32), axis=0).astype(BF16)


def sum_over_chips(blocks):
    return sum_blocks(
        lax.all_to_all(blocks, "expert", 0, 0, axis_index_groups=core_groups(), tiled=True)
    )


def xor_permute(value, axis, d):
    return lax.ppermute(value, axis, [(j, j ^ d) for j in range(lax.axis_size(axis))])


def sum_over_dp(share):
    groups = lax.axis_size("dp")
    me = lax.axis_index("dp")
    blocks = share.reshape(groups, share.shape[0] // groups, -1)
    total = lax.dynamic_index_in_dim(blocks, me, 0, keepdims=False).astype(F32)
    for d in range(1, groups):
        send = lax.dynamic_index_in_dim(blocks, me ^ d, 0, keepdims=False)
        total = total + xor_permute(send, "dp", d).astype(F32)
    return total.astype(BF16)


def gather_over_dp(part):
    groups = lax.axis_size("dp")
    me = lax.axis_index("dp")
    parts = [part] + [xor_permute(part, "dp", d) for d in range(1, groups)]
    parts = jnp.stack(parts)
    for bit in range((groups - 1).bit_length()):
        split = parts.reshape(-1, 2, 1 << bit, *part.shape)
        parts = jnp.where((me >> bit) & 1 == 1, split[:, ::-1], split)
    return parts.reshape(-1, part.shape[1])


def on_device(
    tokens,
    segments,
    routes,
    cotangent,
    w_qkv,
    w_attn_out,
    gain_attn,
    gain_ffn,
    w_router,
    embed,
    w_in,
    w_out,
):
    toks, width = tokens.shape
    experts, rdim = embed.shape
    peers = lax.axis_size("expert")
    shards = lax.axis_size("dp")
    chips = peers // 2
    share = w_in.shape[2] // shards
    me = lax.axis_index("expert").astype(I32).reshape(1)
    core = me & 1
    ga, gf = gain_attn.reshape(1, width), gain_ffn.reshape(1, width)
    segr = segments.reshape(1, toks)
    wrt = w_router.T
    hold = lax.optimization_barrier

    keyr, keyn, g_slots = place(routes.reshape(1, toks), cotangent, peers, 2 * toks)
    g_rows = exchange(g_slots).reshape(peers, 2, toks // peers, width)
    q, k, v, lse, mixt, attn_in, res, xa_slots, xb_slots = attend(
        tokens, segr, keyr, w_qkv, w_attn_out, ga, gf
    )
    x_a = exchange(xa_slots)
    gact_a, gt_a = grad_act(g_rows, 0, w_out, share)
    gact_b, gt_b = grad_act(g_rows, 1, w_out, share)
    x_a, xb_slots, gact_b, gt_b, attn_in = hold((x_a, xb_slots, gact_b, gt_b, attn_in))
    x_b = exchange(xb_slots)
    act_a, gp_a, xt_a, gout_a, gwr_a, gemb_a = expert(me, wrt, embed, x_a, w_in, gact_a, share)
    gback_a = exchange(gout_a)
    act_b, gp_b, xt_b, gout_b, gwr_b, gemb_b = expert(me, wrt, embed, x_b, w_in, gact_b, share)
    gout_b, gback_a = hold((gout_b, gback_a))
    gback_b = exchange(gout_b)
    early = early_grads((gt_a, gt_b), (xt_a, xt_b), (act_a, act_b), (gp_a, gp_b), share)
    early_sum = lax.psum_scatter(early, "dp", scatter_dimension=0, tiled=True)[0]
    attnt = attn_in.T
    gback_b, early, attnt = hold((gback_b, early, attnt))
    gres, gb, ggf = combine_back(keyr, res, cotangent, gf, (gback_a, gback_b))

    small = jnp.concatenate(
        [
            jnp.pad(ggf.reshape(-1, LANES), ((0, 8 - width // LANES), (0, 0))),
            *jnp.split(gwr_a + gwr_b, width // LANES, axis=1),
            jnp.pad(gemb_a + gemb_b, ((0, 0), (0, LANES - rdim))),
        ],
        axis=0,
    )
    rows = 4 * width // chips
    extra = -(-small.shape[0] // (16 * chips)) * 16
    small = jnp.pad(small, ((0, chips * extra - small.shape[0]), (0, 0)))
    small = (small + swap_cores(small)).astype(BF16).reshape(chips, extra, LANES)
    both, grads = [], []
    for turn in range(PAIRS // 2):
        send, keep, grad = attend_back(
            turn, core, segr, q, k, v, lse, mixt, gb, attnt, w_attn_out
        )
        grads.append(grad)
        got = swap_cores(send)
        both.append((keep.astype(F32) + got.astype(F32)).astype(BF16).reshape(chips, -1, PAIR))
        if turn == 0:
            (gb, grad) = hold((gb, grad))
        elif turn == 1:
            gb, both, small, grad = hold((gb, both, small, grad))
            share_one = sum_over_chips(jnp.concatenate([*both, small], axis=1))
    last, late_act, share_one = hold((both[-1], act_b, share_one))
    share_two = sum_over_chips(last)
    fout = expert_out_of(act_a, late_act, w_out, share, peers)
    share_two, fout, late_gp, late_res = hold((share_two, fout, gp_b, gres))
    fback = exchange(fout.reshape(2 * toks, width))
    part = sum_over_dp(jnp.concatenate([share_one, share_two], axis=0))
    late = late_grads((xt_a, xt_b), (gp_a, late_gp), share)
    grad_tokens = grad_tokens_of(tokens, late_res, ga, w_qkv, grads)
    part, fback, late, grad_tokens, early_sum = hold(
        (part, fback, late, grad_tokens, early_sum)
    )
    total = gather_over_dp(part)
    late_sum = lax.psum_scatter(late, "dp", scatter_dimension=0, tiled=True)[0]
    pieces = [total] + [xor_permute(total, "expert", d) for d in range(2, peers, 2)]
    out_tokens = combine(keyn, res, fback)
    pieces, out_tokens = hold((pieces, out_tokens))
    blocks = pieces + [swap_cores(piece) for piece in pieces]
    grad_w_qkv, grad_w_attn_out, grad_gain_attn, grad_gain_ffn, grad_router, grad_embed = (
        shared_sums(me, blocks, rows, extra, w_qkv, ga, experts, rdim)
    )
    grad_w_qkv, late_sum = hold((grad_w_qkv, late_sum))
    grad_w_in, grad_w_out = expert_sums(early_sum, late_sum)
    return (
        out_tokens,
        grad_tokens,
        grad_w_qkv,
        grad_w_attn_out,
        grad_gain_attn,
        grad_gain_ffn,
        grad_router.T,
        grad_embed,
        grad_w_in,
        grad_w_out,
    )


def solution(mesh):
    rows = P(("dp", "expert"), None)
    return jax.shard_map(
        on_device,
        mesh=mesh,
        in_specs=(
            rows,
            rows,
            rows,
            rows,
            P(),
            P(),
            P(),
            P(),
            P(),
            P(),
            P("expert", None, None),
            P("expert", None, None),
        ),
        out_specs=(
            rows,
            rows,
            P(),
            P(),
            P(),
            P(),
            P(),
            P(),
            P("expert", None, "dp"),
            P("expert", "dp", None),
        ),
        check_vma=False,
    )
```

```python
import functools
import math

import jax
import jax.numpy as jnp
from jax import lax
from jax.experimental import pallas as pl
from jax.experimental.pallas import tpu as pltpu
from jax.sharding import PartitionSpec as P

HEADS = 12
HEAD = 64
PAIRS = HEADS // 2
PAIR = 2 * HEAD
QB = 256
LANES = 128
ROUTER_WARMTH = 0.3
NORM_FLOOR = 12.0
EPSILON = 1e-05
MASK_VALUE = -1e30
F32 = jnp.float32
BF16 = jnp.bfloat16
I32 = jnp.int32
NN = (((1,), (0,)), ((), ()))
NT = (((1,), (1,)), ((), ()))
TN = (((0,), (0,)), ((), ()))
HIGHEST = lax.Precision.HIGHEST
MIB = 1 << 20


def mm(a, b, dims=NN, precision=None):
    return lax.dot_general(a, b, dims, precision=precision, preferred_element_type=F32)


def params():
    return pltpu.CompilerParams(vmem_limit_bytes=62 * MIB)


def cost(micros, nbytes=0):
    return pl.CostEstimate(
        flops=int(micros * 1.15e9), bytes_accessed=int(nbytes), transcendentals=0
    )


def whole(shape):
    return pl.BlockSpec(
        shape, lambda *_: (0,) * len(shape), pipeline_mode=pl.Buffered(buffer_count=1)
    )


def smem():
    return pl.BlockSpec(memory_space=pltpu.SMEM)


def norm_back(x, gain, dy):
    inv = lax.rsqrt(jnp.mean(x * x, axis=1, keepdims=True) + EPSILON)
    dn = dy * gain
    dx = inv * dn - x * (inv * inv * inv * jnp.mean(x * dn, axis=1, keepdims=True))
    return dx, jnp.sum(dy * x * inv, axis=0, keepdims=True)


def column_of(row):
    return jnp.broadcast_to(row.astype(F32), (8, row.shape[1])).T[:, :1].astype(row.dtype)


def ones_where(mask):
    return jnp.where(mask, 1.0, 0.0).astype(BF16)


def dispatch(key_row, rows, out_refs):
    at = 0
    for ref in out_refs:
        step = min(2 * QB, ref.shape[0])
        for r in range(0, ref.shape[0], step):
            slot = lax.broadcasted_iota(I32, (step, key_row.shape[1]), 0) + at
            ref[r : r + step, :] = mm(ones_where(key_row == slot), rows).astype(BF16)
            at += step


def place_kernel(peers, rr_ref, cot_ref, keyr_ref, keyn_ref, g_ref):
    toks = cot_ref.shape[0]
    cap = g_ref.shape[0] // peers
    half = cap // 2
    rr = rr_ref[...]
    before = ones_where(
        lax.broadcasted_iota(I32, (toks, toks), 0) <= lax.broadcasted_iota(I32, (toks, toks), 1)
    )
    hot_row = jnp.where(lax.broadcasted_iota(I32, (peers, toks), 0) == rr, 1.0, 0.0)
    upto = mm(hot_row.astype(BF16), before)
    rank = (jnp.sum(hot_row * upto, axis=0, keepdims=True) - 1.0).astype(I32)
    keyr_ref[...] = rr * half + jnp.where(rank < half, rank, rank + (peers - 1) * half)
    keyn_ref[...] = rr * cap + rank
    dispatch(keyn_ref[...], cot_ref[...], (g_ref,))


def place(routes, cot, peers, slots):
    toks, width = cot.shape
    return pl.pallas_call(
        functools.partial(place_kernel, peers),
        out_shape=[
            jax.ShapeDtypeStruct((1, toks), I32),
            jax.ShapeDtypeStruct((1, toks), I32),
            jax.ShapeDtypeStruct((slots, width), BF16),
        ],
        in_specs=[pl.BlockSpec(memory_space=pltpu.VMEM)] * 2,
        compiler_params=params(),
        cost_estimate=cost(5),
        name="place",
    )(routes, cot)


def band(i):
    return max(0, i - 2) * QB, (i + 1) * QB


def fill_bias(bias_ref, segr, count):
    segc = column_of(segr)
    for i in range(count):
        low, high = band(i)
        keys = lax.broadcasted_iota(I32, (high - low, QB), 0) + low
        queries = lax.broadcasted_iota(I32, (high - low, QB), 1) + i * QB
        same = segc[low:high] == segr[:, i * QB : (i + 1) * QB]
        bias_ref[i, : high - low, :] = jnp.where((keys <= queries) & same, 0.0, MASK_VALUE)


def head_mask(values, h):
    lane = lax.broadcasted_iota(I32, values.shape, 1)
    return jnp.where((lane >= h * HEAD) & (lane < (h + 1) * HEAD), values, jnp.zeros_like(values))


def attend_kernel(
    tok_ref,
    segr_ref,
    keyr_ref,
    wq_ref,
    wk_ref,
    wv_ref,
    wo_ref,
    ga_ref,
    gf_ref,
    q_ref,
    k_ref,
    v_ref,
    lse_ref,
    mixt_ref,
    attn_ref,
    res_ref,
    xa_ref,
    xb_ref,
    bias_ref,
    mix_ref,
):
    p = pl.program_id(0)
    toks, width = tok_ref.shape
    count = toks // QB
    both = q_ref.shape[1]

    @pl.when(p == 0)
    def _():
        segr = segr_ref[...]
        segc = column_of(segr)
        for i in range(count):
            low, high = band(i)
            keys = lax.broadcasted_iota(I32, (QB, high - low), 1) + low
            queries = lax.broadcasted_iota(I32, (QB, high - low), 0) + i * QB
            same = segr[:, low:high] == segc[i * QB : (i + 1) * QB]
            bias_ref[i, :, : high - low] = jnp.where((keys <= queries) & same, 0.0, MASK_VALUE)
        x = tok_ref[...].astype(F32)
        inv = lax.rsqrt(jnp.mean(x * x, axis=1, keepdims=True) + EPSILON)
        attn_ref[...] = (x * inv * ga_ref[...].reshape(1, width)).astype(BF16)

    attn_in = attn_ref[...]
    q_ref[...] = mm(attn_in, wq_ref[...]).astype(BF16)
    k_ref[...] = mm(attn_in, wk_ref[...]).astype(BF16)
    v_ref[...] = mm(attn_in, wv_ref[...]).astype(BF16)
    lane = lax.broadcasted_iota(I32, (QB, PAIR), 1)
    for i in range(count):
        low, high = band(i)
        cols = slice(i * QB, (i + 1) * QB)
        for pair in range(both // PAIR):
            lanes = slice(pair * PAIR, (pair + 1) * PAIR)
            q = q_ref[cols, lanes] * HEAD**-0.5
            keys = k_ref[low:high, lanes]
            values = v_ref[low:high, lanes]
            parts, sums = [], []
            for h in range(2):
                s = mm(head_mask(q, h), keys, NT) + bias_ref[i, :, : high - low]
                top = jnp.max(s, axis=1, keepdims=True)
                w = jnp.exp(s - top)
                total = jnp.sum(w, axis=1, keepdims=True)
                sums.append(top + jnp.log(total))
                parts.append(mm((w * (1.0 / total)).astype(BF16), values))
            mixed = jnp.where(lane < HEAD, parts[0], parts[1])
            lse_ref[pair, :, cols] = jnp.where(lane == 0, sums[0], sums[1]).T[:2]
            mixt_ref[lanes, cols] = mixed.T.astype(BF16)
            at = pl.ds(pl.multiple_of(p * both + pair * PAIR, PAIR), PAIR)
            mix_ref[cols, at] = mixed.astype(BF16)

    @pl.when(p == pl.num_programs(0) - 1)
    def _():
        res = tok_ref[...].astype(F32) + mm(mix_ref[...], wo_ref[...])
        res_ref[...] = res
        inv = lax.rsqrt(jnp.mean(res * res, axis=1, keepdims=True) + EPSILON)
        ffn_in = (res * inv * gf_ref[...].reshape(1, width)).astype(BF16)
        dispatch(keyr_ref[...], ffn_in, (xa_ref, xb_ref))


def attend(tokens, segr, keyr, w_qkv, w_o, ga, gf):
    toks, width = tokens.shape
    both = 2 * PAIR
    pair_cols = pl.BlockSpec((toks, both), lambda p: (0, p))
    heads = jax.ShapeDtypeStruct((toks, width), BF16)
    weights = [
        pl.BlockSpec((width, both), lambda p, part=part: (0, part * PAIRS // 2 + p))
        for part in range(3)
    ]
    return pl.pallas_call(
        attend_kernel,
        grid=(PAIRS // 2,),
        in_specs=[
            whole((toks, width)),
            whole((1, toks)),
            whole((1, toks)),
            *weights,
            whole((width, width)),
            whole((width,)),
            whole((width,)),
        ],
        out_specs=[
            pair_cols,
            pair_cols,
            pair_cols,
            pl.BlockSpec((2, 2, toks), lambda p: (p, 0, 0)),
            pl.BlockSpec((both, toks), lambda p: (p, 0)),
            whole((toks, width)),
            whole((toks, width)),
            whole((toks, width)),
            whole((toks, width)),
        ],
        out_shape=[
            heads,
            heads,
            heads,
            jax.ShapeDtypeStruct((PAIRS, 2, toks), F32),
            jax.ShapeDtypeStruct((width, toks), BF16),
            heads,
            jax.ShapeDtypeStruct((toks, width), F32),
            heads,
            heads,
        ],
        scratch_shapes=[
            pltpu.VMEM((toks // QB, QB, 3 * QB), F32),
            pltpu.VMEM((toks, width), BF16),
        ],
        compiler_params=params(),
        cost_estimate=cost(42),
        name="attend",
    )(tokens, segr, keyr, w_qkv, w_qkv, w_qkv, w_o, ga, gf)


def attend_back_kernel(
    core_ref,
    segr_ref,
    q_ref,
    k_ref,
    v_ref,
    lse_ref,
    mixt_ref,
    gb_ref,
    attnt_ref,
    wo_ref,
    send_ref,
    keep_ref,
    gqkv_ref,
    bias_ref,
    dqt_ref,
    dk_ref,
    dv_ref,
    do_ref,
):
    toks, width = gb_ref.shape
    both = q_ref.shape[1]
    count = toks // QB
    scale = HEAD**-0.5
    fill_bias(bias_ref, segr_ref[...], count)
    gb = gb_ref[...]
    grad_out = mm(gb, wo_ref[...], NT)
    do_ref[...] = grad_out.astype(BF16)
    mixt = mixt_ref[...]
    gwo = mm(mixt, gb).astype(BF16)
    weighted = grad_out.astype(BF16).astype(F32).T * mixt.astype(F32)
    delta = [
        jnp.sum(weighted[h * HEAD : (h + 1) * HEAD], axis=0, keepdims=True)
        for h in range(both // HEAD)
    ]
    kt = k_ref[...].astype(F32).T.astype(BF16)
    dk_ref[...] = jnp.zeros_like(dk_ref)
    dv_ref[...] = jnp.zeros_like(dv_ref)
    for i in range(count):
        low, high = band(i)
        cols = slice(i * QB, (i + 1) * QB)
        for pair in range(both // PAIR):
            lanes = slice(pair * PAIR, (pair + 1) * PAIR)
            q = q_ref[cols, lanes] * scale
            do = do_ref[cols, lanes]
            keys = k_ref[low:high, lanes]
            values = v_ref[low:high, lanes]
            dk_add, dv_add = [], []
            for h in range(2):
                head = slice((2 * pair + h) * HEAD, (2 * pair + h + 1) * HEAD)
                qm, dom = head_mask(q, h), head_mask(do, h)
                s = mm(keys, qm, NT) + bias_ref[i, : high - low, :]
                pr = jnp.exp(s - lse_ref[pair, h : h + 1, cols])
                dpr = mm(values, dom, NT)
                ds = (pr * (dpr - delta[2 * pair + h][:, cols])).astype(BF16)
                dv_add.append(mm(pr.astype(BF16), dom))
                dk_add.append(mm(ds, qm))
                dqt_ref[head, cols] = mm(kt[head, low:high], ds) * scale
            dk_ref[low:high, lanes] += dk_add[0] + dk_add[1]
            dv_ref[low:high, lanes] += dv_add[0] + dv_add[1]
    grads = [
        dqt_ref[...].T.astype(BF16),
        dk_ref[...].astype(BF16),
        dv_ref[...].astype(BF16),
    ]
    for part in range(3):
        gqkv_ref[part] = grads[part]
    gw = mm(attnt_ref[...], jnp.concatenate(grads, axis=1)).astype(BF16)
    for core in range(2):

        @pl.when(core_ref[0] == core)
        def _(core=core):
            for pair, ref in ((1 - core, send_ref), (core, keep_ref)):
                for part in range(3):
                    at = part * both + pair * PAIR
                    ref[part] = gw[:, at : at + PAIR]
                for j in range(width // PAIR):
                    ref[3, j * PAIR : (j + 1) * PAIR, :] = gwo[
                        pair * PAIR : (pair + 1) * PAIR, j * PAIR : (j + 1) * PAIR
                    ]


def attend_back(turn, core, segr, q, k, v, lse, mixt, gb, attnt, w_o):
    toks, width = gb.shape
    both = 2 * PAIR
    pair_cols = pl.BlockSpec((toks, both), lambda p: (0, turn))
    gw_shape = jax.ShapeDtypeStruct((4, width, PAIR), BF16)
    return pl.pallas_call(
        attend_back_kernel,
        grid=(1,),
        in_specs=[
            smem(),
            whole((1, toks)),
            pair_cols,
            pair_cols,
            pair_cols,
            pl.BlockSpec((2, 2, toks), lambda p: (turn, 0, 0)),
            pl.BlockSpec((both, toks), lambda p: (turn, 0)),
            whole((toks, width)),
            whole((width, toks)),
            pl.BlockSpec((both, width), lambda p: (turn, 0)),
        ],
        out_specs=[whole((4, width, PAIR)), whole((4, width, PAIR)), whole((3, toks, both))],
        out_shape=[gw_shape, gw_shape, jax.ShapeDtypeStruct((3, toks, both), BF16)],
        scratch_shapes=[
            pltpu.VMEM((toks // QB, 3 * QB, QB), F32),
            pltpu.VMEM((both, toks), F32),
            pltpu.VMEM((toks, both), F32),
            pltpu.VMEM((toks, both), F32),
            pltpu.VMEM((toks, both), BF16),
        ],
        compiler_params=params(),
        cost_estimate=cost(10 if turn + 1 == PAIRS // 2 else 2),
        name="attend_back",
    )(core, segr, q, k, v, lse, mixt, gb, attnt, w_o)


def grad_tokens_kernel(tok_ref, gres_ref, ga_ref, w_ref, *rest):
    *g_refs, out_ref = rest
    grads = [ref[part] for part in range(3) for ref in g_refs]
    dy = mm(jnp.concatenate(grads, axis=1), w_ref[...], NT)
    dx, _ = norm_back(tok_ref[...].astype(F32), ga_ref[...].reshape(1, dy.shape[1]), dy)
    out_ref[...] = gres_ref[...] + dx


def grad_tokens_of(tokens, gres, ga, w_qkv, grads):
    toks, width = tokens.shape
    rows = 2 * QB
    tile = pl.BlockSpec((rows, width), lambda i: (i, 0))
    return pl.pallas_call(
        grad_tokens_kernel,
        grid=(toks // rows,),
        in_specs=[tile, tile, whole((width,)), whole(w_qkv.shape)]
        + [pl.BlockSpec((3, rows, 2 * PAIR), lambda i: (0, i, 0))] * len(grads),
        out_specs=tile,
        out_shape=jax.ShapeDtypeStruct((toks, width), F32),
        compiler_params=params(),
        cost_estimate=cost(9),
        name="grad_tokens",
    )(tokens, gres, ga, w_qkv, *grads)


def unit_scale(values, axis):
    total = jnp.sum(values * values, axis=axis, keepdims=True)
    return lax.rsqrt(jnp.maximum(total, NORM_FLOOR)), total


def unit_back(values, inv, total, grad, axis):
    passed = jnp.where(total > NORM_FLOOR, 1.0, jnp.where(total == NORM_FLOOR, 0.5, 0.0))
    inner = jnp.sum(grad * values, axis=axis, keepdims=True)
    return inv * grad - passed * inv * inv * inv * inner * values


def gelu_and_slope(h):
    cdf = 0.5 + 0.5 * lax.erf(h * 0.7071067811865476)
    pdf = 0.3989422804014327 * jnp.exp(-0.5 * h * h)
    return h * cdf, cdf + h * pdf


def route(me, x, wrt, emb):
    z = mm(wrt, x, NT)
    inv, total = unit_scale(z, 0)
    zn = z * inv
    en = emb * unit_scale(emb, 1)[0]
    logits = mm(en, zn, NN, HIGHEST) / ROUTER_WARMTH
    w = jnp.exp(logits - jnp.max(logits, axis=0, keepdims=True))
    chances = w / jnp.sum(w, axis=0, keepdims=True)
    mine = jnp.where(lax.broadcasted_iota(I32, logits.shape, 0) == me, 1.0, 0.0)
    return z, inv, total, zn, en, chances, mine


def expert_kernel(
    me_ref,
    wrt_ref,
    emb_ref,
    x_ref,
    win_ref,
    ga_ref,
    act_ref,
    gp_ref,
    xt_ref,
    gout_ref,
    gwrt_ref,
    gemb_ref,
    w_s,
    gp_s,
    acc_s,
    gate_s,
):
    c = pl.program_id(0)
    rows, width = x_ref.shape
    me = me_ref[0]

    @pl.when(c == 0)
    def _():
        chances, mine = route(me, x_ref[...], wrt_ref[...], emb_ref[...])[-2:]
        gate = column_of(jnp.sum(chances * mine, axis=0, keepdims=True))
        gate_s[...] = jnp.broadcast_to(gate, (rows, LANES))
        acc_s[...] = jnp.zeros_like(acc_s)
        for r in range(0, rows, QB):
            xt_ref[:, r : r + QB] = x_ref[r : r + QB, :].T

    w_in = win_ref[0]
    wide = w_in.shape[1]
    chunk = pl.ds(pl.multiple_of(c * wide, LANES), wide)
    w_s[:, chunk] = w_in
    step = min(2 * QB, rows)
    for r in range(0, rows, step):
        part = slice(r, r + step)
        h = mm(x_ref[part, :], w_in)
        act, slope = gelu_and_slope(h)
        gate = jnp.concatenate([gate_s[part, :]] * (wide // LANES), axis=1)
        ga = ga_ref[part, :].astype(F32)
        act = act * gate
        act_ref[part, :] = act.astype(BF16)
        gp = (ga * (slope * gate)).astype(BF16)
        gp_s[part, chunk] = gp
        gp_ref[part, :] = gp
        prod = act * ga
        folded = prod[:, :LANES]
        for j in range(LANES, wide, LANES):
            folded = folded + prod[:, j : j + LANES]
        acc_s[part, :] += folded

    @pl.when(c == pl.num_programs(0) - 1)
    def _():
        x, wrt, emb = x_ref[...], wrt_ref[...], emb_ref[...]
        z, inv, total, zn, en, chances, mine = route(me, x, wrt, emb)
        weight = jnp.sum(acc_s[...].T, axis=0, keepdims=True)
        dl = weight * (mine - chances) / ROUTER_WARMTH
        gen = mm(dl, zn, NT, HIGHEST)
        dz = unit_back(z, inv, total, mm(en, dl, TN, HIGHEST), 0)
        dz_top = dz.astype(BF16)
        dz_low = (dz - dz_top.astype(F32)).astype(BF16)
        gwrt_ref[...] = mm(dz_top, x) + mm(dz_low, x)
        einv, etotal = unit_scale(emb, 1)
        gemb_ref[...] = unit_back(emb, einv, etotal, gen, 1)
        dz_top, dz_low = dz_top.astype(F32).T.astype(BF16), dz_low.astype(F32).T.astype(BF16)
        for r in range(0, rows, step):
            part = slice(r, r + step)
            back = mm(gp_s[part, :], w_s[...], NT).astype(BF16).astype(F32)
            back = back + mm(dz_top[part], wrt) + mm(dz_low[part], wrt)
            gout_ref[part, :] = back.astype(BF16)


def expert(me, wrt, emb, x, w_in, ga, wide):
    rows, width = x.shape
    hidden = w_in.shape[2]
    cols = pl.BlockSpec((rows, wide), lambda c: (0, c))
    hid = jax.ShapeDtypeStruct((rows, hidden), BF16)
    return pl.pallas_call(
        expert_kernel,
        grid=(hidden // wide,),
        in_specs=[
            smem(),
            whole(wrt.shape),
            whole(emb.shape),
            whole((rows, width)),
            pl.BlockSpec((1, width, wide), lambda c: (0, 0, c)),
            cols,
        ],
        out_specs=[
            cols,
            cols,
            whole((width, rows)),
            whole((rows, width)),
            whole(wrt.shape),
            whole(emb.shape),
        ],
        out_shape=[
            hid,
            hid,
            jax.ShapeDtypeStruct((width, rows), BF16),
            jax.ShapeDtypeStruct((rows, width), BF16),
            jax.ShapeDtypeStruct(wrt.shape, F32),
            jax.ShapeDtypeStruct(emb.shape, F32),
        ],
        scratch_shapes=[
            pltpu.VMEM((width, hidden), BF16),
            pltpu.VMEM((rows, hidden), BF16),
            pltpu.VMEM((rows, LANES), F32),
            pltpu.VMEM((rows, LANES), F32),
        ],
        compiler_params=params(),
        cost_estimate=cost(23),
        name="expert",
    )(me, wrt, emb, x, w_in, ga)


def early_grads_kernel(
    gta_ref, gtb_ref, xta_ref, xtb_ref, acta_ref, actb_ref, gpa_ref, gpb_ref, out_ref, gt_s, xt_s
):
    rows = gta_ref.shape[1]
    width = gta_ref.shape[0]

    @pl.when(pl.program_id(0) == 0)
    def _():
        gt_s[:, :rows] = gta_ref[...]
        gt_s[:, rows:] = gtb_ref[...]
        xt_s[:, :rows] = xta_ref[...]
        xt_s[:, rows:] = xtb_ref[...]

    act = jnp.concatenate([acta_ref[...], actb_ref[...]], axis=0)
    out_ref[0, :width] = mm(gt_s[...], act).astype(BF16)
    gp = jnp.concatenate([gpa_ref[...], gpb_ref[...]], axis=0)
    out_ref[0, width:] = mm(xt_s[...], gp).astype(BF16)


def early_grads(gts, xts, acts, gps, wide):
    width, rows = gts[0].shape
    third = width // 3
    steps = acts[0].shape[1] // wide
    return pl.pallas_call(
        early_grads_kernel,
        grid=(steps,),
        in_specs=[whole((width, rows))] * 2
        + [whole((third, rows))] * 2
        + [pl.BlockSpec((rows, wide), lambda c: (0, c))] * 4,
        out_specs=pl.BlockSpec((1, width + third, wide), lambda c: (c, 0, 0)),
        out_shape=jax.ShapeDtypeStruct((steps, width + third, wide), BF16),
        scratch_shapes=[
            pltpu.VMEM((width, 2 * rows), BF16),
            pltpu.VMEM((third, 2 * rows), BF16),
        ],
        compiler_params=params(),
        cost_estimate=cost(10),
        name="early_grads",
    )(*gts, *xts, *acts, *gps)


def late_grads_kernel(xta_ref, xtb_ref, gpa_ref, gpb_ref, out_ref, xt_s):
    width, rows = xta_ref.shape
    third = width // 3

    @pl.when(pl.program_id(0) == 0)
    def _():
        xt_s[:, :rows] = xta_ref[third:, :]
        xt_s[:, rows:] = xtb_ref[third:, :]

    gp = jnp.concatenate([gpa_ref[...], gpb_ref[...]], axis=0)
    out_ref[0] = mm(xt_s[...], gp).astype(BF16)


def late_grads(xts, gps, wide):
    width, rows = xts[0].shape
    left = width - width // 3
    steps = gps[0].shape[1] // wide
    return pl.pallas_call(
        late_grads_kernel,
        grid=(steps,),
        in_specs=[whole((width, rows))] * 2 + [pl.BlockSpec((rows, wide), lambda c: (0, c))] * 2,
        out_specs=pl.BlockSpec((1, left, wide), lambda c: (c, 0, 0)),
        out_shape=jax.ShapeDtypeStruct((steps, left, wide), BF16),
        scratch_shapes=[pltpu.VMEM((left, 2 * rows), BF16)],
        compiler_params=params(),
        cost_estimate=cost(10),
        name="late_grads",
    )(*xts, *gps)


def grad_act_kernel(g_ref, wout_ref, out_ref, gt_ref):
    g = g_ref[...].reshape(out_ref.shape[0], g_ref.shape[-1])

    @pl.when(pl.program_id(0) == 0)
    def _():
        gt_ref[...] = g.T

    out_ref[...] = mm(g, wout_ref[0], NT).astype(BF16)


def grad_act(g, half, w_out, wide):
    peers, _, slots, width = g.shape
    rows = peers * slots
    hidden = w_out.shape[1]
    return pl.pallas_call(
        grad_act_kernel,
        grid=(hidden // wide,),
        in_specs=[
            pl.BlockSpec((peers, 1, slots, width), lambda c: (0, half, 0, 0)),
            pl.BlockSpec((1, wide, width), lambda c: (0, c, 0)),
        ],
        out_specs=[pl.BlockSpec((rows, wide), lambda c: (0, c)), whole((width, rows))],
        out_shape=[
            jax.ShapeDtypeStruct((rows, hidden), BF16),
            jax.ShapeDtypeStruct((width, rows), BF16),
        ],
        compiler_params=params(),
        cost_estimate=cost(7),
        name="grad_act",
    )(g, w_out)


def expert_out_kernel(acta_ref, actb_ref, wout_ref, out_ref, acc_ref):
    c = pl.program_id(0)
    rows = acta_ref.shape[0]
    peers, _, slots, width = out_ref.shape

    @pl.when(c == 0)
    def _():
        acc_ref[...] = jnp.zeros_like(acc_ref)

    w_out = wout_ref[0]
    acc_ref[:rows, :] += mm(acta_ref[...], w_out)
    acc_ref[rows:, :] += mm(actb_ref[...], w_out)

    @pl.when(c == pl.num_programs(0) - 1)
    def _():
        for h in range(2):
            part = acc_ref[h * rows : (h + 1) * rows, :].astype(BF16)
            out_ref[:, h] = part.reshape(peers, slots, width)


def expert_out_of(acta, actb, w_out, wide, peers):
    rows, hidden = acta.shape
    width = w_out.shape[2]
    shape = (peers, 2, rows // peers, width)
    cols = pl.BlockSpec((rows, wide), lambda c: (0, c))
    return pl.pallas_call(
        expert_out_kernel,
        grid=(hidden // wide,),
        in_specs=[cols, cols, pl.BlockSpec((1, wide, width), lambda c: (0, c, 0))],
        out_specs=whole(shape),
        out_shape=jax.ShapeDtypeStruct(shape, BF16),
        scratch_shapes=[pltpu.VMEM((2 * rows, width), F32)],
        compiler_params=params(),
        cost_estimate=cost(14),
        name="expert_out",
    )(acta, actb, w_out)


def early_sums_kernel(early_ref, wout_ref):
    wout_ref[0] = early_ref[...].astype(F32).T


def early_sums(early):
    share = early.shape[1]
    width = early.shape[0] * 3 // 4
    wide = 2 * LANES if share % (2 * LANES) == 0 else LANES
    return pl.pallas_call(
        early_sums_kernel,
        grid=(share // wide,),
        in_specs=[pl.BlockSpec((width, wide), lambda k: (0, k))],
        out_specs=pl.BlockSpec((1, wide, width), lambda k: (0, k, 0)),
        out_shape=jax.ShapeDtypeStruct((1, share, width), F32),
        compiler_params=params(),
        cost_estimate=cost(2),
        name="early_sums",
    )(early)


def late_sums_kernel(early_ref, late_ref, win_ref):
    third = early_ref.shape[0]
    win_ref[0, :third] = early_ref[...].astype(F32)
    win_ref[0, third:] = late_ref[...].astype(F32)


def late_sums(early, late):
    left, share = late.shape
    third = left // 2
    wide = 2 * LANES if share % (2 * LANES) == 0 else LANES
    return pl.pallas_call(
        late_sums_kernel,
        grid=(share // wide,),
        in_specs=[
            pl.BlockSpec((third, wide), lambda k: (3, k)),
            pl.BlockSpec((left, wide), lambda k: (0, k)),
        ],
        out_specs=pl.BlockSpec((1, third + left, wide), lambda k: (0, 0, k)),
        out_shape=jax.ShapeDtypeStruct((1, third + left, share), F32),
        compiler_params=params(),
        cost_estimate=cost(2),
        name="late_sums",
    )(early, late)


def gather_rows(key_row, row_refs):
    keys = column_of(key_row)
    total, at = None, 0
    for ref in row_refs:
        column = lax.broadcasted_iota(I32, (keys.shape[0], ref.shape[0]), 1) + at
        part = mm(ones_where(keys == column), ref[...])
        total = part if total is None else total + part
        at += ref.shape[0]
    return total


def combine_back_kernel(
    keyr_ref, res_ref, cot_ref, gf_ref, ra_ref, rb_ref, gres_ref, gb_ref, gain_ref
):
    dy = gather_rows(keyr_ref[...], (ra_ref, rb_ref))

    @pl.when(pl.program_id(0) == 0)
    def _():
        gain_ref[...] = jnp.zeros_like(gain_ref)

    dx, dgain = norm_back(res_ref[...], gf_ref[...].reshape(1, dy.shape[1]), dy)
    gain_ref[...] += dgain
    grad = cot_ref[...].astype(F32) + dx
    gres_ref[...] = grad
    gb_ref[...] = grad.astype(BF16)


def combine_back(keyr, res, cot, gf, rows):
    toks, width = res.shape
    tile = pl.BlockSpec((QB, width), lambda i: (i, 0))
    return pl.pallas_call(
        combine_back_kernel,
        grid=(toks // QB,),
        in_specs=[
            pl.BlockSpec((1, QB), lambda i: (0, i)),
            tile,
            tile,
            whole((width,)),
            *[whole(r.shape) for r in rows],
        ],
        out_specs=[tile, tile, whole((1, width))],
        out_shape=[
            jax.ShapeDtypeStruct((toks, width), F32),
            jax.ShapeDtypeStruct((toks, width), BF16),
            jax.ShapeDtypeStruct((1, width), F32),
        ],
        compiler_params=params(),
        cost_estimate=cost(100),
        name="combine_back",
    )(keyr, res, cot, gf, *rows)


def combine_kernel(keyn_ref, res_ref, rows_ref, out_ref):
    out_ref[...] = (res_ref[...] + gather_rows(keyn_ref[...], (rows_ref,))).astype(BF16)


def combine(keyn, res, rows):
    toks, width = res.shape
    tile = pl.BlockSpec((QB, width), lambda i: (i, 0))
    return pl.pallas_call(
        combine_kernel,
        grid=(toks // QB,),
        in_specs=[
            pl.BlockSpec((1, QB), lambda i: (0, i)),
            tile,
            whole(rows.shape),
        ],
        out_specs=tile,
        out_shape=jax.ShapeDtypeStruct((toks, width), BF16),
        compiler_params=params(),
        cost_estimate=cost(5),
        name="combine",
    )(keyn, res, rows)


def shared_sums_kernel(count, experts, rows, extra, me_ref, w_ref, ga_ref, *rest):
    blocks, rest = rest[: 2 * count], rest[2 * count :]
    qkv_ref, o_ref, gain_ref, gain_ffn_ref, router_ref, embed_ref = rest[:6]
    held, small_s, sems = rest[6:]
    i = pl.program_id(0)
    width = o_ref.shape[1]
    chip, core = me_ref[0] >> 1, me_ref[0] & 1
    grain = math.gcd(rows, PAIR)

    @pl.when(i == 0)
    def _():
        copies = []
        for n, ref in enumerate(blocks):
            side = core if n < count else 1 - core
            copies.append(
                pltpu.make_async_copy(ref, held.at[side, (n % count) ^ chip], sems.at[n])
            )
        for copy in copies:
            copy.start()
        for copy in copies:
            copy.wait()

    def piece(side, two, row):
        base = two * rows + (two // 2) * extra
        pieces = []
        for t in range(0, PAIR, grain):
            at = pl.multiple_of(base + (row + t) % rows, math.gcd(grain, extra))
            pieces.append(held[side, (row + t) // rows, pl.ds(at, grain), :])
        return jnp.concatenate(pieces, axis=0).astype(F32)

    for pair in range(PAIRS):
        for part in range(3):
            at = (part * PAIRS + pair) * PAIR
            qkv_ref[:, at : at + PAIR] = piece(pair % 2, pair // 2, part * width + i * PAIR)
    for two in range(PAIRS // 2):

        @pl.when(i // 2 == two)
        def _(two=two):
            for j in range(width // PAIR):
                o_ref[:, j * PAIR : (j + 1) * PAIR] = piece(i % 2, two, 3 * width + j * PAIR)

    folded = jnp.zeros((PAIR, LANES), F32)
    for at in range(0, qkv_ref.shape[1], LANES):
        folded += qkv_ref[:, at : at + LANES] * w_ref[:, at : at + LANES].astype(F32)
    gain = jnp.sum(folded.T, axis=0, keepdims=True) / ga_ref[pl.ds(pl.multiple_of(i * PAIR, PAIR), PAIR)].reshape(
        1, PAIR
    )
    gain_ref[pl.ds(pl.multiple_of(i * PAIR, PAIR), PAIR)] = gain[0]

    @pl.when(i == 0)
    def _():
        for t in range(count):
            part = slice(2 * rows, 2 * rows + extra)
            small_s[t * extra : (t + 1) * extra, :] = held[0, t, part, :].astype(F32)
        rdim = router_ref.shape[0]
        for j in range(width // LANES):
            lanes = slice(j * LANES, (j + 1) * LANES)
            gain_ffn_ref[lanes] = small_s[j, :]
            at = 8 + j * rdim
            router_ref[:, lanes] = small_s[at : at + rdim, :]
        at = 8 + width // LANES * rdim
        embed_ref[...] = small_s[at : at + experts, :rdim]


def shared_sums(me, blocks, rows, extra, w_qkv, ga, experts, rdim):
    width = w_qkv.shape[0]
    count = len(blocks) // 2
    return pl.pallas_call(
        functools.partial(shared_sums_kernel, count, experts, rows, extra),
        grid=(width // PAIR,),
        in_specs=[smem(), pl.BlockSpec((PAIR, 3 * width), lambda i: (i, 0)), whole((width,))]
        + [pl.BlockSpec(memory_space=pl.ANY)] * (2 * count),
        out_specs=[
            pl.BlockSpec((PAIR, 3 * width), lambda i: (i, 0)),
            pl.BlockSpec((PAIR, width), lambda i: (i, 0)),
            pl.BlockSpec((width,), lambda i: (0,)),
            pl.BlockSpec((width,), lambda i: (0,)),
            whole((rdim, width)),
            whole((experts, rdim)),
        ],
        out_shape=[
            jax.ShapeDtypeStruct((width, 3 * width), F32),
            jax.ShapeDtypeStruct((width, width), F32),
            jax.ShapeDtypeStruct((width,), F32),
            jax.ShapeDtypeStruct((width,), F32),
            jax.ShapeDtypeStruct((rdim, width), F32),
            jax.ShapeDtypeStruct((experts, rdim), F32),
        ],
        scratch_shapes=[
            pltpu.VMEM((2, count, *blocks[0].shape), BF16),
            pltpu.VMEM((count * extra, LANES), F32),
            pltpu.SemaphoreType.DMA((2 * count,)),
        ],
        compiler_params=params(),
        cost_estimate=cost(2),
        name="shared_sums",
    )(me, w_qkv, ga, *blocks)


def exchange(rows):
    peers = lax.axis_size("expert")
    width = rows.shape[1]
    out = lax.all_to_all(
        rows.reshape(peers, -1, width), "expert", split_axis=0, concat_axis=0, tiled=True
    )
    return out.reshape(-1, width)


def core_groups():
    return [[core + 2 * chip for chip in range(lax.axis_size("expert") // 2)] for core in range(2)]


def swap_cores(value):
    peers = lax.axis_size("expert")
    return lax.ppermute(value, "expert", [(j, j ^ 1) for j in range(peers)])


def sum_blocks(blocks):
    return jnp.sum(blocks.astype(F32), axis=0).astype(BF16)


def sum_over_chips(blocks):
    return sum_blocks(
        lax.all_to_all(blocks, "expert", 0, 0, axis_index_groups=core_groups(), tiled=True)
    )


def xor_permute(value, axis, d):
    return lax.ppermute(value, axis, [(j, j ^ d) for j in range(lax.axis_size(axis))])


def sum_over_dp(share):
    groups = lax.axis_size("dp")
    me = lax.axis_index("dp")
    blocks = share.reshape(groups, share.shape[0] // groups, -1)
    total = lax.dynamic_index_in_dim(blocks, me, 0, keepdims=False).astype(F32)
    for d in range(1, groups):
        send = lax.dynamic_index_in_dim(blocks, me ^ d, 0, keepdims=False)
        total = total + xor_permute(send, "dp", d).astype(F32)
    return total.astype(BF16)


def gather_over_dp(part):
    groups = lax.axis_size("dp")
    me = lax.axis_index("dp")
    parts = [part] + [xor_permute(part, "dp", d) for d in range(1, groups)]
    parts = jnp.stack(parts)
    for bit in range((groups - 1).bit_length()):
        split = parts.reshape(-1, 2, 1 << bit, *part.shape)
        parts = jnp.where((me >> bit) & 1 == 1, split[:, ::-1], split)
    return parts.reshape(-1, part.shape[1])


def on_device(
    tokens,
    segments,
    routes,
    cotangent,
    w_qkv,
    w_attn_out,
    gain_attn,
    gain_ffn,
    w_router,
    embed,
    w_in,
    w_out,
):
    toks, width = tokens.shape
    experts, rdim = embed.shape
    peers = lax.axis_size("expert")
    shards = lax.axis_size("dp")
    chips = peers // 2
    share = w_in.shape[2] // shards
    me = lax.axis_index("expert").astype(I32).reshape(1)
    core = me & 1
    ga, gf = gain_attn, gain_ffn
    segr = segments.reshape(1, toks)
    wrt = w_router.T
    hold = lax.optimization_barrier

    keyr, keyn, g_slots = place(routes.reshape(1, toks), cotangent, peers, 2 * toks)
    g_rows = exchange(g_slots).reshape(peers, 2, toks // peers, width)
    q, k, v, lse, mixt, attn_in, res, xa_slots, xb_slots = attend(
        tokens, segr, keyr, w_qkv, w_attn_out, ga, gf
    )
    x_a = exchange(xa_slots)
    gact_a, gt_a = grad_act(g_rows, 0, w_out, share)
    gact_b, gt_b = grad_act(g_rows, 1, w_out, share)
    x_a, xb_slots, gact_b, gt_b, attn_in = hold((x_a, xb_slots, gact_b, gt_b, attn_in))
    x_b = exchange(xb_slots)
    act_a, gp_a, xt_a, gout_a, gwr_a, gemb_a = expert(me, wrt, embed, x_a, w_in, gact_a, share)
    gback_a = exchange(gout_a)
    act_b, gp_b, xt_b, gout_b, gwr_b, gemb_b = expert(me, wrt, embed, x_b, w_in, gact_b, share)
    gout_b, gback_a = hold((gout_b, gback_a))
    gback_b = exchange(gout_b)
    early = early_grads((gt_a, gt_b), (xt_a, xt_b), (act_a, act_b), (gp_a, gp_b), share)
    early_sum = lax.psum_scatter(early, "dp", scatter_dimension=0, tiled=True)[0]
    attnt = attn_in.T
    gback_b, early, attnt = hold((gback_b, early, attnt))
    gres, gb, ggf = combine_back(keyr, res, cotangent, gf, (gback_a, gback_b))

    small = jnp.concatenate(
        [
            jnp.pad(ggf.reshape(-1, LANES), ((0, 8 - width // LANES), (0, 0))),
            *jnp.split(gwr_a + gwr_b, width // LANES, axis=1),
            jnp.pad(gemb_a + gemb_b, ((0, 0), (0, LANES - rdim))),
        ],
        axis=0,
    )
    rows = 4 * width // chips
    extra = -(-small.shape[0] // (16 * chips)) * 16
    small = jnp.pad(small, ((0, chips * extra - small.shape[0]), (0, 0)))
    small = (small + swap_cores(small)).astype(BF16).reshape(chips, extra, LANES)
    both, grads = [], []
    for turn in range(PAIRS // 2):
        send, keep, grad = attend_back(
            turn, core, segr, q, k, v, lse, mixt, gb, attnt, w_attn_out
        )
        grads.append(grad)
        got = swap_cores(send)
        both.append((keep.astype(F32) + got.astype(F32)).astype(BF16).reshape(chips, -1, PAIR))
        if turn == 0:
            (gb, grad) = hold((gb, grad))
        elif turn == 1:
            gb, both, small, grad = hold((gb, both, small, grad))
            share_one = sum_over_chips(jnp.concatenate([*both, small], axis=1))
    last, late_act, share_one = hold((both[-1], act_b, share_one))
    share_two = sum_over_chips(last)
    fout = expert_out_of(act_a, late_act, w_out, share, peers)
    share_two, fout, late_gp, late_res = hold((share_two, fout, gp_b, gres))
    fback = exchange(fout.reshape(2 * toks, width))
    part = sum_over_dp(jnp.concatenate([share_one, share_two], axis=0))
    late = late_grads((xt_a, xt_b), (gp_a, late_gp), share)
    grad_tokens = grad_tokens_of(tokens, late_res, ga, w_qkv, grads)
    part, fback, late, grad_tokens, early_sum = hold(
        (part, fback, late, grad_tokens, early_sum)
    )
    total = gather_over_dp(part)
    late_sum = lax.psum_scatter(late, "dp", scatter_dimension=0, tiled=True)[0]
    pieces = [total] + [xor_permute(total, "expert", d) for d in range(2, peers, 2)]
    out_tokens = combine(keyn, res, fback)
    grad_w_out = early_sums(early_sum)
    pieces, out_tokens, grad_w_out = hold((pieces, out_tokens, grad_w_out))
    blocks = pieces + [swap_cores(piece) for piece in pieces]
    grad_w_qkv, grad_w_attn_out, grad_gain_attn, grad_gain_ffn, grad_router, grad_embed = (
        shared_sums(me, blocks, rows, extra, w_qkv, ga, experts, rdim)
    )
    grad_w_qkv, late_sum = hold((grad_w_qkv, late_sum))
    grad_w_in = late_sums(early_sum, late_sum)
    return (
        out_tokens,
        grad_tokens,
        grad_w_qkv,
        grad_w_attn_out,
        grad_gain_attn,
        grad_gain_ffn,
        grad_router.T,
        grad_embed,
        grad_w_in,
        grad_w_out,
    )


def solution(mesh):
    rows = P(("dp", "expert"), None)
    return jax.shard_map(
        on_device,
        mesh=mesh,
        in_specs=(
            rows,
            rows,
            rows,
            rows,
            P(),
            P(),
            P(),
            P(),
            P(),
            P(),
            P("expert", None, None),
            P("expert", None, None),
        ),
        out_specs=(
            rows,
            rows,
            P(),
            P(),
            P(),
            P(),
            P(),
            P(),
            P("expert", None, "dp"),
            P("expert", "dp", None),
        ),
        check_vma=False,
    )
```

```python
import functools
import math

import jax
import jax.numpy as jnp
from jax import lax
from jax.experimental import pallas as pl
from jax.experimental.pallas import tpu as pltpu
from jax.sharding import PartitionSpec as P

HEADS = 12
HEAD = 64
PAIRS = HEADS // 2
PAIR = 2 * HEAD
QB = 256
LANES = 128
ROUTER_WARMTH = 0.3
NORM_FLOOR = 12.0
EPSILON = 1e-05
MASK_VALUE = -1e30
F32 = jnp.float32
BF16 = jnp.bfloat16
I32 = jnp.int32
NN = (((1,), (0,)), ((), ()))
NT = (((1,), (1,)), ((), ()))
TN = (((0,), (0,)), ((), ()))
HIGHEST = lax.Precision.HIGHEST
MIB = 1 << 20


def mm(a, b, dims=NN, precision=None):
    return lax.dot_general(a, b, dims, precision=precision, preferred_element_type=F32)


def params():
    return pltpu.CompilerParams(vmem_limit_bytes=62 * MIB)


def cost(micros, nbytes=0):
    return pl.CostEstimate(
        flops=int(micros * 1.15e9), bytes_accessed=int(nbytes), transcendentals=0
    )


def whole(shape):
    return pl.BlockSpec(
        shape, lambda *_: (0,) * len(shape), pipeline_mode=pl.Buffered(buffer_count=1)
    )


def smem():
    return pl.BlockSpec(memory_space=pltpu.SMEM)


def norm_back(x, gain, dy):
    inv = lax.rsqrt(jnp.mean(x * x, axis=1, keepdims=True) + EPSILON)
    dn = dy * gain
    dx = inv * dn - x * (inv * inv * inv * jnp.mean(x * dn, axis=1, keepdims=True))
    return dx, jnp.sum(dy * x * inv, axis=0, keepdims=True)


def column_of(row):
    return jnp.broadcast_to(row.astype(F32), (8, row.shape[1])).T[:, :1].astype(row.dtype)


def ones_where(mask):
    return jnp.where(mask, 1.0, 0.0).astype(BF16)


def dispatch(key_row, rows, out_refs):
    at = 0
    for ref in out_refs:
        step = min(2 * QB, ref.shape[0])
        for r in range(0, ref.shape[0], step):
            slot = lax.broadcasted_iota(I32, (step, key_row.shape[1]), 0) + at
            ref[r : r + step, :] = mm(ones_where(key_row == slot), rows).astype(BF16)
            at += step


def place_kernel(peers, rr_ref, cot_ref, keyr_ref, keyn_ref, g_ref):
    toks = cot_ref.shape[0]
    cap = g_ref.shape[0] // peers
    half = cap // 2
    rr = rr_ref[...]
    before = ones_where(
        lax.broadcasted_iota(I32, (toks, toks), 0) <= lax.broadcasted_iota(I32, (toks, toks), 1)
    )
    hot_row = jnp.where(lax.broadcasted_iota(I32, (peers, toks), 0) == rr, 1.0, 0.0)
    upto = mm(hot_row.astype(BF16), before)
    rank = (jnp.sum(hot_row * upto, axis=0, keepdims=True) - 1.0).astype(I32)
    keyr_ref[...] = rr * half + jnp.where(rank < half, rank, rank + (peers - 1) * half)
    keyn_ref[...] = rr * cap + rank
    dispatch(keyn_ref[...], cot_ref[...], (g_ref,))


def place(routes, cot, peers, slots):
    toks, width = cot.shape
    return pl.pallas_call(
        functools.partial(place_kernel, peers),
        out_shape=[
            jax.ShapeDtypeStruct((1, toks), I32),
            jax.ShapeDtypeStruct((1, toks), I32),
            jax.ShapeDtypeStruct((slots, width), BF16),
        ],
        in_specs=[pl.BlockSpec(memory_space=pltpu.VMEM)] * 2,
        compiler_params=params(),
        cost_estimate=cost(5),
        name="place",
    )(routes, cot)


def band(i):
    return max(0, i - 2) * QB, (i + 1) * QB


def fill_bias(bias_ref, segr, count):
    segc = column_of(segr)
    for i in range(count):
        low, high = band(i)
        keys = lax.broadcasted_iota(I32, (high - low, QB), 0) + low
        queries = lax.broadcasted_iota(I32, (high - low, QB), 1) + i * QB
        same = segc[low:high] == segr[:, i * QB : (i + 1) * QB]
        bias_ref[i, : high - low, :] = jnp.where((keys <= queries) & same, 0.0, MASK_VALUE)


def head_mask(values, h):
    lane = lax.broadcasted_iota(I32, values.shape, 1)
    return jnp.where((lane >= h * HEAD) & (lane < (h + 1) * HEAD), values, jnp.zeros_like(values))


def attend_kernel(
    tok_ref,
    segr_ref,
    keyr_ref,
    wq_ref,
    wk_ref,
    wv_ref,
    wo_ref,
    ga_ref,
    gf_ref,
    q_ref,
    k_ref,
    v_ref,
    lse_ref,
    mixt_ref,
    attn_ref,
    res_ref,
    xa_ref,
    xb_ref,
    bias_ref,
    mix_ref,
):
    p = pl.program_id(0)
    toks, width = tok_ref.shape
    count = toks // QB
    both = q_ref.shape[1]

    @pl.when(p == 0)
    def _():
        segr = segr_ref[...]
        segc = column_of(segr)
        for i in range(count):
            low, high = band(i)
            keys = lax.broadcasted_iota(I32, (QB, high - low), 1) + low
            queries = lax.broadcasted_iota(I32, (QB, high - low), 0) + i * QB
            same = segr[:, low:high] == segc[i * QB : (i + 1) * QB]
            bias_ref[i, :, : high - low] = jnp.where((keys <= queries) & same, 0.0, MASK_VALUE)
        x = tok_ref[...].astype(F32)
        inv = lax.rsqrt(jnp.mean(x * x, axis=1, keepdims=True) + EPSILON)
        attn_ref[...] = (x * inv * ga_ref[...].reshape(1, width)).astype(BF16)

    attn_in = attn_ref[...]
    weights = jnp.concatenate([wq_ref[...], wk_ref[...], wv_ref[...]], axis=1)
    qkv = mm(attn_in, weights)
    for part, ref in enumerate((q_ref, k_ref, v_ref)):
        ref[...] = qkv[:, part * both : (part + 1) * both].astype(BF16)
    lane = lax.broadcasted_iota(I32, (QB, PAIR), 1)
    for i in range(count):
        low, high = band(i)
        cols = slice(i * QB, (i + 1) * QB)
        for pair in range(both // PAIR):
            lanes = slice(pair * PAIR, (pair + 1) * PAIR)
            q = q_ref[cols, lanes] * HEAD**-0.5
            keys = k_ref[low:high, lanes]
            values = v_ref[low:high, lanes]
            parts, sums = [], []
            for h in range(2):
                s = mm(head_mask(q, h), keys, NT) + bias_ref[i, :, : high - low]
                top = jnp.max(s, axis=1, keepdims=True)
                w = jnp.exp(s - top)
                total = jnp.sum(w, axis=1, keepdims=True)
                sums.append(top + jnp.log(total))
                parts.append(mm((w * (1.0 / total)).astype(BF16), values))
            mixed = jnp.where(lane < HEAD, parts[0], parts[1])
            lse_ref[pair, :, cols] = jnp.where(lane == 0, sums[0], sums[1]).T[:2]
            mixt_ref[lanes, cols] = mixed.T.astype(BF16)
            at = pl.ds(pl.multiple_of(p * both + pair * PAIR, PAIR), PAIR)
            mix_ref[cols, at] = mixed.astype(BF16)

    @pl.when(p == pl.num_programs(0) - 1)
    def _():
        res = tok_ref[...].astype(F32) + mm(mix_ref[...], wo_ref[...])
        res_ref[...] = res
        inv = lax.rsqrt(jnp.mean(res * res, axis=1, keepdims=True) + EPSILON)
        ffn_in = (res * inv * gf_ref[...].reshape(1, width)).astype(BF16)
        dispatch(keyr_ref[...], ffn_in, (xa_ref, xb_ref))


def attend(tokens, segr, keyr, w_qkv, w_o, ga, gf):
    toks, width = tokens.shape
    both = PAIR
    pair_cols = pl.BlockSpec((toks, both), lambda p: (0, p))
    heads = jax.ShapeDtypeStruct((toks, width), BF16)
    weights = [
        pl.BlockSpec((width, both), lambda p, part=part: (0, part * PAIRS + p))
        for part in range(3)
    ]
    return pl.pallas_call(
        attend_kernel,
        grid=(PAIRS,),
        in_specs=[
            whole((toks, width)),
            whole((1, toks)),
            whole((1, toks)),
            *weights,
            whole((width, width)),
            whole((width,)),
            whole((width,)),
        ],
        out_specs=[
            pair_cols,
            pair_cols,
            pair_cols,
            pl.BlockSpec((1, 2, toks), lambda p: (p, 0, 0)),
            pl.BlockSpec((both, toks), lambda p: (p, 0)),
            whole((toks, width)),
            whole((toks, width)),
            whole((toks, width)),
            whole((toks, width)),
        ],
        out_shape=[
            heads,
            heads,
            heads,
            jax.ShapeDtypeStruct((PAIRS, 2, toks), F32),
            jax.ShapeDtypeStruct((width, toks), BF16),
            heads,
            jax.ShapeDtypeStruct((toks, width), F32),
            heads,
            heads,
        ],
        scratch_shapes=[
            pltpu.VMEM((toks // QB, QB, 3 * QB), F32),
            pltpu.VMEM((toks, width), BF16),
        ],
        compiler_params=params(),
        cost_estimate=cost(42),
        name="attend",
    )(tokens, segr, keyr, w_qkv, w_qkv, w_qkv, w_o, ga, gf)


def attend_back_kernel(
    core_ref,
    segr_ref,
    q_ref,
    k_ref,
    v_ref,
    lse_ref,
    mixt_ref,
    gb_ref,
    attnt_ref,
    wo_ref,
    send_ref,
    keep_ref,
    gqkv_ref,
    bias_ref,
    dqt_ref,
    dk_ref,
    dv_ref,
    do_ref,
):
    toks, width = gb_ref.shape
    both = q_ref.shape[1]
    count = toks // QB
    scale = HEAD**-0.5
    fill_bias(bias_ref, segr_ref[...], count)
    gb = gb_ref[...]
    grad_out = mm(gb, wo_ref[...], NT)
    do_ref[...] = grad_out.astype(BF16)
    mixt = mixt_ref[...]
    gwo = mm(mixt, gb).astype(BF16)
    weighted = grad_out.astype(BF16).astype(F32).T * mixt.astype(F32)
    delta = [
        jnp.sum(weighted[h * HEAD : (h + 1) * HEAD], axis=0, keepdims=True)
        for h in range(both // HEAD)
    ]
    kt = k_ref[...].astype(F32).T.astype(BF16)
    dk_ref[...] = jnp.zeros_like(dk_ref)
    dv_ref[...] = jnp.zeros_like(dv_ref)
    for i in range(count):
        low, high = band(i)
        cols = slice(i * QB, (i + 1) * QB)
        for pair in range(both // PAIR):
            lanes = slice(pair * PAIR, (pair + 1) * PAIR)
            q = q_ref[cols, lanes] * scale
            do = do_ref[cols, lanes]
            keys = k_ref[low:high, lanes]
            values = v_ref[low:high, lanes]
            dk_add, dv_add = [], []
            for h in range(2):
                head = slice((2 * pair + h) * HEAD, (2 * pair + h + 1) * HEAD)
                qm, dom = head_mask(q, h), head_mask(do, h)
                s = mm(keys, qm, NT) + bias_ref[i, : high - low, :]
                pr = jnp.exp(s - lse_ref[pair, h : h + 1, cols])
                dpr = mm(values, dom, NT)
                ds = (pr * (dpr - delta[2 * pair + h][:, cols])).astype(BF16)
                dv_add.append(mm(pr.astype(BF16), dom))
                dk_add.append(mm(ds, qm))
                dqt_ref[head, cols] = mm(kt[head, low:high], ds) * scale
            dk_ref[low:high, lanes] += dk_add[0] + dk_add[1]
            dv_ref[low:high, lanes] += dv_add[0] + dv_add[1]
    grads = [
        dqt_ref[...].T.astype(BF16),
        dk_ref[...].astype(BF16),
        dv_ref[...].astype(BF16),
    ]
    for part in range(3):
        gqkv_ref[part] = grads[part]
    gw = mm(attnt_ref[...], jnp.concatenate(grads, axis=1)).astype(BF16)
    for core in range(2):

        @pl.when(core_ref[0] == core)
        def _(core=core):
            for pair, ref in ((1 - core, send_ref), (core, keep_ref)):
                for part in range(3):
                    at = part * both + pair * PAIR
                    ref[part] = gw[:, at : at + PAIR]
                for j in range(width // PAIR):
                    ref[3, j * PAIR : (j + 1) * PAIR, :] = gwo[
                        pair * PAIR : (pair + 1) * PAIR, j * PAIR : (j + 1) * PAIR
                    ]


def attend_back(turn, core, segr, q, k, v, lse, mixt, gb, attnt, w_o):
    toks, width = gb.shape
    both = 2 * PAIR
    pair_cols = pl.BlockSpec((toks, both), lambda p: (0, turn))
    gw_shape = jax.ShapeDtypeStruct((4, width, PAIR), BF16)
    return pl.pallas_call(
        attend_back_kernel,
        grid=(1,),
        in_specs=[
            smem(),
            whole((1, toks)),
            pair_cols,
            pair_cols,
            pair_cols,
            pl.BlockSpec((2, 2, toks), lambda p: (turn, 0, 0)),
            pl.BlockSpec((both, toks), lambda p: (turn, 0)),
            whole((toks, width)),
            whole((width, toks)),
            pl.BlockSpec((both, width), lambda p: (turn, 0)),
        ],
        out_specs=[whole((4, width, PAIR)), whole((4, width, PAIR)), whole((3, toks, both))],
        out_shape=[gw_shape, gw_shape, jax.ShapeDtypeStruct((3, toks, both), BF16)],
        scratch_shapes=[
            pltpu.VMEM((toks // QB, 3 * QB, QB), F32),
            pltpu.VMEM((both, toks), F32),
            pltpu.VMEM((toks, both), F32),
            pltpu.VMEM((toks, both), F32),
            pltpu.VMEM((toks, both), BF16),
        ],
        compiler_params=params(),
        cost_estimate=cost(10 if turn + 1 == PAIRS // 2 else 2),
        name="attend_back",
    )(core, segr, q, k, v, lse, mixt, gb, attnt, w_o)


def grad_tokens_kernel(tok_ref, gres_ref, ga_ref, w_ref, *rest):
    *g_refs, out_ref = rest
    grads = [ref[part] for part in range(3) for ref in g_refs]
    dy = mm(jnp.concatenate(grads, axis=1), w_ref[...], NT)
    dx, _ = norm_back(tok_ref[...].astype(F32), ga_ref[...].reshape(1, dy.shape[1]), dy)
    out_ref[...] = gres_ref[...] + dx


def grad_tokens_of(tokens, gres, ga, w_qkv, grads):
    toks, width = tokens.shape
    rows = 2 * QB
    tile = pl.BlockSpec((rows, width), lambda i: (i, 0))
    return pl.pallas_call(
        grad_tokens_kernel,
        grid=(toks // rows,),
        in_specs=[tile, tile, whole((width,)), whole(w_qkv.shape)]
        + [pl.BlockSpec((3, rows, 2 * PAIR), lambda i: (0, i, 0))] * len(grads),
        out_specs=tile,
        out_shape=jax.ShapeDtypeStruct((toks, width), F32),
        compiler_params=params(),
        cost_estimate=cost(9),
        name="grad_tokens",
    )(tokens, gres, ga, w_qkv, *grads)


def unit_scale(values, axis):
    total = jnp.sum(values * values, axis=axis, keepdims=True)
    return lax.rsqrt(jnp.maximum(total, NORM_FLOOR)), total


def unit_back(values, inv, total, grad, axis):
    passed = jnp.where(total > NORM_FLOOR, 1.0, jnp.where(total == NORM_FLOOR, 0.5, 0.0))
    inner = jnp.sum(grad * values, axis=axis, keepdims=True)
    return inv * grad - passed * inv * inv * inv * inner * values


def gelu_and_slope(h):
    cdf = 0.5 + 0.5 * lax.erf(h * 0.7071067811865476)
    pdf = 0.3989422804014327 * jnp.exp(-0.5 * h * h)
    return h * cdf, cdf + h * pdf


def route(me, x, wrt, emb):
    z = mm(wrt, x, NT)
    inv, total = unit_scale(z, 0)
    zn = z * inv
    en = emb * unit_scale(emb, 1)[0]
    logits = mm(en, zn, NN, HIGHEST) / ROUTER_WARMTH
    w = jnp.exp(logits - jnp.max(logits, axis=0, keepdims=True))
    chances = w / jnp.sum(w, axis=0, keepdims=True)
    mine = jnp.where(lax.broadcasted_iota(I32, logits.shape, 0) == me, 1.0, 0.0)
    return z, inv, total, zn, en, chances, mine


def expert_kernel(
    me_ref,
    wrt_ref,
    emb_ref,
    x_ref,
    win_ref,
    ga_ref,
    act_ref,
    gp_ref,
    xt_ref,
    gout_ref,
    gwrt_ref,
    gemb_ref,
    w_s,
    gp_s,
    acc_s,
    gate_s,
):
    c = pl.program_id(0)
    rows, width = x_ref.shape
    me = me_ref[0]

    @pl.when(c == 0)
    def _():
        chances, mine = route(me, x_ref[...], wrt_ref[...], emb_ref[...])[-2:]
        gate = column_of(jnp.sum(chances * mine, axis=0, keepdims=True))
        gate_s[...] = jnp.broadcast_to(gate, (rows, LANES))
        acc_s[...] = jnp.zeros_like(acc_s)
        for r in range(0, rows, QB):
            xt_ref[:, r : r + QB] = x_ref[r : r + QB, :].T

    w_in = win_ref[0]
    wide = w_in.shape[1]
    chunk = pl.ds(pl.multiple_of(c * wide, LANES), wide)
    w_s[:, chunk] = w_in
    step = min(2 * QB, rows)
    for r in range(0, rows, step):
        part = slice(r, r + step)
        h = mm(x_ref[part, :], w_in)
        act, slope = gelu_and_slope(h)
        gate = jnp.concatenate([gate_s[part, :]] * (wide // LANES), axis=1)
        ga = ga_ref[part, :].astype(F32)
        act = act * gate
        act_ref[part, :] = act.astype(BF16)
        gp = (ga * (slope * gate)).astype(BF16)
        gp_s[part, chunk] = gp
        gp_ref[part, :] = gp
        prod = act * ga
        folded = prod[:, :LANES]
        for j in range(LANES, wide, LANES):
            folded = folded + prod[:, j : j + LANES]
        acc_s[part, :] += folded

    @pl.when(c == pl.num_programs(0) - 1)
    def _():
        x, wrt, emb = x_ref[...], wrt_ref[...], emb_ref[...]
        z, inv, total, zn, en, chances, mine = route(me, x, wrt, emb)
        weight = jnp.sum(acc_s[...].T, axis=0, keepdims=True)
        dl = weight * (mine - chances) / ROUTER_WARMTH
        gen = mm(dl, zn, NT, HIGHEST)
        dz = unit_back(z, inv, total, mm(en, dl, TN, HIGHEST), 0)
        dz_top = dz.astype(BF16)
        dz_low = (dz - dz_top.astype(F32)).astype(BF16)
        gwrt_ref[...] = mm(dz_top, x) + mm(dz_low, x)
        einv, etotal = unit_scale(emb, 1)
        gemb_ref[...] = unit_back(emb, einv, etotal, gen, 1)
        dz_top, dz_low = dz_top.astype(F32).T.astype(BF16), dz_low.astype(F32).T.astype(BF16)
        for r in range(0, rows, step):
            part = slice(r, r + step)
            back = mm(gp_s[part, :], w_s[...], NT).astype(BF16).astype(F32)
            back = back + mm(dz_top[part], wrt) + mm(dz_low[part], wrt)
            gout_ref[part, :] = back.astype(BF16)


def expert(me, wrt, emb, x, w_in, ga, wide):
    rows, width = x.shape
    hidden = w_in.shape[2]
    cols = pl.BlockSpec((rows, wide), lambda c: (0, c))
    hid = jax.ShapeDtypeStruct((rows, hidden), BF16)
    return pl.pallas_call(
        expert_kernel,
        grid=(hidden // wide,),
        in_specs=[
            smem(),
            whole(wrt.shape),
            whole(emb.shape),
            whole((rows, width)),
            pl.BlockSpec((1, width, wide), lambda c: (0, 0, c)),
            cols,
        ],
        out_specs=[
            cols,
            cols,
            whole((width, rows)),
            whole((rows, width)),
            whole(wrt.shape),
            whole(emb.shape),
        ],
        out_shape=[
            hid,
            hid,
            jax.ShapeDtypeStruct((width, rows), BF16),
            jax.ShapeDtypeStruct((rows, width), BF16),
            jax.ShapeDtypeStruct(wrt.shape, F32),
            jax.ShapeDtypeStruct(emb.shape, F32),
        ],
        scratch_shapes=[
            pltpu.VMEM((width, hidden), BF16),
            pltpu.VMEM((rows, hidden), BF16),
            pltpu.VMEM((rows, LANES), F32),
            pltpu.VMEM((rows, LANES), F32),
        ],
        compiler_params=params(),
        cost_estimate=cost(23),
        name="expert",
    )(me, wrt, emb, x, w_in, ga)


def early_grads_kernel(
    gta_ref, gtb_ref, xta_ref, xtb_ref, acta_ref, actb_ref, gpa_ref, gpb_ref, out_ref, gt_s, xt_s
):
    rows = gta_ref.shape[1]
    width = gta_ref.shape[0]

    @pl.when(pl.program_id(0) == 0)
    def _():
        gt_s[:, :rows] = gta_ref[...]
        gt_s[:, rows:] = gtb_ref[...]
        xt_s[:, :rows] = xta_ref[...]
        xt_s[:, rows:] = xtb_ref[...]

    act = jnp.concatenate([acta_ref[...], actb_ref[...]], axis=0)
    out_ref[0, :width] = mm(gt_s[...], act).astype(BF16)
    gp = jnp.concatenate([gpa_ref[...], gpb_ref[...]], axis=0)
    out_ref[0, width:] = mm(xt_s[...], gp).astype(BF16)


def early_grads(gts, xts, acts, gps, wide):
    width, rows = gts[0].shape
    third = width // 3
    steps = acts[0].shape[1] // wide
    return pl.pallas_call(
        early_grads_kernel,
        grid=(steps,),
        in_specs=[whole((width, rows))] * 2
        + [whole((third, rows))] * 2
        + [pl.BlockSpec((rows, wide), lambda c: (0, c))] * 4,
        out_specs=pl.BlockSpec((1, width + third, wide), lambda c: (c, 0, 0)),
        out_shape=jax.ShapeDtypeStruct((steps, width + third, wide), BF16),
        scratch_shapes=[
            pltpu.VMEM((width, 2 * rows), BF16),
            pltpu.VMEM((third, 2 * rows), BF16),
        ],
        compiler_params=params(),
        cost_estimate=cost(10),
        name="early_grads",
    )(*gts, *xts, *acts, *gps)


def late_grads_kernel(xta_ref, xtb_ref, gpa_ref, gpb_ref, out_ref, xt_s):
    width, rows = xta_ref.shape
    third = width // 3

    @pl.when(pl.program_id(0) == 0)
    def _():
        xt_s[:, :rows] = xta_ref[third:, :]
        xt_s[:, rows:] = xtb_ref[third:, :]

    gp = jnp.concatenate([gpa_ref[...], gpb_ref[...]], axis=0)
    out_ref[0] = mm(xt_s[...], gp).astype(BF16)


def late_grads(xts, gps, wide):
    width, rows = xts[0].shape
    left = width - width // 3
    steps = gps[0].shape[1] // wide
    return pl.pallas_call(
        late_grads_kernel,
        grid=(steps,),
        in_specs=[whole((width, rows))] * 2 + [pl.BlockSpec((rows, wide), lambda c: (0, c))] * 2,
        out_specs=pl.BlockSpec((1, left, wide), lambda c: (c, 0, 0)),
        out_shape=jax.ShapeDtypeStruct((steps, left, wide), BF16),
        scratch_shapes=[pltpu.VMEM((left, 2 * rows), BF16)],
        compiler_params=params(),
        cost_estimate=cost(10),
        name="late_grads",
    )(*xts, *gps)


def grad_act_kernel(g_ref, wout_ref, out_ref, gt_ref):
    g = g_ref[...].reshape(out_ref.shape[0], g_ref.shape[-1])

    @pl.when(pl.program_id(0) == 0)
    def _():
        gt_ref[...] = g.T

    out_ref[...] = mm(g, wout_ref[0], NT).astype(BF16)


def grad_act(g, half, w_out, wide):
    peers, _, slots, width = g.shape
    rows = peers * slots
    hidden = w_out.shape[1]
    return pl.pallas_call(
        grad_act_kernel,
        grid=(hidden // wide,),
        in_specs=[
            pl.BlockSpec((peers, 1, slots, width), lambda c: (0, half, 0, 0)),
            pl.BlockSpec((1, wide, width), lambda c: (0, c, 0)),
        ],
        out_specs=[pl.BlockSpec((rows, wide), lambda c: (0, c)), whole((width, rows))],
        out_shape=[
            jax.ShapeDtypeStruct((rows, hidden), BF16),
            jax.ShapeDtypeStruct((width, rows), BF16),
        ],
        compiler_params=params(),
        cost_estimate=cost(7),
        name="grad_act",
    )(g, w_out)


def expert_out_kernel(acta_ref, actb_ref, wout_ref, out_ref, acc_ref):
    c = pl.program_id(0)
    rows = acta_ref.shape[0]
    peers, _, slots, width = out_ref.shape

    @pl.when(c == 0)
    def _():
        acc_ref[...] = jnp.zeros_like(acc_ref)

    w_out = wout_ref[0]
    acc_ref[:rows, :] += mm(acta_ref[...], w_out)
    acc_ref[rows:, :] += mm(actb_ref[...], w_out)

    @pl.when(c == pl.num_programs(0) - 1)
    def _():
        for h in range(2):
            part = acc_ref[h * rows : (h + 1) * rows, :].astype(BF16)
            out_ref[:, h] = part.reshape(peers, slots, width)


def expert_out_of(acta, actb, w_out, wide, peers):
    rows, hidden = acta.shape
    width = w_out.shape[2]
    shape = (peers, 2, rows // peers, width)
    cols = pl.BlockSpec((rows, wide), lambda c: (0, c))
    return pl.pallas_call(
        expert_out_kernel,
        grid=(hidden // wide,),
        in_specs=[cols, cols, pl.BlockSpec((1, wide, width), lambda c: (0, c, 0))],
        out_specs=whole(shape),
        out_shape=jax.ShapeDtypeStruct(shape, BF16),
        scratch_shapes=[pltpu.VMEM((2 * rows, width), F32)],
        compiler_params=params(),
        cost_estimate=cost(14),
        name="expert_out",
    )(acta, actb, w_out)


def early_sums_kernel(early_ref, wout_ref):
    wout_ref[0] = early_ref[...].astype(F32).T


def early_sums(early):
    share = early.shape[1]
    width = early.shape[0] * 3 // 4
    wide = 2 * LANES if share % (2 * LANES) == 0 else LANES
    return pl.pallas_call(
        early_sums_kernel,
        grid=(share // wide,),
        in_specs=[pl.BlockSpec((width, wide), lambda k: (0, k))],
        out_specs=pl.BlockSpec((1, wide, width), lambda k: (0, k, 0)),
        out_shape=jax.ShapeDtypeStruct((1, share, width), F32),
        compiler_params=params(),
        cost_estimate=cost(2),
        name="early_sums",
    )(early)


def late_sums_kernel(early_ref, late_ref, win_ref):
    third = early_ref.shape[0]
    win_ref[0, :third] = early_ref[...].astype(F32)
    win_ref[0, third:] = late_ref[...].astype(F32)


def late_sums(early, late):
    left, share = late.shape
    third = left // 2
    wide = 2 * LANES if share % (2 * LANES) == 0 else LANES
    return pl.pallas_call(
        late_sums_kernel,
        grid=(share // wide,),
        in_specs=[
            pl.BlockSpec((third, wide), lambda k: (3, k)),
            pl.BlockSpec((left, wide), lambda k: (0, k)),
        ],
        out_specs=pl.BlockSpec((1, third + left, wide), lambda k: (0, 0, k)),
        out_shape=jax.ShapeDtypeStruct((1, third + left, share), F32),
        compiler_params=params(),
        cost_estimate=cost(2),
        name="late_sums",
    )(early, late)


def gather_rows(key_row, row_refs):
    keys = column_of(key_row)
    total, at = None, 0
    for ref in row_refs:
        column = lax.broadcasted_iota(I32, (keys.shape[0], ref.shape[0]), 1) + at
        part = mm(ones_where(keys == column), ref[...])
        total = part if total is None else total + part
        at += ref.shape[0]
    return total


def combine_back_kernel(
    keyr_ref, res_ref, cot_ref, gf_ref, ra_ref, rb_ref, gres_ref, gb_ref, gain_ref
):
    dy = gather_rows(keyr_ref[...], (ra_ref, rb_ref))

    @pl.when(pl.program_id(0) == 0)
    def _():
        gain_ref[...] = jnp.zeros_like(gain_ref)

    dx, dgain = norm_back(res_ref[...], gf_ref[...].reshape(1, dy.shape[1]), dy)
    gain_ref[...] += dgain
    grad = cot_ref[...].astype(F32) + dx
    gres_ref[...] = grad
    gb_ref[...] = grad.astype(BF16)


def combine_back(keyr, res, cot, gf, rows):
    toks, width = res.shape
    tile = pl.BlockSpec((QB, width), lambda i: (i, 0))
    return pl.pallas_call(
        combine_back_kernel,
        grid=(toks // QB,),
        in_specs=[
            pl.BlockSpec((1, QB), lambda i: (0, i)),
            tile,
            tile,
            whole((width,)),
            *[whole(r.shape) for r in rows],
        ],
        out_specs=[tile, tile, whole((1, width))],
        out_shape=[
            jax.ShapeDtypeStruct((toks, width), F32),
            jax.ShapeDtypeStruct((toks, width), BF16),
            jax.ShapeDtypeStruct((1, width), F32),
        ],
        compiler_params=params(),
        cost_estimate=cost(100),
        name="combine_back",
    )(keyr, res, cot, gf, *rows)


def combine_kernel(keyn_ref, res_ref, rows_ref, out_ref):
    out_ref[...] = (res_ref[...] + gather_rows(keyn_ref[...], (rows_ref,))).astype(BF16)


def combine(keyn, res, rows):
    toks, width = res.shape
    tile = pl.BlockSpec((QB, width), lambda i: (i, 0))
    return pl.pallas_call(
        combine_kernel,
        grid=(toks // QB,),
        in_specs=[
            pl.BlockSpec((1, QB), lambda i: (0, i)),
            tile,
            whole(rows.shape),
        ],
        out_specs=tile,
        out_shape=jax.ShapeDtypeStruct((toks, width), BF16),
        compiler_params=params(),
        cost_estimate=cost(5),
        name="combine",
    )(keyn, res, rows)


def shared_sums_kernel(count, experts, rows, extra, me_ref, w_ref, ga_ref, *rest):
    blocks, rest = rest[: 2 * count], rest[2 * count :]
    qkv_ref, o_ref, gain_ref, gain_ffn_ref, router_ref, embed_ref = rest[:6]
    held, small_s, sems = rest[6:]
    i = pl.program_id(0)
    width = o_ref.shape[1]
    chip, core = me_ref[0] >> 1, me_ref[0] & 1
    grain = math.gcd(rows, PAIR)

    @pl.when(i == 0)
    def _():
        copies = []
        for n, ref in enumerate(blocks):
            side = core if n < count else 1 - core
            copies.append(
                pltpu.make_async_copy(ref, held.at[side, (n % count) ^ chip], sems.at[n])
            )
        for copy in copies:
            copy.start()
        for copy in copies:
            copy.wait()

    def piece(side, two, row):
        base = two * rows + (two // 2) * extra
        pieces = []
        for t in range(0, PAIR, grain):
            at = pl.multiple_of(base + (row + t) % rows, math.gcd(grain, extra))
            pieces.append(held[side, (row + t) // rows, pl.ds(at, grain), :])
        return jnp.concatenate(pieces, axis=0).astype(F32)

    for pair in range(PAIRS):
        for part in range(3):
            at = (part * PAIRS + pair) * PAIR
            qkv_ref[:, at : at + PAIR] = piece(pair % 2, pair // 2, part * width + i * PAIR)
    for two in range(PAIRS // 2):

        @pl.when(i // 2 == two)
        def _(two=two):
            for j in range(width // PAIR):
                o_ref[:, j * PAIR : (j + 1) * PAIR] = piece(i % 2, two, 3 * width + j * PAIR)

    folded = jnp.zeros((PAIR, LANES), F32)
    for at in range(0, qkv_ref.shape[1], LANES):
        folded += qkv_ref[:, at : at + LANES] * w_ref[:, at : at + LANES].astype(F32)
    gain = jnp.sum(folded.T, axis=0, keepdims=True) / ga_ref[pl.ds(pl.multiple_of(i * PAIR, PAIR), PAIR)].reshape(
        1, PAIR
    )
    gain_ref[pl.ds(pl.multiple_of(i * PAIR, PAIR), PAIR)] = gain[0]

    @pl.when(i == 0)
    def _():
        for t in range(count):
            part = slice(2 * rows, 2 * rows + extra)
            small_s[t * extra : (t + 1) * extra, :] = held[0, t, part, :].astype(F32)
        rdim = router_ref.shape[0]
        for j in range(width // LANES):
            lanes = slice(j * LANES, (j + 1) * LANES)
            gain_ffn_ref[lanes] = small_s[j, :]
            at = 8 + j * rdim
            router_ref[:, lanes] = small_s[at : at + rdim, :]
        at = 8 + width // LANES * rdim
        embed_ref[...] = small_s[at : at + experts, :rdim]


def shared_sums(me, blocks, rows, extra, w_qkv, ga, experts, rdim):
    width = w_qkv.shape[0]
    count = len(blocks) // 2
    return pl.pallas_call(
        functools.partial(shared_sums_kernel, count, experts, rows, extra),
        grid=(width // PAIR,),
        in_specs=[smem(), pl.BlockSpec((PAIR, 3 * width), lambda i: (i, 0)), whole((width,))]
        + [pl.BlockSpec(memory_space=pl.ANY)] * (2 * count),
        out_specs=[
            pl.BlockSpec((PAIR, 3 * width), lambda i: (i, 0)),
            pl.BlockSpec((PAIR, width), lambda i: (i, 0)),
            pl.BlockSpec((width,), lambda i: (0,)),
            pl.BlockSpec((width,), lambda i: (0,)),
            whole((rdim, width)),
            whole((experts, rdim)),
        ],
        out_shape=[
            jax.ShapeDtypeStruct((width, 3 * width), F32),
            jax.ShapeDtypeStruct((width, width), F32),
            jax.ShapeDtypeStruct((width,), F32),
            jax.ShapeDtypeStruct((width,), F32),
            jax.ShapeDtypeStruct((rdim, width), F32),
            jax.ShapeDtypeStruct((experts, rdim), F32),
        ],
        scratch_shapes=[
            pltpu.VMEM((2, count, *blocks[0].shape), BF16),
            pltpu.VMEM((count * extra, LANES), F32),
            pltpu.SemaphoreType.DMA((2 * count,)),
        ],
        compiler_params=params(),
        cost_estimate=cost(2),
        name="shared_sums",
    )(me, w_qkv, ga, *blocks)


def exchange(rows):
    peers = lax.axis_size("expert")
    width = rows.shape[1]
    out = lax.all_to_all(
        rows.reshape(peers, -1, width), "expert", split_axis=0, concat_axis=0, tiled=True
    )
    return out.reshape(-1, width)


def core_groups():
    return [[core + 2 * chip for chip in range(lax.axis_size("expert") // 2)] for core in range(2)]


def swap_cores(value):
    peers = lax.axis_size("expert")
    return lax.ppermute(value, "expert", [(j, j ^ 1) for j in range(peers)])


def sum_blocks(blocks):
    return jnp.sum(blocks.astype(F32), axis=0).astype(BF16)


def sum_over_chips(blocks):
    return sum_blocks(
        lax.all_to_all(blocks, "expert", 0, 0, axis_index_groups=core_groups(), tiled=True)
    )


def xor_permute(value, axis, d):
    return lax.ppermute(value, axis, [(j, j ^ d) for j in range(lax.axis_size(axis))])


def sum_over_dp(share):
    groups = lax.axis_size("dp")
    me = lax.axis_index("dp")
    blocks = share.reshape(groups, share.shape[0] // groups, -1)
    total = lax.dynamic_index_in_dim(blocks, me, 0, keepdims=False).astype(F32)
    for d in range(1, groups):
        send = lax.dynamic_index_in_dim(blocks, me ^ d, 0, keepdims=False)
        total = total + xor_permute(send, "dp", d).astype(F32)
    return total.astype(BF16)


def gather_over_dp(part):
    groups = lax.axis_size("dp")
    me = lax.axis_index("dp")
    parts = [part] + [xor_permute(part, "dp", d) for d in range(1, groups)]
    parts = jnp.stack(parts)
    for bit in range((groups - 1).bit_length()):
        split = parts.reshape(-1, 2, 1 << bit, *part.shape)
        parts = jnp.where((me >> bit) & 1 == 1, split[:, ::-1], split)
    return parts.reshape(-1, part.shape[1])


def on_device(
    tokens,
    segments,
    routes,
    cotangent,
    w_qkv,
    w_attn_out,
    gain_attn,
    gain_ffn,
    w_router,
    embed,
    w_in,
    w_out,
):
    toks, width = tokens.shape
    experts, rdim = embed.shape
    peers = lax.axis_size("expert")
    shards = lax.axis_size("dp")
    chips = peers // 2
    share = w_in.shape[2] // shards
    me = lax.axis_index("expert").astype(I32).reshape(1)
    core = me & 1
    ga, gf = gain_attn, gain_ffn
    segr = segments.reshape(1, toks)
    wrt = w_router.T
    hold = lax.optimization_barrier

    keyr, keyn, g_slots = place(routes.reshape(1, toks), cotangent, peers, 2 * toks)
    g_rows = exchange(g_slots).reshape(peers, 2, toks // peers, width)
    q, k, v, lse, mixt, attn_in, res, xa_slots, xb_slots = attend(
        tokens, segr, keyr, w_qkv, w_attn_out, ga, gf
    )
    x_a = exchange(xa_slots)
    gact_a, gt_a = grad_act(g_rows, 0, w_out, share)
    gact_b, gt_b = grad_act(g_rows, 1, w_out, share)
    x_a, xb_slots, gact_b, gt_b, attn_in = hold((x_a, xb_slots, gact_b, gt_b, attn_in))
    x_b = exchange(xb_slots)
    act_a, gp_a, xt_a, gout_a, gwr_a, gemb_a = expert(me, wrt, embed, x_a, w_in, gact_a, share)
    gback_a = exchange(gout_a)
    act_b, gp_b, xt_b, gout_b, gwr_b, gemb_b = expert(me, wrt, embed, x_b, w_in, gact_b, share)
    gout_b, gback_a = hold((gout_b, gback_a))
    gback_b = exchange(gout_b)
    early = early_grads((gt_a, gt_b), (xt_a, xt_b), (act_a, act_b), (gp_a, gp_b), share)
    early_sum = lax.psum_scatter(early, "dp", scatter_dimension=0, tiled=True)[0]
    attnt = attn_in.T
    gback_b, early, attnt = hold((gback_b, early, attnt))
    gres, gb, ggf = combine_back(keyr, res, cotangent, gf, (gback_a, gback_b))

    small = jnp.concatenate(
        [
            jnp.pad(ggf.reshape(-1, LANES), ((0, 8 - width // LANES), (0, 0))),
            *jnp.split(gwr_a + gwr_b, width // LANES, axis=1),
            jnp.pad(gemb_a + gemb_b, ((0, 0), (0, LANES - rdim))),
        ],
        axis=0,
    )
    rows = 4 * width // chips
    extra = -(-small.shape[0] // (16 * chips)) * 16
    small = jnp.pad(small, ((0, chips * extra - small.shape[0]), (0, 0)))
    small = (small + swap_cores(small)).astype(BF16).reshape(chips, extra, LANES)
    both, grads = [], []
    for turn in range(PAIRS // 2):
        send, keep, grad = attend_back(
            turn, core, segr, q, k, v, lse, mixt, gb, attnt, w_attn_out
        )
        grads.append(grad)
        got = swap_cores(send)
        both.append((keep.astype(F32) + got.astype(F32)).astype(BF16).reshape(chips, -1, PAIR))
        if turn == 0:
            (gb, grad) = hold((gb, grad))
        elif turn == 1:
            gb, both, small, grad = hold((gb, both, small, grad))
            share_one = sum_over_chips(jnp.concatenate([*both, small], axis=1))
    last, late_act, share_one = hold((both[-1], act_b, share_one))
    share_two = sum_over_chips(last)
    fout = expert_out_of(act_a, late_act, w_out, share, peers)
    share_two, fout, late_gp, late_res = hold((share_two, fout, gp_b, gres))
    fback = exchange(fout.reshape(2 * toks, width))
    part = sum_over_dp(jnp.concatenate([share_one, share_two], axis=0))
    late = late_grads((xt_a, xt_b), (gp_a, late_gp), share)
    grad_tokens = grad_tokens_of(tokens, late_res, ga, w_qkv, grads)
    part, fback, late, grad_tokens, early_sum = hold(
        (part, fback, late, grad_tokens, early_sum)
    )
    total = gather_over_dp(part)
    late_sum = lax.psum_scatter(late, "dp", scatter_dimension=0, tiled=True)[0]
    pieces = [total] + [xor_permute(total, "expert", d) for d in range(2, peers, 2)]
    out_tokens = combine(keyn, res, fback)
    grad_w_out = early_sums(early_sum)
    pieces, out_tokens, grad_w_out = hold((pieces, out_tokens, grad_w_out))
    blocks = pieces + [swap_cores(piece) for piece in pieces]
    grad_w_qkv, grad_w_attn_out, grad_gain_attn, grad_gain_ffn, grad_router, grad_embed = (
        shared_sums(me, blocks, rows, extra, w_qkv, ga, experts, rdim)
    )
    grad_w_qkv, late_sum = hold((grad_w_qkv, late_sum))
    grad_w_in = late_sums(early_sum, late_sum)
    return (
        out_tokens,
        grad_tokens,
        grad_w_qkv,
        grad_w_attn_out,
        grad_gain_attn,
        grad_gain_ffn,
        grad_router.T,
        grad_embed,
        grad_w_in,
        grad_w_out,
    )


def solution(mesh):
    rows = P(("dp", "expert"), None)
    return jax.shard_map(
        on_device,
        mesh=mesh,
        in_specs=(
            rows,
            rows,
            rows,
            rows,
            P(),
            P(),
            P(),
            P(),
            P(),
            P(),
            P("expert", None, None),
            P("expert", None, None),
        ),
        out_specs=(
            rows,
            rows,
            P(),
            P(),
            P(),
            P(),
            P(),
            P(),
            P("expert", None, "dp"),
            P("expert", "dp", None),
        ),
        check_vma=False,
    )
```
